32 devices in a mesh: chan: 4 (over z), rows: 8 (over y, x, core).
Axes of the slice: x: 2, y: 2, z: 4, core: 2. Of those that a mesh axis runs over, the one named last changes fastest.
Arguments:
- estimate: float32 [4, 2048, 2048], P('chan', 'rows'), may hold values from -3 to 3
- dirty_image: float32 [4, 2048, 2048], P('chan', 'rows'), may hold values from -40 to 40
- psf_weights: float32 [4, 2048, 2048], P('chan', None, 'rows'), may hold values from 0.05 to 2
Outputs:
- new_estimate: float32 [4, 2048, 2048], P('chan', 'rows')
- residual: float32 [4, 2048, 2048], P('chan', 'rows')
The draws below stay inside these ranges and needn't reach their ends.
All inputs are finite; a program needn't handle non-finite values.
Results may differ from the reference program's by a relative error of at most 0.0001.
Values sent between devices are 32-bit elements; how exact they have to be, the bound alone decides.
No kernel may reach another device: no remote copies, remote signals or barrier semaphores. Data moves between devices by JAX's collectives and lax.ppermute only.
A program may use at most 128 MiB of HBM per device.

```python
import jax
import jax.numpy as jnp
from jax import lax

N = 2048
CH = 4


def draw_dirty_image(key, part):
    key_list = jax.random.split(key, 3)
    noise_part = jax.random.normal(key_list[0], (CH, N, N), jnp.float32)
    row_log = jax.random.uniform(key_list[1], (N,), jnp.float32) - 0.5
    col_log = jax.random.uniform(key_list[2], (N,), jnp.float32) - 0.5
    position = jnp.arange(N, dtype=jnp.float32) / N - 0.5
    channel = jnp.arange(CH, dtype=jnp.float32) / (CH - 1) - 0.5
    rise_factor = 3.0
    scaling = (10.0 ** row_log)[:, None] * (10.0 ** col_log)[None, :] * (rise_factor ** position)[:, None]
    values = noise_part * scaling[None] * (3.0 ** channel)[:, None, None]
    return jnp.clip(values, -40.0, 40.0)


def shard_levels(own_key, dims, cuts, smallest, top_value):
    level, own = 1.0, jax.random.fold_in(own_key, 6)
    for dim, parts in cuts:
        steps = jnp.exp(jax.random.uniform(jax.random.fold_in(own, dim), (parts,), jnp.float32, smallest / len(cuts), top_value / len(cuts)))
        level = level * jnp.repeat(steps, dims[dim] // parts).reshape([-1 if axis == dim else 1 for axis in range(len(dims))])
    return level


def scatter_about(own_key, extent, deviation, bound, cuts=(), held_as=jnp.bfloat16):
    gain = shard_levels(own_key, extent, cuts, -0.22, 0.18) if cuts else 1.0
    drawn = jax.random.normal(own_key, extent, jnp.float32) * deviation * gain
    return jnp.minimum(jnp.maximum(drawn, -bound), bound).astype(held_as)


def setup_inputs(seed: int = 0) -> dict:
    arg_keys = jax.random.split(jax.random.key(seed), 4)
    estimate = scatter_about(arg_keys[0], (CH, N, N), 0.5, 3.0, ((0, 4), (1, 8)), jnp.float32)
    dirty_image = draw_dirty_image(jax.random.fold_in(arg_keys[3], 71), 0)
    psf_weights = jnp.clip(0.05 + 1.95 * jax.random.uniform(arg_keys[2], (CH, N, N), jnp.float32) ** shard_levels(arg_keys[2], (CH, N, N), ((0, 4), (2, 8)), -0.2, 0.2), 0.05, 2.0)
    return dict(estimate=estimate, dirty_image=dirty_image, psf_weights=psf_weights)


fractions = (0.03, 0.02, 0.015)
taps = (0.0625, 0.25, 0.375, 0.25, 0.0625)
step_size = 0.9

def psf_apply(values, weights):
    spectrum = jnp.fft.fft2(values)
    return jnp.real(jnp.fft.ifft2(spectrum * weights)).astype(values.dtype)

def smooth(values, spacing):
    count = values.shape[2]
    padded = jnp.pad(values, ((0, 0), (0, 0), (2 * spacing, 2 * spacing)))
    across = taps[0] * padded[:, :, 0:count]
    for tap_index in range(1, 5):
        across = across + taps[tap_index] * padded[:, :, tap_index * spacing:tap_index * spacing + count]
    height = values.shape[1]
    padded = jnp.pad(across, ((0, 0), (2 * spacing, 2 * spacing), (0, 0)))
    result = taps[0] * padded[:, 0:height]
    for tap_index in range(1, 5):
        result = result + taps[tap_index] * padded[:, tap_index * spacing:tap_index * spacing + height]
    return result

def reference(estimate, dirty_image, psf_weights):
    blurred = psf_apply(estimate, psf_weights)
    residual = dirty_image - blurred
    halfway = estimate + step_size * residual
    current = halfway
    details = []
    for scale_level in range(3):
        smoother = smooth(current, 1 << scale_level)
        details.append(current - smoother)
        current = smoother
    output = current
    for scale_level in range(3):
        detail = details[scale_level]
        energy = lax.optimization_barrier(jnp.sum(detail * detail, axis=0))
        peak = jnp.sqrt(jnp.max(energy))
        threshold = fractions[scale_level] * peak
        factor = 1.0 - threshold / jnp.maximum(jnp.sqrt(energy), threshold)
        output = output + factor[None] * detail
    return (output, residual)
```

```python
import math

import jax
import jax.numpy as jnp
from jax import lax
from jax.sharding import PartitionSpec as P

fractions = (0.03, 0.02, 0.015)
taps = (0.0625, 0.25, 0.375, 0.25, 0.0625)
step_size = 0.9
inner_length = 128
highest = lax.Precision.HIGHEST


def with_halo(cells, sides, width):
    for axis, dim in sides:
        count = lax.axis_size(axis)
        ends = count - 1
        head = lax.slice_in_dim(cells, 0, width, axis=dim)
        tail = lax.slice_in_dim(cells, cells.shape[dim] - width, cells.shape[dim], axis=dim)
        cells = jnp.concatenate(
            [
                lax.ppermute(tail, axis, [(i, (i + 1) % count) for i in range(ends)]),
                cells,
                lax.ppermute(head, axis, [((i + 1) % count, i) for i in range(ends)]),
            ],
            axis=dim,
        )
    return cells


def phase_table(first_count, second_count, length, sign):
    first_ids = lax.iota(jnp.int32, first_count)
    second_ids = lax.iota(jnp.int32, second_count)
    angles = (first_ids[:, None] * second_ids[None, :] % length).astype(jnp.float32) * (
        2.0 * math.pi / length
    )
    return (jnp.cos(angles), sign * jnp.sin(angles))


def dft_last(real_in, imag_in, sign):
    batch, length = real_in.shape
    outer = length // inner_length
    real_part = real_in.reshape(batch, outer, inner_length)
    imag_part = imag_in.reshape(batch, outer, inner_length)
    cos_small, sin_small = phase_table(outer, outer, outer, sign)
    first_real = jnp.einsum("kn,bnm->bkm", cos_small, real_part, precision=highest) - jnp.einsum(
        "kn,bnm->bkm", sin_small, imag_part, precision=highest
    )
    first_imag = jnp.einsum("kn,bnm->bkm", cos_small, imag_part, precision=highest) + jnp.einsum(
        "kn,bnm->bkm", sin_small, real_part, precision=highest
    )
    cos_twist, sin_twist = phase_table(outer, inner_length, length, sign)
    twist_real = first_real * cos_twist - first_imag * sin_twist
    twist_imag = first_imag * cos_twist + first_real * sin_twist
    cos_large, sin_large = phase_table(inner_length, inner_length, inner_length, sign)
    last_real = jnp.einsum("bkm,mj->bkj", twist_real, cos_large, precision=highest) - jnp.einsum(
        "bkm,mj->bkj", twist_imag, sin_large, precision=highest
    )
    last_imag = jnp.einsum("bkm,mj->bkj", twist_imag, cos_large, precision=highest) + jnp.einsum(
        "bkm,mj->bkj", twist_real, sin_large, precision=highest
    )
    return (
        jnp.transpose(last_real, (0, 2, 1)).reshape(batch, length),
        jnp.transpose(last_imag, (0, 2, 1)).reshape(batch, length),
    )


def dft_first(real_in, imag_in, sign):
    length, width = real_in.shape
    outer = length // inner_length
    real_part = real_in.reshape(outer, inner_length, width)
    imag_part = imag_in.reshape(outer, inner_length, width)
    cos_small, sin_small = phase_table(outer, outer, outer, sign)
    first_real = jnp.einsum("kn,nmw->kmw", cos_small, real_part, precision=highest) - jnp.einsum(
        "kn,nmw->kmw", sin_small, imag_part, precision=highest
    )
    first_imag = jnp.einsum("kn,nmw->kmw", cos_small, imag_part, precision=highest) + jnp.einsum(
        "kn,nmw->kmw", sin_small, real_part, precision=highest
    )
    cos_twist, sin_twist = phase_table(outer, inner_length, length, sign)
    cos_twist = cos_twist[:, :, None]
    sin_twist = sin_twist[:, :, None]
    twist_real = first_real * cos_twist - first_imag * sin_twist
    twist_imag = first_imag * cos_twist + first_real * sin_twist
    cos_large, sin_large = phase_table(inner_length, inner_length, inner_length, sign)
    last_real = jnp.einsum("kmw,mj->kjw", twist_real, cos_large, precision=highest) - jnp.einsum(
        "kmw,mj->kjw", twist_imag, sin_large, precision=highest
    )
    last_imag = jnp.einsum("kmw,mj->kjw", twist_imag, cos_large, precision=highest) + jnp.einsum(
        "kmw,mj->kjw", twist_real, sin_large, precision=highest
    )
    return (
        jnp.transpose(last_real, (1, 0, 2)).reshape(length, width),
        jnp.transpose(last_imag, (1, 0, 2)).reshape(length, width),
    )


def columns_forward(pieces):
    real_out, imag_out = dft_first(pieces[0][:, 0, :], pieces[1][:, 0, :], -1.0)
    return (real_out[:, None, :], imag_out[:, None, :])


def rows_inverse(pieces):
    real_in = pieces[0][0]
    imag_in = pieces[1][0]
    length = real_in.shape[1]
    real_out, imag_out = dft_last(real_in, imag_in, 1.0)
    return (real_out * (1.0 / (length * length)))[None]


def max_over(cells, axis):
    count = lax.axis_size(axis)
    if count & (count - 1):
        return lax.pmax(cells, axis)
    distance = 1
    while distance < count:
        other = lax.ppermute(cells, axis, [(i, i ^ distance) for i in range(count)])
        cells = jnp.maximum(cells, other)
        distance *= 2
    return cells


def smooth_both(values, spacing):
    for dim in (2, 1):
        count = values.shape[dim] - 4 * spacing
        total = taps[0] * lax.slice_in_dim(values, 0, count, axis=dim)
        for tap_index in range(1, 5):
            start = tap_index * spacing
            total = total + taps[tap_index] * lax.slice_in_dim(
                values, start, start + count, axis=dim
            )
        values = total
    return values


def shards(estimate, dirty_image, psf_weights):
    values = estimate[0]
    height, length = values.shape
    row_count = lax.axis_size("rows")
    narrow = length // row_count
    spec_real, spec_imag = dft_last(values, jnp.zeros_like(values), -1.0)
    spec_real = spec_real.reshape(height, row_count, narrow)
    spec_imag = spec_imag.reshape(height, row_count, narrow)
    col_real, col_imag = columns_forward(
        (
            lax.all_to_all(spec_real, "rows", split_axis=1, concat_axis=0, tiled=True),
            lax.all_to_all(spec_imag, "rows", split_axis=1, concat_axis=0, tiled=True),
        )
    )
    weights = psf_weights[0]
    prod_real = weights * col_real[:, 0, :]
    prod_imag = weights * col_imag[:, 0, :]
    back_real, back_imag = dft_first(prod_real, prod_imag, 1.0)
    back_real = back_real.reshape(row_count, height, narrow)
    back_imag = back_imag.reshape(row_count, height, narrow)
    blurred = rows_inverse(
        (
            lax.all_to_all(back_real, "rows", split_axis=0, concat_axis=2, tiled=True),
            lax.all_to_all(back_imag, "rows", split_axis=0, concat_axis=2, tiled=True),
        )
    )[0]
    residual = dirty_image[0] - blurred
    halfway = values + step_size * residual
    depth = 14
    chan_count = lax.axis_size("chan")
    part = length // chan_count
    padded = with_halo(halfway, (("rows", 0),), depth)
    padded = jnp.pad(padded, ((0, 0), (depth, depth)))
    pieces = jnp.stack(
        [padded[:, q * part : (q + 1) * part + 2 * depth] for q in range(chan_count)]
    )
    current = lax.all_to_all(pieces, "chan", split_axis=0, concat_axis=0, tiled=True)
    row_ids = lax.axis_index("rows") * height - depth + lax.iota(jnp.int32, height + 2 * depth)
    col_ids = lax.axis_index("chan") * part - depth + lax.iota(jnp.int32, part + 2 * depth)
    margin = depth
    details = []
    for scale_level in range(3):
        reach = 2 << scale_level
        smoother = smooth_both(current, 1 << scale_level)
        row_ids = row_ids[reach:-reach]
        col_ids = col_ids[reach:-reach]
        inside = ((row_ids >= 0) & (row_ids < length))[:, None] & (
            (col_ids >= 0) & (col_ids < length)
        )[None, :]
        smoother = jnp.where(inside[None], smoother, 0.0)
        new_margin = margin - reach
        details.append(
            current[:, margin : margin + height, margin : margin + part]
            - smoother[:, new_margin : new_margin + height, new_margin : new_margin + part]
        )
        current = smoother
        margin = new_margin
    energies = [jnp.sum(detail * detail, axis=0) for detail in details]
    peaks = jnp.stack([jnp.broadcast_to(jnp.max(energy), (128,)) for energy in energies])
    peaks = max_over(max_over(peaks, "rows"), "chan")
    output = current
    for scale_level in range(3):
        threshold = fractions[scale_level] * jnp.sqrt(peaks[scale_level, 0])
        factor = 1.0 - threshold / jnp.maximum(jnp.sqrt(energies[scale_level]), threshold)
        output = output + factor[None] * details[scale_level]
    output = lax.all_to_all(output, "chan", split_axis=0, concat_axis=2, tiled=True)[0]
    new_estimate = output[None]
    return (new_estimate, residual[None])


def solution(mesh):
    return jax.shard_map(
        shards,
        mesh=mesh,
        in_specs=(P("chan", "rows", None), P("chan", "rows", None), P("chan", None, "rows")),
        out_specs=(P("chan", "rows", None), P("chan", "rows", None)),
        check_vma=False,
    )
```

```python
import functools
import math

import jax
import jax.numpy as jnp
import ml_dtypes
import numpy as np
from jax import lax
from jax.experimental import pallas as pl
from jax.experimental.pallas import tpu as pltpu
from jax.sharding import PartitionSpec as P

fractions = (0.03, 0.02, 0.015)
taps = (0.0625, 0.25, 0.375, 0.25, 0.0625)
step_size = 0.9
inner_length = 128
highest = lax.Precision.HIGHEST
lane_count = 128
vmem_bytes = 56 * 1024 * 1024


def with_halo(cells, sides, width):
    for axis, dim in sides:
        count = lax.axis_size(axis)
        ends = count - 1
        head = lax.slice_in_dim(cells, 0, width, axis=dim)
        tail = lax.slice_in_dim(cells, cells.shape[dim] - width, cells.shape[dim], axis=dim)
        cells = jnp.concatenate(
            [
                lax.ppermute(tail, axis, [(i, (i + 1) % count) for i in range(ends)]),
                cells,
                lax.ppermute(head, axis, [((i + 1) % count, i) for i in range(ends)]),
            ],
            axis=dim,
        )
    return cells


def phase_table(first_count, second_count, length, sign):
    first_ids = lax.iota(jnp.int32, first_count)
    second_ids = lax.iota(jnp.int32, second_count)
    angles = (first_ids[:, None] * second_ids[None, :] % length).astype(jnp.float32) * (
        2.0 * math.pi / length
    )
    return (jnp.cos(angles), sign * jnp.sin(angles))


def dft_last(real_in, imag_in, sign):
    batch, length = real_in.shape
    outer = length // inner_length
    real_part = real_in.reshape(batch, outer, inner_length)
    imag_part = imag_in.reshape(batch, outer, inner_length)
    cos_small, sin_small = phase_table(outer, outer, outer, sign)
    first_real = jnp.einsum("kn,bnm->bkm", cos_small, real_part, precision=highest) - jnp.einsum(
        "kn,bnm->bkm", sin_small, imag_part, precision=highest
    )
    first_imag = jnp.einsum("kn,bnm->bkm", cos_small, imag_part, precision=highest) + jnp.einsum(
        "kn,bnm->bkm", sin_small, real_part, precision=highest
    )
    cos_twist, sin_twist = phase_table(outer, inner_length, length, sign)
    twist_real = first_real * cos_twist - first_imag * sin_twist
    twist_imag = first_imag * cos_twist + first_real * sin_twist
    cos_large, sin_large = phase_table(inner_length, inner_length, inner_length, sign)
    last_real = jnp.einsum("bkm,mj->bkj", twist_real, cos_large, precision=highest) - jnp.einsum(
        "bkm,mj->bkj", twist_imag, sin_large, precision=highest
    )
    last_imag = jnp.einsum("bkm,mj->bkj", twist_imag, cos_large, precision=highest) + jnp.einsum(
        "bkm,mj->bkj", twist_real, sin_large, precision=highest
    )
    return (
        jnp.transpose(last_real, (0, 2, 1)).reshape(batch, length),
        jnp.transpose(last_imag, (0, 2, 1)).reshape(batch, length),
    )


def dft_first(real_in, imag_in, sign):
    length, width = real_in.shape
    outer = length // inner_length
    real_part = real_in.reshape(outer, inner_length, width)
    imag_part = imag_in.reshape(outer, inner_length, width)
    cos_small, sin_small = phase_table(outer, outer, outer, sign)
    first_real = jnp.einsum("kn,nmw->kmw", cos_small, real_part, precision=highest) - jnp.einsum(
        "kn,nmw->kmw", sin_small, imag_part, precision=highest
    )
    first_imag = jnp.einsum("kn,nmw->kmw", cos_small, imag_part, precision=highest) + jnp.einsum(
        "kn,nmw->kmw", sin_small, real_part, precision=highest
    )
    cos_twist, sin_twist = phase_table(outer, inner_length, length, sign)
    cos_twist = cos_twist[:, :, None]
    sin_twist = sin_twist[:, :, None]
    twist_real = first_real * cos_twist - first_imag * sin_twist
    twist_imag = first_imag * cos_twist + first_real * sin_twist
    cos_large, sin_large = phase_table(inner_length, inner_length, inner_length, sign)
    last_real = jnp.einsum("kmw,mj->kjw", twist_real, cos_large, precision=highest) - jnp.einsum(
        "kmw,mj->kjw", twist_imag, sin_large, precision=highest
    )
    last_imag = jnp.einsum("kmw,mj->kjw", twist_imag, cos_large, precision=highest) + jnp.einsum(
        "kmw,mj->kjw", twist_real, sin_large, precision=highest
    )
    return (
        jnp.transpose(last_real, (1, 0, 2)).reshape(length, width),
        jnp.transpose(last_imag, (1, 0, 2)).reshape(length, width),
    )


def columns_forward(pieces):
    real_out, imag_out = dft_first(pieces[0][:, 0, :], pieces[1][:, 0, :], -1.0)
    return (real_out[:, None, :], imag_out[:, None, :])


def rows_inverse(pieces):
    real_in = pieces[0][0]
    imag_in = pieces[1][0]
    length = real_in.shape[1]
    real_out, imag_out = dft_last(real_in, imag_in, 1.0)
    return (real_out * (1.0 / (length * length)))[None]


def max_over(cells, axis):
    count = lax.axis_size(axis)
    if count & (count - 1):
        return lax.pmax(cells, axis)
    distance = 1
    while distance < count:
        other = lax.ppermute(cells, axis, [(i, i ^ distance) for i in range(count)])
        cells = jnp.maximum(cells, other)
        distance *= 2
    return cells


def smooth_both(values, spacing):
    for dim in (2, 1):
        count = values.shape[dim] - 4 * spacing
        total = taps[0] * lax.slice_in_dim(values, 0, count, axis=dim)
        for tap_index in range(1, 5):
            start = tap_index * spacing
            total = total + taps[tap_index] * lax.slice_in_dim(
                values, start, start + count, axis=dim
            )
        values = total
    return values


def real_dft(parts):
    count = len(parts)
    if count == 1:
        return [(parts[0], None)]
    if count == 2:
        return [(parts[0] + parts[1], None), (parts[0] - parts[1], None)]
    even = real_dft(parts[0::2])
    odd = real_dft(parts[1::2])
    out = [None] * (count // 2 + 1)
    for k in range(count // 4 + 1):
        turned = spin(odd[k], -2.0 * math.pi * k / count)
        out[k] = pair_add(even[k], turned)
        low = pair_sub(even[k], turned)
        out[count // 2 - k] = (low[0], None if low[1] is None else -low[1])
    out[0] = (out[0][0], None)
    out[count // 2] = (out[count // 2][0], None)
    return out


def real_inverse_dft(pairs):
    count = 2 * (len(pairs) - 1)
    if count == 2:
        return [pairs[0][0] + pairs[1][0], pairs[0][0] - pairs[1][0]]
    even, odd = [], []
    for k in range(count // 4 + 1):
        low = pairs[k]
        high = pairs[count // 2 - k]
        high = (high[0], None if high[1] is None else -high[1])
        even.append(pair_add(low, high))
        odd.append(spin(pair_sub(low, high), 2.0 * math.pi * k / count))
    for half in (even, odd):
        half[0] = (half[0][0], None)
        half[-1] = (half[-1][0], None)
    even = real_inverse_dft(even)
    odd = real_inverse_dft(odd)
    return [cells for both in zip(even, odd) for cells in both]


def complex_dft(pairs, sign):
    count = len(pairs)
    if count == 1:
        return pairs
    even = complex_dft(pairs[0::2], sign)
    odd = complex_dft(pairs[1::2], sign)
    turned = [spin(odd[k], sign * 2.0 * math.pi * k / count) for k in range(count // 2)]
    return [pair_add(a, b) for a, b in zip(even, turned)] + [
        pair_sub(a, b) for a, b in zip(even, turned)
    ]


def pair_add(a, b):
    if a[1] is None or b[1] is None:
        return (a[0] + b[0], a[1] if b[1] is None else b[1])
    return (a[0] + b[0], a[1] + b[1])


def pair_sub(a, b):
    if b[1] is None:
        return (a[0] - b[0], a[1])
    return (a[0] - b[0], -b[1] if a[1] is None else a[1] - b[1])


def spin(pair, angle):
    quarter = angle / (0.5 * math.pi)
    turns = round(quarter)
    real, imag = pair
    if abs(quarter - turns) < 1e-9:
        turns %= 4
        if turns == 0:
            return pair
        if turns == 2:
            return (-real, None if imag is None else -imag)
        if imag is None:
            return (jnp.zeros_like(real), real if turns == 1 else -real)
        return (-imag, real) if turns == 1 else (imag, -real)
    cosine, sine = math.cos(angle), math.sin(angle)
    if imag is None:
        return (real * cosine, real * sine)
    if abs(abs(cosine) - abs(sine)) < 1e-9:
        a, b = math.copysign(1.0, cosine), math.copysign(1.0, sine)
        root = abs(cosine)
        first = real if a > 0 else -real
        second = imag if b > 0 else -imag
        third = real if b > 0 else -real
        fourth = imag if a > 0 else -imag
        return ((first - second) * root, (third + fourth) * root)
    return (real * cosine - imag * sine, real * sine + imag * cosine)


def split(cells):
    high = cells.astype(jnp.bfloat16)
    return high, (cells - high.astype(jnp.float32)).astype(jnp.bfloat16)


def dot(a, b):
    return jnp.dot(a, b, preferred_element_type=jnp.float32)


def split_table(table):
    high = table.astype(np.float32).astype(ml_dtypes.bfloat16)
    low = (table - high.astype(np.float64)).astype(np.float32).astype(ml_dtypes.bfloat16)
    return np.stack([high, low], axis=-3)


def group_columns(length, count, group):
    radix = 2 * count
    lanes = length // radix
    spots = np.arange(lanes)
    if group:
        return group + radix * spots
    half = lanes // 2
    return np.where(spots < half, radix * spots, count + radix * (spots - half))


def row_tables(length, count):
    radix = 2 * count
    lanes = length // radix
    half = lanes // 2
    spots = np.arange(lanes)
    there, back = [], []
    for group in range(count):
        columns = group_columns(length, count, group)
        angles = 2.0 * np.pi * (np.outer(spots, columns) % length) / length
        cosine, sine = np.cos(angles), np.sin(angles)
        ahead = np.zeros((2, lanes, 2, lanes))
        behind = np.zeros((2, lanes, 2, lanes))
        if group:
            ahead[0, :, 0], ahead[0, :, 1] = cosine, -sine
            ahead[1, :, 0], ahead[1, :, 1] = sine, cosine
            behind[0, :, 0], behind[0, :, 1] = cosine.T, sine.T
            behind[1, :, 0], behind[1, :, 1] = -sine.T, cosine.T
        else:
            for part, where in enumerate((slice(0, half), slice(half, lanes))):
                ahead[part, :, 0, where] = cosine[:, where]
                ahead[part, :, 1, where] = -sine[:, where]
                behind[0, where, part] = 2.0 * cosine[:, where].T
                behind[1, where, part] = -2.0 * sine[:, where].T
            ahead[0, :, 1, 0] = (-1.0) ** spots
            behind[0, 0, 0] = 1.0
            behind[1, 0, 0] = (-1.0) ** spots
        there.append(ahead.reshape(2 * lanes, 2 * lanes))
        back.append(behind.reshape(2 * lanes, 2 * lanes) / float(length) ** 2)
    return split_table(np.stack(there)), split_table(np.stack(back))


def column_tables(length, steps):
    size = length // steps
    spots = np.arange(size)
    there = []
    for step in range(steps):
        angles = 2.0 * np.pi * ((np.outer(spots, steps * spots + step)) % length) / length
        cosine, sine = np.cos(angles), np.sin(angles)
        there.append(np.block([[cosine, sine], [-sine, cosine]]))
    there = np.stack(there)
    return split_table(there), split_table(np.swapaxes(there, 1, 2))


def weight_tables(length, count):
    width = length // count
    lanes = length // (2 * count)
    per_class = width // (2 * count)
    packs = lanes // (2 * per_class)
    radix = 2 * count

    def classes(group):
        return (group, radix - group) if group else (0, count)

    pick = np.zeros((packs, width, count, lanes))
    for group in range(count):
        for which, kind in enumerate(classes(group)):
            for q in range(per_class):
                for pack in range(packs):
                    lane = pack * 2 * per_class + which * per_class + q
                    pick[pack, radix * q + kind, group, lane] = 1.0
    place = np.zeros((2, count, lanes, packs * 2 + 1, lanes))

    def slot(group, column, pack):
        column %= length
        source, rest = divmod(column, width)
        which = classes(group).index(rest % radix)
        return source, pack * 2 * per_class + which * per_class + rest // radix

    for version, group in ((0, 0), (1, 1)):
        columns = group_columns(length, count, group)
        for pack in range(packs):
            for lane in range(lanes):
                column = int(columns[lane])
                mates = [(column, 0, 0.5), (-column, 1, 0.5)]
                if group == 0 and lane == 0:
                    mates = [(c, s, 0.25) for c in (0, length // 2) for s in (0, 1)]
                for mate, side, value in mates:
                    source, where = slot(group, mate, pack)
                    place[version, source, where, pack * 2 + side, lane] += value
            if group == 0:
                for mate, value in ((0, 0.25), (length // 2, -0.25)):
                    source, where = slot(group, mate, pack)
                    place[version, source, where, packs * 2, pack] += value
    flip = np.zeros((lanes, 2 * lanes))
    flip[np.arange(1, lanes), lanes - np.arange(1, lanes)] = 1.0
    flip[0, lanes] = 1.0
    as_half = lambda table: table.astype(np.float32).astype(ml_dtypes.bfloat16)
    return (
        as_half(pick.reshape(packs * width, count * lanes)),
        as_half(place.reshape(2, count * lanes, (packs * 2 + 1) * lanes)),
        as_half(flip),
    )


def whole_call(body, out_shapes, scratch, name):
    return pl.pallas_call(
        body,
        out_shape=out_shapes,
        scratch_shapes=scratch,
        compiler_params=pltpu.CompilerParams(vmem_limit_bytes=vmem_bytes),
        name=name,
    )


def row_forward_body(steps, x_ref, table_ref, out_ref, held):
    groups, _, height, lanes = out_ref.shape
    each = height // steps
    for start in range(0, height, 16):
        rows = pl.ds(start, 16)
        tiles = [x_ref[rows, pl.ds(lanes * t, lanes)] for t in range(2 * groups)]
        pairs = real_dft(tiles)
        pairs = [(pairs[0][0], pairs[groups][0])] + pairs[1:groups]
        for group in range(groups):
            high, low = split(jnp.concatenate(pairs[group], axis=1))
            held[0, group, rows, :] = high
            held[1, group, rows, :] = low
    for group in range(groups):
        done = (
            dot(held[0, group], table_ref[group, 0])
            + dot(held[1, group], table_ref[group, 0])
            + dot(held[0, group], table_ref[group, 1])
        )
        for start in range(0, height, 8):
            spread = pl.ds(start % steps * each + start // steps, 8, stride=each)
            out_ref[group, 0, spread, :] = done[start : start + 8, :lanes]
            out_ref[group, 1, spread, :] = done[start : start + 8, lanes:]


def row_inverse_body(steps, in_ref, table_ref, est_ref, dirty_ref, res_ref, half_ref, held):
    groups, _, height, lanes = in_ref.shape
    each = height // steps
    for group in range(groups):
        parts = []
        for part in range(2):
            pieces = [
                in_ref[
                    group,
                    part,
                    pl.ds(start % steps * each + start // steps, 8, stride=each),
                    :,
                ]
                for start in range(0, height, 8)
            ]
            parts.append(jnp.concatenate(pieces, axis=0))
        high, low = split(jnp.concatenate(parts, axis=1))
        held[group] = (
            dot(high, table_ref[group, 0])
            + dot(low, table_ref[group, 0])
            + dot(high, table_ref[group, 1])
        )
    for start in range(0, height, 8):
        rows = pl.ds(start, 8)
        pairs = [
            (held[group, rows, pl.ds(0, lanes)], held[group, rows, pl.ds(lanes, lanes)])
            for group in range(groups)
        ]
        pairs = [(pairs[0][0], None)] + pairs[1:] + [(pairs[0][1], None)]
        tiles = real_inverse_dft(pairs)
        for t in range(2 * groups):
            where = pl.ds(lanes * t, lanes)
            residual = dirty_ref[rows, where] - tiles[t]
            res_ref[rows, where] = residual
            half_ref[rows, where] = est_ref[rows, where] + step_size * residual


def column_body(
    steps, in_ref, there_ref, back_ref, weight_ref, mirror_ref, flip_ref, out_ref, held, made
):
    count, _, height, lanes = in_ref.shape
    each = height // steps
    size = each * count
    for step in range(steps):
        rows = pl.ds(step * each, each)
        block = jnp.concatenate(
            [in_ref[source, part, rows, :] for part in range(2) for source in range(count)],
            axis=0,
        )
        high, low = split(block)
        done = (
            dot(there_ref[step, 0], high)
            + dot(there_ref[step, 1], high)
            + dot(there_ref[step, 0], low)
        )
        held[0, step] = done[:size]
        held[1, step] = done[size:]

    def forward(chunk, carry):
        rows = pl.ds(pl.multiple_of(chunk * 8, 8), 8)
        pairs = [(held[0, step, rows, :], held[1, step, rows, :]) for step in range(steps)]
        for step, pair in enumerate(complex_dft(pairs, -1.0)):
            held[0, step, rows, :] = pair[0]
            held[1, step, rows, :] = pair[1]
        return carry

    lax.fori_loop(0, size // 8, forward, 0)
    for step in range(steps):
        facing = [
            jnp.concatenate([held[0, other], held[1, other]], axis=1)
            for other in (steps - 1 - step, (steps - step) % steps)
        ]
        high, low = split(jnp.concatenate(facing, axis=0))
        turned = dot(flip_ref[...], high) + dot(flip_ref[...], low)
        weight = weight_ref[step]
        mirror = mirror_ref[step]
        made[0, step] = weight * held[0, step] + mirror * turned[:, :lanes]
        made[1, step] = weight * held[1, step] - mirror * turned[:, lanes:]

    def backward(chunk, carry):
        rows = pl.ds(pl.multiple_of(chunk * 8, 8), 8)
        pairs = [(made[0, step, rows, :], made[1, step, rows, :]) for step in range(steps)]
        for step, pair in enumerate(complex_dft(pairs, 1.0)):
            made[0, step, rows, :] = pair[0]
            made[1, step, rows, :] = pair[1]
        return carry

    lax.fori_loop(0, size // 8, backward, 0)
    for step in range(steps):
        high, low = split(jnp.concatenate([made[0, step], made[1, step]], axis=0))
        done = (
            dot(back_ref[step, 0], high)
            + dot(back_ref[step, 1], high)
            + dot(back_ref[step, 0], low)
        )
        rows = pl.ds(step * each, each)
        for part in range(2):
            for target in range(count):
                start = part * size + target * each
                out_ref[target, part, rows, :] = done[start : start + each]


def weight_pick_body(w_ref, pick_ref, out_ref):
    count, _, lanes = out_ref.shape
    packs, _, width = w_ref.shape
    total = 0.0
    for pack in range(packs):
        high, low = split(w_ref[pack])
        chosen = pick_ref[pl.ds(pack * width, width), :]
        total = total + dot(high, chosen) + dot(low, chosen)
    for target in range(count):
        out_ref[target] = total[:, target * lanes : (target + 1) * lanes]


def weight_place_body(in_ref, place_ref, flip_ref, weight_ref, mirror_ref, held):
    count, depth, lanes = in_ref.shape
    steps, size, _ = weight_ref.shape
    packs = steps * size // depth
    total = 0.0
    for source in range(count):
        high, low = split(in_ref[source])
        chosen = place_ref[pl.ds(source * lanes, lanes), :]
        total = total + dot(high, chosen) + dot(low, chosen)
    inner = depth // size
    extra = total[:, 2 * packs * lanes :]
    first = lax.broadcasted_iota(jnp.int32, (size, lanes), 1) == 0
    for step in range(steps):
        pack, rest = divmod(step, inner)
        rows = slice(rest * size, (rest + 1) * size)
        lone = extra[rows]
        if pack:
            lone = pltpu.roll(lone, lanes - pack, 1)
        lone = jnp.where(first, lone, 0.0)
        mirror_ref[step] = lone
        weight_ref[step] = total[rows, 2 * pack * lanes : (2 * pack + 1) * lanes]
        held[step] = jnp.concatenate(
            [total[rows, (2 * pack + 1) * lanes : (2 * pack + 2) * lanes], lone], axis=1
        )
    for step in range(steps):
        high, low = split(
            jnp.concatenate([held[steps - 1 - step], held[(steps - step) % steps]], axis=0)
        )
        turned = dot(flip_ref[...], high) + dot(flip_ref[...], low)
        weight_ref[step] += turned[:, :lanes]
        mirror_ref[step] += turned[:, lanes:]


def filtered(values, dirty, weights):
    height, length = values.shape
    count = lax.axis_size("rows")
    lanes = length // (2 * count)
    steps = height // 16
    size = length // steps
    width = weights.shape[1]
    f32 = jnp.float32
    pick, place, flip = [jnp.asarray(table) for table in weight_tables(length, count)]
    there, back = [jnp.asarray(table) for table in row_tables(length, count)]
    down, up = [jnp.asarray(table) for table in column_tables(length, steps)]
    shape = lambda *dims: jax.ShapeDtypeStruct(dims, f32)
    packs = length * width // (count * lanes) // (length // count)
    packs = pick.shape[0] // width
    depth = length // packs

    sent = whole_call(weight_pick_body, shape(count, depth, lanes), [], "weight_pick")(
        weights.reshape(packs, depth, width), pick
    )
    sent = lax.all_to_all(sent, "rows", 0, 0, tiled=True)
    ahead = whole_call(
        functools.partial(row_forward_body, steps),
        shape(count, 2, height, lanes),
        [pltpu.VMEM((2, count, height, 2 * lanes), jnp.bfloat16)],
        "row_forward",
    )(values, there)
    ahead = lax.all_to_all(ahead, "rows", 0, 0, tiled=True)
    mine = jnp.where(lax.axis_index("rows") == 0, place[0], place[1])
    weight, mirror = whole_call(
        weight_place_body,
        [shape(steps, size, lanes)] * 2,
        [pltpu.VMEM((steps, size, 2 * lanes), f32)],
        "weight_place",
    )(sent, mine, flip)
    behind = whole_call(
        functools.partial(column_body, steps),
        shape(count, 2, height, lanes),
        [pltpu.VMEM((2, steps, size, lanes), f32)] * 2,
        "column_filter",
    )(ahead, down, up, weight, mirror, flip)
    behind = lax.all_to_all(behind, "rows", 0, 0, tiled=True)
    return whole_call(
        functools.partial(row_inverse_body, steps),
        [shape(height, length)] * 2,
        [pltpu.VMEM((count, height, 2 * lanes), f32)],
        "row_inverse",
    )(behind, back, values, dirty)


def filtered_plain(values, dirty, weights):
    height, length = values.shape
    row_count = lax.axis_size("rows")
    narrow = length // row_count
    spec_real, spec_imag = dft_last(values, jnp.zeros_like(values), -1.0)
    spec_real = spec_real.reshape(height, row_count, narrow)
    spec_imag = spec_imag.reshape(height, row_count, narrow)
    col_real, col_imag = columns_forward(
        (
            lax.all_to_all(spec_real, "rows", split_axis=1, concat_axis=0, tiled=True),
            lax.all_to_all(spec_imag, "rows", split_axis=1, concat_axis=0, tiled=True),
        )
    )
    prod_real = weights * col_real[:, 0, :]
    prod_imag = weights * col_imag[:, 0, :]
    back_real, back_imag = dft_first(prod_real, prod_imag, 1.0)
    back_real = back_real.reshape(row_count, height, narrow)
    back_imag = back_imag.reshape(row_count, height, narrow)
    blurred = rows_inverse(
        (
            lax.all_to_all(back_real, "rows", split_axis=0, concat_axis=2, tiled=True),
            lax.all_to_all(back_imag, "rows", split_axis=0, concat_axis=2, tiled=True),
        )
    )[0]
    residual = dirty - blurred
    return residual, values + step_size * residual


def shards(estimate, dirty_image, psf_weights):
    values = estimate[0]
    height, length = values.shape
    row_count = lax.axis_size("rows")
    if length == 2 * row_count * lane_count:
        residual, halfway = filtered(values, dirty_image[0], psf_weights[0])
    else:
        residual, halfway = filtered_plain(values, dirty_image[0], psf_weights[0])
    depth = 14
    chan_count = lax.axis_size("chan")
    part = length // chan_count
    padded = with_halo(halfway, (("rows", 0),), depth)
    padded = jnp.pad(padded, ((0, 0), (depth, depth)))
    pieces = jnp.stack(
        [padded[:, q * part : (q + 1) * part + 2 * depth] for q in range(chan_count)]
    )
    current = lax.all_to_all(pieces, "chan", split_axis=0, concat_axis=0, tiled=True)
    row_ids = lax.axis_index("rows") * height - depth + lax.iota(jnp.int32, height + 2 * depth)
    col_ids = lax.axis_index("chan") * part - depth + lax.iota(jnp.int32, part + 2 * depth)
    margin = depth
    details = []
    for scale_level in range(3):
        reach = 2 << scale_level
        smoother = smooth_both(current, 1 << scale_level)
        row_ids = row_ids[reach:-reach]
        col_ids = col_ids[reach:-reach]
        inside = ((row_ids >= 0) & (row_ids < length))[:, None] & (
            (col_ids >= 0) & (col_ids < length)
        )[None, :]
        smoother = jnp.where(inside[None], smoother, 0.0)
        new_margin = margin - reach
        details.append(
            current[:, margin : margin + height, margin : margin + part]
            - smoother[:, new_margin : new_margin + height, new_margin : new_margin + part]
        )
        current = smoother
        margin = new_margin
    energies = [jnp.sum(detail * detail, axis=0) for detail in details]
    peaks = jnp.stack([jnp.broadcast_to(jnp.max(energy), (128,)) for energy in energies])
    peaks = max_over(max_over(peaks, "rows"), "chan")
    output = current
    for scale_level in range(3):
        threshold = fractions[scale_level] * jnp.sqrt(peaks[scale_level, 0])
        factor = 1.0 - threshold / jnp.maximum(jnp.sqrt(energies[scale_level]), threshold)
        output = output + factor[None] * details[scale_level]
    output = lax.all_to_all(output, "chan", split_axis=0, concat_axis=2, tiled=True)[0]
    new_estimate = output[None]
    return (new_estimate, residual[None])


def solution(mesh):
    return jax.shard_map(
        shards,
        mesh=mesh,
        in_specs=(P("chan", "rows", None), P("chan", "rows", None), P("chan", None, "rows")),
        out_specs=(P("chan", "rows", None), P("chan", "rows", None)),
        check_vma=False,
    )
```

```python
import functools
import math

import jax
import jax.numpy as jnp
import ml_dtypes
import numpy as np
from jax import lax
from jax.experimental import pallas as pl
from jax.experimental.pallas import tpu as pltpu
from jax.sharding import PartitionSpec as P

fractions = (0.03, 0.02, 0.015)
taps = (0.0625, 0.25, 0.375, 0.25, 0.0625)
step_size = 0.9
inner_length = 128
highest = lax.Precision.HIGHEST
lane_count = 128
vmem_bytes = 56 * 1024 * 1024
rim = 16
halo_rows = 16


def with_halo(cells, sides, width):
    for axis, dim in sides:
        count = lax.axis_size(axis)
        ends = count - 1
        head = lax.slice_in_dim(cells, 0, width, axis=dim)
        tail = lax.slice_in_dim(cells, cells.shape[dim] - width, cells.shape[dim], axis=dim)
        cells = jnp.concatenate(
            [
                lax.ppermute(tail, axis, [(i, (i + 1) % count) for i in range(ends)]),
                cells,
                lax.ppermute(head, axis, [((i + 1) % count, i) for i in range(ends)]),
            ],
            axis=dim,
        )
    return cells


def phase_table(first_count, second_count, length, sign):
    first_ids = lax.iota(jnp.int32, first_count)
    second_ids = lax.iota(jnp.int32, second_count)
    angles = (first_ids[:, None] * second_ids[None, :] % length).astype(jnp.float32) * (
        2.0 * math.pi / length
    )
    return (jnp.cos(angles), sign * jnp.sin(angles))


def dft_last(real_in, imag_in, sign):
    batch, length = real_in.shape
    outer = length // inner_length
    real_part = real_in.reshape(batch, outer, inner_length)
    imag_part = imag_in.reshape(batch, outer, inner_length)
    cos_small, sin_small = phase_table(outer, outer, outer, sign)
    first_real = jnp.einsum("kn,bnm->bkm", cos_small, real_part, precision=highest) - jnp.einsum(
        "kn,bnm->bkm", sin_small, imag_part, precision=highest
    )
    first_imag = jnp.einsum("kn,bnm->bkm", cos_small, imag_part, precision=highest) + jnp.einsum(
        "kn,bnm->bkm", sin_small, real_part, precision=highest
    )
    cos_twist, sin_twist = phase_table(outer, inner_length, length, sign)
    twist_real = first_real * cos_twist - first_imag * sin_twist
    twist_imag = first_imag * cos_twist + first_real * sin_twist
    cos_large, sin_large = phase_table(inner_length, inner_length, inner_length, sign)
    last_real = jnp.einsum("bkm,mj->bkj", twist_real, cos_large, precision=highest) - jnp.einsum(
        "bkm,mj->bkj", twist_imag, sin_large, precision=highest
    )
    last_imag = jnp.einsum("bkm,mj->bkj", twist_imag, cos_large, precision=highest) + jnp.einsum(
        "bkm,mj->bkj", twist_real, sin_large, precision=highest
    )
    return (
        jnp.transpose(last_real, (0, 2, 1)).reshape(batch, length),
        jnp.transpose(last_imag, (0, 2, 1)).reshape(batch, length),
    )


def dft_first(real_in, imag_in, sign):
    length, width = real_in.shape
    outer = length // inner_length
    real_part = real_in.reshape(outer, inner_length, width)
    imag_part = imag_in.reshape(outer, inner_length, width)
    cos_small, sin_small = phase_table(outer, outer, outer, sign)
    first_real = jnp.einsum("kn,nmw->kmw", cos_small, real_part, precision=highest) - jnp.einsum(
        "kn,nmw->kmw", sin_small, imag_part, precision=highest
    )
    first_imag = jnp.einsum("kn,nmw->kmw", cos_small, imag_part, precision=highest) + jnp.einsum(
        "kn,nmw->kmw", sin_small, real_part, precision=highest
    )
    cos_twist, sin_twist = phase_table(outer, inner_length, length, sign)
    cos_twist = cos_twist[:, :, None]
    sin_twist = sin_twist[:, :, None]
    twist_real = first_real * cos_twist - first_imag * sin_twist
    twist_imag = first_imag * cos_twist + first_real * sin_twist
    cos_large, sin_large = phase_table(inner_length, inner_length, inner_length, sign)
    last_real = jnp.einsum("kmw,mj->kjw", twist_real, cos_large, precision=highest) - jnp.einsum(
        "kmw,mj->kjw", twist_imag, sin_large, precision=highest
    )
    last_imag = jnp.einsum("kmw,mj->kjw", twist_imag, cos_large, precision=highest) + jnp.einsum(
        "kmw,mj->kjw", twist_real, sin_large, precision=highest
    )
    return (
        jnp.transpose(last_real, (1, 0, 2)).reshape(length, width),
        jnp.transpose(last_imag, (1, 0, 2)).reshape(length, width),
    )


def columns_forward(pieces):
    real_out, imag_out = dft_first(pieces[0][:, 0, :], pieces[1][:, 0, :], -1.0)
    return (real_out[:, None, :], imag_out[:, None, :])


def rows_inverse(pieces):
    real_in = pieces[0][0]
    imag_in = pieces[1][0]
    length = real_in.shape[1]
    real_out, imag_out = dft_last(real_in, imag_in, 1.0)
    return (real_out * (1.0 / (length * length)))[None]


def max_over(cells, axis):
    count = lax.axis_size(axis)
    if count & (count - 1):
        return lax.pmax(cells, axis)
    distance = 1
    while distance < count:
        other = lax.ppermute(cells, axis, [(i, i ^ distance) for i in range(count)])
        cells = jnp.maximum(cells, other)
        distance *= 2
    return cells


def smooth_both(values, spacing):
    for dim in (2, 1):
        count = values.shape[dim] - 4 * spacing
        total = taps[0] * lax.slice_in_dim(values, 0, count, axis=dim)
        for tap_index in range(1, 5):
            start = tap_index * spacing
            total = total + taps[tap_index] * lax.slice_in_dim(
                values, start, start + count, axis=dim
            )
        values = total
    return values


def real_dft(parts):
    count = len(parts)
    if count == 1:
        return [(parts[0], None)]
    if count == 2:
        return [(parts[0] + parts[1], None), (parts[0] - parts[1], None)]
    even = real_dft(parts[0::2])
    odd = real_dft(parts[1::2])
    out = [None] * (count // 2 + 1)
    for k in range(count // 4 + 1):
        turned = spin(odd[k], -2.0 * math.pi * k / count)
        out[k] = pair_add(even[k], turned)
        low = pair_sub(even[k], turned)
        out[count // 2 - k] = (low[0], None if low[1] is None else -low[1])
    out[0] = (out[0][0], None)
    out[count // 2] = (out[count // 2][0], None)
    return out


def real_inverse_dft(pairs):
    count = 2 * (len(pairs) - 1)
    if count == 2:
        return [pairs[0][0] + pairs[1][0], pairs[0][0] - pairs[1][0]]
    even, odd = [], []
    for k in range(count // 4 + 1):
        low = pairs[k]
        high = pairs[count // 2 - k]
        high = (high[0], None if high[1] is None else -high[1])
        even.append(pair_add(low, high))
        odd.append(spin(pair_sub(low, high), 2.0 * math.pi * k / count))
    for half in (even, odd):
        half[0] = (half[0][0], None)
        half[-1] = (half[-1][0], None)
    even = real_inverse_dft(even)
    odd = real_inverse_dft(odd)
    return [cells for both in zip(even, odd) for cells in both]


def complex_dft(pairs, sign):
    count = len(pairs)
    if count == 1:
        return pairs
    even = complex_dft(pairs[0::2], sign)
    odd = complex_dft(pairs[1::2], sign)
    turned = [spin(odd[k], sign * 2.0 * math.pi * k / count) for k in range(count // 2)]
    return [pair_add(a, b) for a, b in zip(even, turned)] + [
        pair_sub(a, b) for a, b in zip(even, turned)
    ]


def pair_add(a, b):
    if a[1] is None or b[1] is None:
        return (a[0] + b[0], a[1] if b[1] is None else b[1])
    return (a[0] + b[0], a[1] + b[1])


def pair_sub(a, b):
    if b[1] is None:
        return (a[0] - b[0], a[1])
    return (a[0] - b[0], -b[1] if a[1] is None else a[1] - b[1])


def spin(pair, angle):
    quarter = angle / (0.5 * math.pi)
    turns = round(quarter)
    real, imag = pair
    if abs(quarter - turns) < 1e-9:
        turns %= 4
        if turns == 0:
            return pair
        if turns == 2:
            return (-real, None if imag is None else -imag)
        if imag is None:
            return (jnp.zeros_like(real), real if turns == 1 else -real)
        return (-imag, real) if turns == 1 else (imag, -real)
    cosine, sine = math.cos(angle), math.sin(angle)
    if imag is None:
        return (real * cosine, real * sine)
    if abs(abs(cosine) - abs(sine)) < 1e-9:
        a, b = math.copysign(1.0, cosine), math.copysign(1.0, sine)
        root = abs(cosine)
        first = real if a > 0 else -real
        second = imag if b > 0 else -imag
        third = real if b > 0 else -real
        fourth = imag if a > 0 else -imag
        return ((first - second) * root, (third + fourth) * root)
    return (real * cosine - imag * sine, real * sine + imag * cosine)


def split(cells):
    high = cells.astype(jnp.bfloat16)
    return high, (cells - high.astype(jnp.float32)).astype(jnp.bfloat16)


def dot(a, b):
    return jnp.dot(a, b, preferred_element_type=jnp.float32)


def split_table(table):
    high = table.astype(np.float32).astype(ml_dtypes.bfloat16)
    low = (table - high.astype(np.float64)).astype(np.float32).astype(ml_dtypes.bfloat16)
    return np.stack([high, low], axis=-3)


def group_columns(length, count, group):
    radix = 2 * count
    lanes = length // radix
    spots = np.arange(lanes)
    if group:
        return group + radix * spots
    half = lanes // 2
    return np.where(spots < half, radix * spots, count + radix * (spots - half))


def row_tables(length, count):
    radix = 2 * count
    lanes = length // radix
    half = lanes // 2
    spots = np.arange(lanes)
    there, back = [], []
    for group in range(count):
        columns = group_columns(length, count, group)
        angles = 2.0 * np.pi * (np.outer(spots, columns) % length) / length
        cosine, sine = np.cos(angles), np.sin(angles)
        ahead = np.zeros((2, lanes, 2, lanes))
        behind = np.zeros((2, lanes, 2, lanes))
        if group:
            ahead[0, :, 0], ahead[0, :, 1] = cosine, -sine
            ahead[1, :, 0], ahead[1, :, 1] = sine, cosine
            behind[0, :, 0], behind[0, :, 1] = cosine.T, sine.T
            behind[1, :, 0], behind[1, :, 1] = -sine.T, cosine.T
        else:
            for part, where in enumerate((slice(0, half), slice(half, lanes))):
                ahead[part, :, 0, where] = cosine[:, where]
                ahead[part, :, 1, where] = -sine[:, where]
                behind[0, where, part] = 2.0 * cosine[:, where].T
                behind[1, where, part] = -2.0 * sine[:, where].T
            ahead[0, :, 1, 0] = (-1.0) ** spots
            behind[0, 0, 0] = 1.0
            behind[1, 0, 0] = (-1.0) ** spots
        there.append(ahead.reshape(2 * lanes, 2 * lanes))
        back.append(behind.reshape(2 * lanes, 2 * lanes) / float(length) ** 2)
    return split_table(np.stack(there)), split_table(np.stack(back))


def column_tables(length, count, steps):
    size = length // steps
    each = size // count
    quarter = each // 4
    order = np.r_[0:quarter, each - quarter : each, quarter : each - quarter]
    order = (np.arange(count)[:, None] * each + order[None]).reshape(-1)
    order = np.concatenate([order, size + order])
    spots = np.arange(size)
    there = []
    for step in range(steps):
        angles = 2.0 * np.pi * ((np.outer(spots, steps * spots + step)) % length) / length
        cosine, sine = np.cos(angles), np.sin(angles)
        there.append(np.block([[cosine, sine], [-sine, cosine]]))
    there = np.stack(there)
    return split_table(there), split_table(np.swapaxes(there, 1, 2)[:, order])


def weight_tables(length, count):
    width = length // count
    lanes = length // (2 * count)
    per_class = width // (2 * count)
    packs = lanes // (2 * per_class)
    radix = 2 * count

    def classes(group):
        return (group, radix - group) if group else (0, count)

    pick = np.zeros((packs, width, count, lanes))
    for group in range(count):
        for which, kind in enumerate(classes(group)):
            for q in range(per_class):
                for pack in range(packs):
                    lane = pack * 2 * per_class + which * per_class + q
                    pick[pack, radix * q + kind, group, lane] = 1.0
    place = np.zeros((2, count, lanes, packs * 2 + 1, lanes))

    def slot(group, column, pack):
        column %= length
        source, rest = divmod(column, width)
        which = classes(group).index(rest % radix)
        return source, pack * 2 * per_class + which * per_class + rest // radix

    for version, group in ((0, 0), (1, 1)):
        columns = group_columns(length, count, group)
        for pack in range(packs):
            for lane in range(lanes):
                column = int(columns[lane])
                mates = [(column, 0, 0.5), (-column, 1, 0.5)]
                if group == 0 and lane == 0:
                    mates = [(c, s, 0.25) for c in (0, length // 2) for s in (0, 1)]
                for mate, side, value in mates:
                    source, where = slot(group, mate, pack)
                    place[version, source, where, pack * 2 + side, lane] += value
            if group == 0:
                for mate, value in ((0, 0.25), (length // 2, -0.25)):
                    source, where = slot(group, mate, pack)
                    place[version, source, where, packs * 2, pack] += value
    flip = np.zeros((lanes, 2 * lanes))
    flip[np.arange(1, lanes), lanes - np.arange(1, lanes)] = 1.0
    flip[0, lanes] = 1.0
    as_half = lambda table: table.astype(np.float32).astype(ml_dtypes.bfloat16)
    return (
        as_half(pick.reshape(packs * width, count * lanes)),
        as_half(place.reshape(2, count * lanes, (packs * 2 + 1) * lanes)),
        as_half(flip),
    )


def busy(microseconds):
    return pl.CostEstimate(
        flops=0, bytes_accessed=int(microseconds * 3.5e6), transcendentals=0
    )


def whole_call(body, out_shapes, scratch, name, microseconds):
    return pl.pallas_call(
        body,
        out_shape=out_shapes,
        scratch_shapes=scratch,
        compiler_params=pltpu.CompilerParams(vmem_limit_bytes=vmem_bytes),
        name=name,
        cost_estimate=busy(microseconds),
    )


def row_forward_body(steps, x_ref, table_ref, out_ref, held):
    groups, _, height, lanes = out_ref.shape
    each = height // steps
    for start in range(0, height, 16):
        rows = pl.ds(start, 16)
        tiles = [x_ref[rows, pl.ds(lanes * t, lanes)] for t in range(2 * groups)]
        pairs = real_dft(tiles)
        pairs = [(pairs[0][0], pairs[groups][0])] + pairs[1:groups]
        for group in range(groups):
            high, low = split(jnp.concatenate(pairs[group], axis=1))
            held[0, group, rows, :] = high
            held[1, group, rows, :] = low
    for group in range(groups):
        done = (
            dot(held[0, group], table_ref[group, 0])
            + dot(held[1, group], table_ref[group, 0])
            + dot(held[0, group], table_ref[group, 1])
        )
        for start in range(0, height, 8):
            spread = pl.ds(start % steps * each + start // steps, 8, stride=each)
            out_ref[group, 0, spread, :] = done[start : start + 8, :lanes]
            out_ref[group, 1, spread, :] = done[start : start + 8, lanes:]


def row_inverse_body(
    steps, in_ref, table_ref, est_ref, dirty_ref, old_ref, res_ref, half_ref, held
):
    del old_ref
    groups, _, chunk, lanes = in_ref.shape
    parts, _, wide = half_ref.shape
    each = chunk // steps
    block = est_ref.shape[0]
    turn = pl.program_id(0)

    @pl.when(turn == 0)
    def _():
        for group in range(groups):
            halves = []
            for part in range(2):
                pieces = [
                    in_ref[
                        group,
                        part,
                        pl.ds(start % steps * each + start // steps, 8, stride=each),
                        :,
                    ]
                    for start in range(0, chunk, 8)
                ]
                halves.append(jnp.concatenate(pieces, axis=0))
            high, low = split(jnp.concatenate(halves, axis=1))
            held[group] = (
                dot(high, table_ref[group, 0])
                + dot(low, table_ref[group, 0])
                + dot(high, table_ref[group, 1])
            )

    per = wide // lanes
    lane_ids = lax.broadcasted_iota(jnp.int32, (8, lanes), 1)
    sides = [None] * parts
    for start in range(0, block, 8):
        rows = pl.ds(start, 8)
        chunk_rows = pl.ds(pl.multiple_of(turn * block + start, 8), 8)
        pairs = [
            (held[group, chunk_rows, pl.ds(0, lanes)], held[group, chunk_rows, pl.ds(lanes, lanes)])
            for group in range(groups)
        ]
        pairs = [(pairs[0][0], None)] + pairs[1:] + [(pairs[0][1], None)]
        tiles = real_inverse_dft(pairs)
        for t in range(2 * groups):
            where = pl.ds(lanes * t, lanes)
            residual = dirty_ref[rows, where] - tiles[t]
            res_ref[rows, where] = residual
            tiles[t] = est_ref[rows, where] + step_size * residual
            half_ref[t // per, chunk_rows, pl.ds(lanes * (t % per), lanes)] = tiles[t]
        offset = start // 8 * 2 * rim % lanes
        for part in range(parts):
            done = jnp.zeros_like(tiles[0]) if offset == 0 else sides[part]
            if part > 0:
                turned = pltpu.roll(tiles[part * per - 1], (offset + rim) % lanes, 1)
                done = jnp.where((lane_ids >= offset) & (lane_ids < offset + rim), turned, done)
            if part < parts - 1:
                turned = pltpu.roll(tiles[(part + 1) * per], (offset + rim) % lanes, 1)
                done = jnp.where(
                    (lane_ids >= offset + rim) & (lane_ids < offset + 2 * rim), turned, done
                )
            sides[part] = done
            if offset + 2 * rim == lanes:
                spot = turn * (block // 8 * 2 * rim // lanes) + start // 8 * 2 * rim // lanes
                where = pl.ds(pl.multiple_of(spot * lanes, lanes), lanes)
                half_ref[part, pl.ds(chunk, 8), where] = done


def starlet_body(chans, q_ref, *refs):
    edges, cores = refs[:chans], refs[chans : 2 * chans]
    above, below = refs[2 * chans : 3 * chans], refs[3 * chans : 4 * chans]
    detail_ref, energy_ref, peak_ref, cells, across = refs[4 * chans :]
    _, _, height, part = detail_ref.shape
    margin = 8
    base = margin + halo_rows
    lanes = lane_count
    chunk = height // 2
    quarter = height // 4
    total = part + lanes
    no_left, no_right = q_ref[0] > 0, q_ref[1] > 0
    no_top, no_bottom = q_ref[2] > 0, q_ref[3] > 0
    lane_ids = lax.broadcasted_iota(jnp.int32, (8, total), 1)
    outside = ((lane_ids >= total - lanes // 2) & no_left) | (
        (lane_ids >= part) & (lane_ids < total - lanes // 2) & no_right
    )

    def fill(target, source, source_row, count, pack_row, group):
        cells[pl.ds(target, count), pl.ds(0, part)] = source[pl.ds(source_row, count), :]
        for i in range(count // 8):
            spot = (group + i) * 2 * rim
            tile = source[pl.ds(pack_row, 8), pl.ds(spot // lanes * lanes, lanes)]
            shift = (lanes - spot % lanes - rim) % lanes
            cells[pl.ds(target + 8 * i, 8), pl.ds(part, lanes)] = pltpu.roll(tile, shift, 1)

    for chan in range(chans):
        edge, core = edges[chan], cores[chan]
        fill(margin, above[chan], 0, halo_rows, halo_rows, (chunk - halo_rows) // 8)
        fill(base, edge, 0, quarter, chunk, 0)
        fill(base + quarter, core, 0, chunk, chunk, 0)
        fill(base + 3 * quarter, edge, quarter, quarter, chunk, quarter // 8)
        fill(base + height, below[chan], 0, halo_rows, halo_rows, 0)
        for level in range(3):
            gap = 1 << level
            blocks = (height + 2 * halo_rows) // 8

            def sweep(i, carry):
                rows = pl.ds(pl.multiple_of(margin + 8 * i, 8), 8)
                row = cells[rows, :]
                near = pltpu.roll(row, gap, 1) + pltpu.roll(row, total - gap, 1)
                far = pltpu.roll(row, 2 * gap, 1) + pltpu.roll(row, total - 2 * gap, 1)
                across[rows, :] = (far + 4.0 * near) + 6.0 * row
                return carry

            lax.fori_loop(0, blocks, sweep, 0, unroll=6)

            def down(i, carry, inner):
                start = margin + 8 * i
                if not isinstance(start, int):
                    start = pl.multiple_of(start, 8)
                rows = pl.ds(start, 8)
                window = across[pl.ds(start - 8, 24), :]
                near = window[8 - gap : 16 - gap] + window[8 + gap : 16 + gap]
                far = window[8 - 2 * gap : 16 - 2 * gap] + window[8 + 2 * gap : 16 + 2 * gap]
                smooth = ((far + 4.0 * near) + 6.0 * window[8:16]) * (1.0 / 256.0)
                if not inner:
                    gone = no_top if i < halo_rows // 8 else no_bottom
                    cells[rows, :] = jnp.where(gone | outside, 0.0, smooth)
                    return carry
                smooth = jnp.where(outside, 0.0, smooth)
                detail = cells[rows, pl.ds(0, part)] - smooth[:, :part]
                cells[rows, :] = smooth
                to = pl.ds(pl.multiple_of(8 * i - halo_rows, 8), 8)
                detail_ref[chan, level, to, :] = detail
                if level == 2:
                    detail_ref[chan, 3, to, :] = smooth[:, :part]
                square = detail * detail
                if chan:
                    square = square + energy_ref[level, to, :]
                energy_ref[level, to, :] = square
                if chan == chans - 1:
                    return jnp.maximum(carry, square)
                return carry

            skirt = halo_rows // 8
            if level < 2:
                for i in range(skirt):
                    down(i, 0, False)
                    down(blocks - 1 - i, 0, False)
            peak = lax.fori_loop(
                skirt,
                blocks - skirt,
                functools.partial(down, inner=True),
                jnp.zeros((8, part), jnp.float32),
                unroll=8,
            )
            if chan == chans - 1:
                most = peak[:, :lanes]
                for t in range(1, part // lanes):
                    most = jnp.maximum(most, peak[:, t * lanes : (t + 1) * lanes])
                peak_ref[level] = most


def shrink_body(chans, detail_ref, energy_ref, peak_ref, *out_refs):
    factors = []
    for level in range(3):
        threshold = fractions[level] * jnp.sqrt(jnp.max(peak_ref[level], keepdims=True))
        energy = jnp.sqrt(energy_ref[level])
        threshold = jnp.broadcast_to(threshold, energy.shape)
        factors.append(1.0 - threshold / jnp.maximum(energy, threshold))
    for chan in range(chans):
        total = detail_ref[chan, 3]
        for level in range(3):
            total = total + factors[level] * detail_ref[chan, level]
        out_refs[chan][...] = total


def join_body(me_ref, *refs):
    chans = len(refs) - 1
    part = refs[0].shape[1]
    for chan in range(chans):
        start = pl.multiple_of((me_ref[0] ^ chan) * part, part)
        refs[-1][:, pl.ds(start, part)] = refs[chan][...]


def column_body(
    steps, in_ref, there_ref, back_ref, weight_ref, mirror_ref, flip_ref, edge_ref, core_ref, held, made
):
    count, _, height, lanes = in_ref.shape
    each = height // steps
    size = each * count
    for step in range(steps):
        rows = pl.ds(step * each, each)
        block = jnp.concatenate(
            [in_ref[source, part, rows, :] for part in range(2) for source in range(count)],
            axis=0,
        )
        high, low = split(block)
        done = (
            dot(there_ref[step, 0], high)
            + dot(there_ref[step, 1], high)
            + dot(there_ref[step, 0], low)
        )
        held[0, step] = done[:size]
        held[1, step] = done[size:]

    def forward(chunk, carry):
        rows = pl.ds(pl.multiple_of(chunk * 8, 8), 8)
        pairs = [(held[0, step, rows, :], held[1, step, rows, :]) for step in range(steps)]
        for step, pair in enumerate(complex_dft(pairs, -1.0)):
            held[0, step, rows, :] = pair[0]
            held[1, step, rows, :] = pair[1]
        return carry

    lax.fori_loop(0, size // 8, forward, 0)
    for step in range(steps):
        facing = [
            jnp.concatenate([held[0, other], held[1, other]], axis=1)
            for other in (steps - 1 - step, (steps - step) % steps)
        ]
        high, low = split(jnp.concatenate(facing, axis=0))
        turned = dot(flip_ref[...], high) + dot(flip_ref[...], low)
        weight = weight_ref[step]
        mirror = mirror_ref[step]
        made[0, step] = weight * held[0, step] + mirror * turned[:, :lanes]
        made[1, step] = weight * held[1, step] - mirror * turned[:, lanes:]

    def backward(chunk, carry):
        rows = pl.ds(pl.multiple_of(chunk * 8, 8), 8)
        pairs = [(made[0, step, rows, :], made[1, step, rows, :]) for step in range(steps)]
        for step, pair in enumerate(complex_dft(pairs, 1.0)):
            made[0, step, rows, :] = pair[0]
            made[1, step, rows, :] = pair[1]
        return carry

    lax.fori_loop(0, size // 8, backward, 0)
    for step in range(steps):
        high, low = split(jnp.concatenate([made[0, step], made[1, step]], axis=0))
        done = (
            dot(back_ref[step, 0], high)
            + dot(back_ref[step, 1], high)
            + dot(back_ref[step, 0], low)
        )
        half = each // 2
        rows = pl.ds(step * half, half)
        for part in range(2):
            for target in range(count):
                start = part * size + target * each
                edge_ref[target, part, rows, :] = done[start : start + half]
                core_ref[target, part, rows, :] = done[start + half : start + each]


def weight_pick_body(w_ref, pick_ref, out_ref):
    count, _, lanes = out_ref.shape
    packs, _, width = w_ref.shape
    total = 0.0
    for pack in range(packs):
        high, low = split(w_ref[pack])
        chosen = pick_ref[pl.ds(pack * width, width), :]
        total = total + dot(high, chosen) + dot(low, chosen)
    for target in range(count):
        out_ref[target] = total[:, target * lanes : (target + 1) * lanes]


def weight_place_body(in_ref, place_ref, flip_ref, weight_ref, mirror_ref, held):
    count, depth, lanes = in_ref.shape
    steps, size, _ = weight_ref.shape
    packs = steps * size // depth
    total = 0.0
    for source in range(count):
        high, low = split(in_ref[source])
        chosen = place_ref[pl.ds(source * lanes, lanes), :]
        total = total + dot(high, chosen) + dot(low, chosen)
    inner = depth // size
    extra = total[:, 2 * packs * lanes :]
    first = lax.broadcasted_iota(jnp.int32, (size, lanes), 1) == 0
    for step in range(steps):
        pack, rest = divmod(step, inner)
        rows = slice(rest * size, (rest + 1) * size)
        lone = extra[rows]
        if pack:
            lone = pltpu.roll(lone, lanes - pack, 1)
        lone = jnp.where(first, lone, 0.0)
        mirror_ref[step] = lone
        weight_ref[step] = total[rows, 2 * pack * lanes : (2 * pack + 1) * lanes]
        held[step] = jnp.concatenate(
            [total[rows, (2 * pack + 1) * lanes : (2 * pack + 2) * lanes], lone], axis=1
        )
    for step in range(steps):
        high, low = split(
            jnp.concatenate([held[steps - 1 - step], held[(steps - step) % steps]], axis=0)
        )
        turned = dot(flip_ref[...], high) + dot(flip_ref[...], low)
        weight_ref[step] += turned[:, :lanes]
        mirror_ref[step] += turned[:, lanes:]


def filtered(values, dirty, weights):
    height, length = values.shape
    count = lax.axis_size("rows")
    lanes = length // (2 * count)
    steps = height // 16
    size = length // steps
    width = weights.shape[1]
    f32 = jnp.float32
    pick, place, flip = [jnp.asarray(table) for table in weight_tables(length, count)]
    there, back = [jnp.asarray(table) for table in row_tables(length, count)]
    down, up = [jnp.asarray(table) for table in column_tables(length, count, steps)]
    shape = lambda *dims: jax.ShapeDtypeStruct(dims, f32)
    packs = length * width // (count * lanes) // (length // count)
    packs = pick.shape[0] // width
    depth = length // packs

    sent = whole_call(weight_pick_body, shape(count, depth, lanes), [], "weight_pick", 6)(
        weights.reshape(packs, depth, width), pick
    )
    sent = lax.all_to_all(sent, "rows", 0, 0, tiled=True)
    ahead = whole_call(
        functools.partial(row_forward_body, steps),
        shape(count, 2, height, lanes),
        [pltpu.VMEM((2, count, height, 2 * lanes), jnp.bfloat16)],
        "row_forward",
        6,
    )(values, there)
    ahead = lax.all_to_all(ahead, "rows", 0, 0, tiled=True)
    mine = jnp.where(lax.axis_index("rows") == 0, place[0], place[1])
    weight, mirror = whole_call(
        weight_place_body,
        [shape(steps, size, lanes)] * 2,
        [pltpu.VMEM((steps, size, 2 * lanes), f32)],
        "weight_place",
        10,
    )(sent, mine, flip)
    half = height // 2
    edge, core = whole_call(
        functools.partial(column_body, steps),
        [shape(count, 2, half, lanes)] * 2,
        [pltpu.VMEM((2, steps, size, lanes), f32)] * 2,
        "column_filter",
        12,
    )(ahead, down, up, weight, mirror, flip)
    edge = lax.all_to_all(edge, "rows", 0, 0, tiled=True)
    core = lax.all_to_all(core, "rows", 0, 0, tiled=True)
    chans = lax.axis_size("chan")
    part = length // chans
    quarter = height // 4

    def row_inverse(cells, old, blocks):
        rows_spec = pl.BlockSpec((quarter, length), lambda i: (blocks[0] + i * blocks[1], 0))
        whole = lambda *dims: pl.BlockSpec(dims, lambda i: (0,) * len(dims))
        return pl.pallas_call(
            functools.partial(row_inverse_body, steps),
            grid=(2,),
            in_specs=[
                whole(*cells.shape),
                whole(*back.shape),
                rows_spec,
                rows_spec,
                pl.BlockSpec(memory_space=pl.ANY),
            ],
            out_specs=[rows_spec, whole(chans, half + 8, part)],
            out_shape=[shape(height, length), shape(chans, half + 8, part)],
            scratch_shapes=[pltpu.VMEM((count, half, 2 * lanes), f32)],
            input_output_aliases={4: 0} if old is not dirty else {},
            compiler_params=pltpu.CompilerParams(vmem_limit_bytes=vmem_bytes),
            name="row_inverse",
        cost_estimate=busy(5),
        )(cells, back, values, dirty, old)

    def over_chans(cells):
        me = lax.axis_index("chan")
        got = []
        for turn in range(chans):
            mine = lax.dynamic_index_in_dim(cells, me ^ turn, 0, keepdims=False)
            if turn:
                mine = lax.ppermute(mine, "chan", [(i, i ^ turn) for i in range(chans)])
            got.append(mine)
        return got

    residual, outer = row_inverse(edge, dirty, (0, 3))
    outer = over_chans(outer)
    core, *outer = lax.optimization_barrier((core, *outer))
    residual, inner = row_inverse(core, residual, (1, 1))
    inner = over_chans(inner)
    ahead_pairs = [(i, i + 1) for i in range(count - 1)]
    back_pairs = [(i + 1, i) for i in range(count - 1)]
    last = jnp.stack([cells[half - halo_rows :] for cells in outer])
    first = jnp.stack(
        [jnp.concatenate([cells[:halo_rows], cells[half:]], axis=0) for cells in outer]
    )
    last = lax.ppermute(last, "rows", ahead_pairs)
    first = lax.ppermute(first, "rows", back_pairs)
    above = [last[c] for c in range(chans)]
    below = [first[c] for c in range(chans)]
    chan_id, row_id = lax.axis_index("chan"), lax.axis_index("rows")
    at_end = jnp.stack(
        [chan_id == 0, chan_id == chans - 1, row_id == 0, row_id == count - 1]
    ).astype(jnp.int32)
    vmem = pl.BlockSpec(memory_space=pltpu.VMEM)
    details, energy, peaks = pl.pallas_call(
        functools.partial(starlet_body, chans),
        in_specs=[pl.BlockSpec(memory_space=pltpu.SMEM)] + [vmem] * (4 * chans),
        out_specs=[vmem] * 3,
        out_shape=[shape(chans, 4, height, part), shape(3, height, part), shape(3, 8, lanes)],
        scratch_shapes=[
            pltpu.VMEM((height + 2 * halo_rows + 16, part + lanes), f32),
            pltpu.VMEM((height + 2 * halo_rows + 16, part + lanes), f32),
        ],
        compiler_params=pltpu.CompilerParams(vmem_limit_bytes=vmem_bytes),
        name="starlet",
        cost_estimate=busy(25),
    )(at_end, *outer, *inner, *above, *below)
    peaks = max_over(max_over(peaks, "rows"), "chan")
    thick = height // 4
    shrunk = pl.pallas_call(
        functools.partial(shrink_body, chans),
        grid=(4,),
        in_specs=[
            pl.BlockSpec((chans, 4, thick, part), lambda i: (0, 0, i, 0)),
            pl.BlockSpec((3, thick, part), lambda i: (0, i, 0)),
            pl.BlockSpec((3, 8, lanes), lambda i: (0, 0, 0)),
        ],
        out_specs=[pl.BlockSpec((thick, part), lambda i: (i, 0))] * chans,
        out_shape=[shape(height, part)] * chans,
        compiler_params=pltpu.CompilerParams(vmem_limit_bytes=vmem_bytes),
        name="shrink",
        cost_estimate=busy(6),
    )(details, energy, peaks)
    shrunk = [shrunk[0]] + [
        lax.ppermute(shrunk[turn], "chan", [(i, i ^ turn) for i in range(chans)])
        for turn in range(1, chans)
    ]
    new_estimate = pl.pallas_call(
        join_body,
        grid_spec=pltpu.PrefetchScalarGridSpec(
            num_scalar_prefetch=1,
            grid=(4,),
            in_specs=[pl.BlockSpec((thick, part), lambda i, me: (i, 0))] * chans,
            out_specs=pl.BlockSpec((thick, length), lambda i, me: (i, 0)),
        ),
        out_shape=shape(height, length),
        name="join",
        cost_estimate=busy(4),
    )(jnp.reshape(chan_id, (1,)).astype(jnp.int32), *shrunk)
    return new_estimate, residual


def filtered_plain(values, dirty, weights):
    height, length = values.shape
    row_count = lax.axis_size("rows")
    narrow = length // row_count
    spec_real, spec_imag = dft_last(values, jnp.zeros_like(values), -1.0)
    spec_real = spec_real.reshape(height, row_count, narrow)
    spec_imag = spec_imag.reshape(height, row_count, narrow)
    col_real, col_imag = columns_forward(
        (
            lax.all_to_all(spec_real, "rows", split_axis=1, concat_axis=0, tiled=True),
            lax.all_to_all(spec_imag, "rows", split_axis=1, concat_axis=0, tiled=True),
        )
    )
    prod_real = weights * col_real[:, 0, :]
    prod_imag = weights * col_imag[:, 0, :]
    back_real, back_imag = dft_first(prod_real, prod_imag, 1.0)
    back_real = back_real.reshape(row_count, height, narrow)
    back_imag = back_imag.reshape(row_count, height, narrow)
    blurred = rows_inverse(
        (
            lax.all_to_all(back_real, "rows", split_axis=0, concat_axis=2, tiled=True),
            lax.all_to_all(back_imag, "rows", split_axis=0, concat_axis=2, tiled=True),
        )
    )[0]
    residual = dirty - blurred
    return residual, values + step_size * residual


def joined_plain(halfway):
    height, length = halfway.shape
    depth = 14
    chan_count = lax.axis_size("chan")
    part = length // chan_count
    padded = with_halo(halfway, (("rows", 0),), depth)
    padded = jnp.pad(padded, ((0, 0), (depth, depth)))
    pieces = jnp.stack(
        [padded[:, q * part : (q + 1) * part + 2 * depth] for q in range(chan_count)]
    )
    current = lax.all_to_all(pieces, "chan", split_axis=0, concat_axis=0, tiled=True)
    row_ids = lax.axis_index("rows") * height - depth + lax.iota(jnp.int32, height + 2 * depth)
    col_ids = lax.axis_index("chan") * part - depth + lax.iota(jnp.int32, part + 2 * depth)
    margin = depth
    details = []
    for scale_level in range(3):
        reach = 2 << scale_level
        smoother = smooth_both(current, 1 << scale_level)
        row_ids = row_ids[reach:-reach]
        col_ids = col_ids[reach:-reach]
        inside = ((row_ids >= 0) & (row_ids < length))[:, None] & (
            (col_ids >= 0) & (col_ids < length)
        )[None, :]
        smoother = jnp.where(inside[None], smoother, 0.0)
        new_margin = margin - reach
        details.append(
            current[:, margin : margin + height, margin : margin + part]
            - smoother[:, new_margin : new_margin + height, new_margin : new_margin + part]
        )
        current = smoother
        margin = new_margin
    energies = [jnp.sum(detail * detail, axis=0) for detail in details]
    peaks = jnp.stack([jnp.broadcast_to(jnp.max(energy), (128,)) for energy in energies])
    peaks = max_over(max_over(peaks, "rows"), "chan")
    output = current
    for scale_level in range(3):
        threshold = fractions[scale_level] * jnp.sqrt(peaks[scale_level, 0])
        factor = 1.0 - threshold / jnp.maximum(jnp.sqrt(energies[scale_level]), threshold)
        output = output + factor[None] * details[scale_level]
    output = lax.all_to_all(output, "chan", split_axis=0, concat_axis=2, tiled=True)[0]
    return output


def shards(estimate, dirty_image, psf_weights):
    values, dirty, weights = estimate[0], dirty_image[0], psf_weights[0]
    height, length = values.shape
    row_count, chan_count = lax.axis_size("rows"), lax.axis_size("chan")
    whole_tiles = length == 2 * row_count * lane_count and length % (chan_count * lane_count) == 0
    if whole_tiles and chan_count & (chan_count - 1) == 0:
        new_estimate, residual = filtered(values, dirty, weights)
    else:
        residual, halfway = filtered_plain(values, dirty, weights)
        new_estimate = joined_plain(halfway)
    return (new_estimate[None], residual[None])


def solution(mesh):
    return jax.shard_map(
        shards,
        mesh=mesh,
        in_specs=(P("chan", "rows", None), P("chan", "rows", None), P("chan", None, "rows")),
        out_specs=(P("chan", "rows", None), P("chan", "rows", None)),
        check_vma=False,
    )
```

```python
import functools
import math

import jax
import jax.numpy as jnp
import ml_dtypes
import numpy as np
from jax import lax
from jax.experimental import pallas as pl
from jax.experimental.pallas import tpu as pltpu
from jax.sharding import PartitionSpec as P

fractions = (0.03, 0.02, 0.015)
taps = (0.0625, 0.25, 0.375, 0.25, 0.0625)
step_size = 0.9
inner_length = 128
highest = lax.Precision.HIGHEST
lane_count = 128
vmem_bytes = 56 * 1024 * 1024
rim = 16
halo_rows = 16
unroll = 2


def with_halo(cells, sides, width):
    for axis, dim in sides:
        count = lax.axis_size(axis)
        ends = count - 1
        head = lax.slice_in_dim(cells, 0, width, axis=dim)
        tail = lax.slice_in_dim(cells, cells.shape[dim] - width, cells.shape[dim], axis=dim)
        cells = jnp.concatenate(
            [
                lax.ppermute(tail, axis, [(i, (i + 1) % count) for i in range(ends)]),
                cells,
                lax.ppermute(head, axis, [((i + 1) % count, i) for i in range(ends)]),
            ],
            axis=dim,
        )
    return cells


def phase_table(first_count, second_count, length, sign):
    first_ids = lax.iota(jnp.int32, first_count)
    second_ids = lax.iota(jnp.int32, second_count)
    angles = (first_ids[:, None] * second_ids[None, :] % length).astype(jnp.float32) * (
        2.0 * math.pi / length
    )
    return (jnp.cos(angles), sign * jnp.sin(angles))


def dft_last(real_in, imag_in, sign):
    batch, length = real_in.shape
    outer = length // inner_length
    real_part = real_in.reshape(batch, outer, inner_length)
    imag_part = imag_in.reshape(batch, outer, inner_length)
    cos_small, sin_small = phase_table(outer, outer, outer, sign)
    first_real = jnp.einsum("kn,bnm->bkm", cos_small, real_part, precision=highest) - jnp.einsum(
        "kn,bnm->bkm", sin_small, imag_part, precision=highest
    )
    first_imag = jnp.einsum("kn,bnm->bkm", cos_small, imag_part, precision=highest) + jnp.einsum(
        "kn,bnm->bkm", sin_small, real_part, precision=highest
    )
    cos_twist, sin_twist = phase_table(outer, inner_length, length, sign)
    twist_real = first_real * cos_twist - first_imag * sin_twist
    twist_imag = first_imag * cos_twist + first_real * sin_twist
    cos_large, sin_large = phase_table(inner_length, inner_length, inner_length, sign)
    last_real = jnp.einsum("bkm,mj->bkj", twist_real, cos_large, precision=highest) - jnp.einsum(
        "bkm,mj->bkj", twist_imag, sin_large, precision=highest
    )
    last_imag = jnp.einsum("bkm,mj->bkj", twist_imag, cos_large, precision=highest) + jnp.einsum(
        "bkm,mj->bkj", twist_real, sin_large, precision=highest
    )
    return (
        jnp.transpose(last_real, (0, 2, 1)).reshape(batch, length),
        jnp.transpose(last_imag, (0, 2, 1)).reshape(batch, length),
    )


def dft_first(real_in, imag_in, sign):
    length, width = real_in.shape
    outer = length // inner_length
    real_part = real_in.reshape(outer, inner_length, width)
    imag_part = imag_in.reshape(outer, inner_length, width)
    cos_small, sin_small = phase_table(outer, outer, outer, sign)
    first_real = jnp.einsum("kn,nmw->kmw", cos_small, real_part, precision=highest) - jnp.einsum(
        "kn,nmw->kmw", sin_small, imag_part, precision=highest
    )
    first_imag = jnp.einsum("kn,nmw->kmw", cos_small, imag_part, precision=highest) + jnp.einsum(
        "kn,nmw->kmw", sin_small, real_part, precision=highest
    )
    cos_twist, sin_twist = phase_table(outer, inner_length, length, sign)
    cos_twist = cos_twist[:, :, None]
    sin_twist = sin_twist[:, :, None]
    twist_real = first_real * cos_twist - first_imag * sin_twist
    twist_imag = first_imag * cos_twist + first_real * sin_twist
    cos_large, sin_large = phase_table(inner_length, inner_length, inner_length, sign)
    last_real = jnp.einsum("kmw,mj->kjw", twist_real, cos_large, precision=highest) - jnp.einsum(
        "kmw,mj->kjw", twist_imag, sin_large, precision=highest
    )
    last_imag = jnp.einsum("kmw,mj->kjw", twist_imag, cos_large, precision=highest) + jnp.einsum(
        "kmw,mj->kjw", twist_real, sin_large, precision=highest
    )
    return (
        jnp.transpose(last_real, (1, 0, 2)).reshape(length, width),
        jnp.transpose(last_imag, (1, 0, 2)).reshape(length, width),
    )


def columns_forward(pieces):
    real_out, imag_out = dft_first(pieces[0][:, 0, :], pieces[1][:, 0, :], -1.0)
    return (real_out[:, None, :], imag_out[:, None, :])


def rows_inverse(pieces):
    real_in = pieces[0][0]
    imag_in = pieces[1][0]
    length = real_in.shape[1]
    real_out, imag_out = dft_last(real_in, imag_in, 1.0)
    return (real_out * (1.0 / (length * length)))[None]


def max_over(cells, axis, distances):
    count = lax.axis_size(axis)
    others = [
        lax.ppermute(cells, axis, [(i, i ^ distance) for i in range(count)])
        for distance in distances
    ]
    for other in others:
        cells = jnp.maximum(cells, other)
    return cells


def smooth_both(values, spacing):
    for dim in (2, 1):
        count = values.shape[dim] - 4 * spacing
        total = taps[0] * lax.slice_in_dim(values, 0, count, axis=dim)
        for tap_index in range(1, 5):
            start = tap_index * spacing
            total = total + taps[tap_index] * lax.slice_in_dim(
                values, start, start + count, axis=dim
            )
        values = total
    return values


def real_dft(parts):
    count = len(parts)
    if count == 1:
        return [(parts[0], None)]
    if count == 2:
        return [(parts[0] + parts[1], None), (parts[0] - parts[1], None)]
    even = real_dft(parts[0::2])
    odd = real_dft(parts[1::2])
    out = [None] * (count // 2 + 1)
    for k in range(count // 4 + 1):
        turned = spin(odd[k], -2.0 * math.pi * k / count)
        out[k] = pair_add(even[k], turned)
        low = pair_sub(even[k], turned)
        out[count // 2 - k] = (low[0], None if low[1] is None else -low[1])
    out[0] = (out[0][0], None)
    out[count // 2] = (out[count // 2][0], None)
    return out


def real_inverse_dft(pairs):
    count = 2 * (len(pairs) - 1)
    if count == 2:
        return [pairs[0][0] + pairs[1][0], pairs[0][0] - pairs[1][0]]
    even, odd = [], []
    for k in range(count // 4 + 1):
        low = pairs[k]
        high = pairs[count // 2 - k]
        high = (high[0], None if high[1] is None else -high[1])
        even.append(pair_add(low, high))
        odd.append(spin(pair_sub(low, high), 2.0 * math.pi * k / count))
    for half in (even, odd):
        half[0] = (half[0][0], None)
        half[-1] = (half[-1][0], None)
    even = real_inverse_dft(even)
    odd = real_inverse_dft(odd)
    return [cells for both in zip(even, odd) for cells in both]


def complex_dft(pairs, sign):
    count = len(pairs)
    if count == 1:
        return pairs
    even = complex_dft(pairs[0::2], sign)
    odd = complex_dft(pairs[1::2], sign)
    turned = [spin(odd[k], sign * 2.0 * math.pi * k / count) for k in range(count // 2)]
    return [pair_add(a, b) for a, b in zip(even, turned)] + [
        pair_sub(a, b) for a, b in zip(even, turned)
    ]


def pair_add(a, b):
    if a[1] is None or b[1] is None:
        return (a[0] + b[0], a[1] if b[1] is None else b[1])
    return (a[0] + b[0], a[1] + b[1])


def pair_sub(a, b):
    if b[1] is None:
        return (a[0] - b[0], a[1])
    return (a[0] - b[0], -b[1] if a[1] is None else a[1] - b[1])


def spin(pair, angle):
    quarter = angle / (0.5 * math.pi)
    turns = round(quarter)
    real, imag = pair
    if abs(quarter - turns) < 1e-9:
        turns %= 4
        if turns == 0:
            return pair
        if turns == 2:
            return (-real, None if imag is None else -imag)
        if imag is None:
            return (jnp.zeros_like(real), real if turns == 1 else -real)
        return (-imag, real) if turns == 1 else (imag, -real)
    cosine, sine = math.cos(angle), math.sin(angle)
    if imag is None:
        return (real * cosine, real * sine)
    if abs(abs(cosine) - abs(sine)) < 1e-9:
        a, b = math.copysign(1.0, cosine), math.copysign(1.0, sine)
        root = abs(cosine)
        first = real if a > 0 else -real
        second = imag if b > 0 else -imag
        third = real if b > 0 else -real
        fourth = imag if a > 0 else -imag
        return ((first - second) * root, (third + fourth) * root)
    return (real * cosine - imag * sine, real * sine + imag * cosine)


def split(cells):
    high = cells.astype(jnp.bfloat16)
    return high, (cells - high.astype(jnp.float32)).astype(jnp.bfloat16)


def dot(a, b):
    return jnp.dot(a, b, preferred_element_type=jnp.float32)


def split_table(table):
    high = table.astype(np.float32).astype(ml_dtypes.bfloat16)
    low = (table - high.astype(np.float64)).astype(np.float32).astype(ml_dtypes.bfloat16)
    return np.stack([high, low], axis=-3)


def group_columns(length, count, group):
    radix = 2 * count
    lanes = length // radix
    spots = np.arange(lanes)
    if group:
        return group + radix * spots
    half = lanes // 2
    return np.where(spots < half, radix * spots, count + radix * (spots - half))


def row_tables(length, count):
    radix = 2 * count
    lanes = length // radix
    half = lanes // 2
    spots = np.arange(lanes)
    there, back = [], []
    for group in range(count):
        columns = group_columns(length, count, group)
        angles = 2.0 * np.pi * (np.outer(spots, columns) % length) / length
        cosine, sine = np.cos(angles), np.sin(angles)
        ahead = np.zeros((2, lanes, 2, lanes))
        behind = np.zeros((2, lanes, 2, lanes))
        if group:
            ahead[0, :, 0], ahead[0, :, 1] = cosine, -sine
            ahead[1, :, 0], ahead[1, :, 1] = sine, cosine
            behind[0, :, 0], behind[0, :, 1] = cosine.T, sine.T
            behind[1, :, 0], behind[1, :, 1] = -sine.T, cosine.T
        else:
            for part, where in enumerate((slice(0, half), slice(half, lanes))):
                ahead[part, :, 0, where] = cosine[:, where]
                ahead[part, :, 1, where] = -sine[:, where]
                behind[0, where, part] = 2.0 * cosine[:, where].T
                behind[1, where, part] = -2.0 * sine[:, where].T
            ahead[0, :, 1, 0] = (-1.0) ** spots
            behind[0, 0, 0] = 1.0
            behind[1, 0, 0] = (-1.0) ** spots
        there.append(ahead.reshape(2 * lanes, 2 * lanes))
        back.append(behind.reshape(2 * lanes, 2 * lanes) / float(length) ** 2)
    return split_table(np.stack(there)), split_table(np.stack(back))


def column_tables(length, count, steps):
    size = length // steps
    each = size // count
    quarter = each // 4
    order = np.r_[0:quarter, each - quarter : each, quarter : each - quarter]
    order = (np.arange(count)[:, None] * each + order[None]).reshape(-1)
    order = np.concatenate([order, size + order])
    spots = np.arange(size)
    there = []
    for step in range(steps):
        angles = 2.0 * np.pi * ((np.outer(spots, steps * spots + step)) % length) / length
        cosine, sine = np.cos(angles), np.sin(angles)
        there.append(np.block([[cosine, sine], [-sine, cosine]]))
    there = np.stack(there)
    return split_table(there), split_table(np.swapaxes(there, 1, 2)[:, order])


def weight_tables(length, count):
    width = length // count
    lanes = length // (2 * count)
    per_class = width // (2 * count)
    packs = lanes // (2 * per_class)
    radix = 2 * count

    def classes(group):
        return (group, radix - group) if group else (0, count)

    pick = np.zeros((packs, width, count, lanes))
    for group in range(count):
        for which, kind in enumerate(classes(group)):
            for q in range(per_class):
                for pack in range(packs):
                    lane = pack * 2 * per_class + which * per_class + q
                    pick[pack, radix * q + kind, group, lane] = 1.0
    place = np.zeros((2, count, lanes, packs * 2 + 1, lanes))

    def slot(group, column, pack):
        column %= length
        source, rest = divmod(column, width)
        which = classes(group).index(rest % radix)
        return source, pack * 2 * per_class + which * per_class + rest // radix

    for version, group in ((0, 0), (1, 1)):
        columns = group_columns(length, count, group)
        for pack in range(packs):
            for lane in range(lanes):
                column = int(columns[lane])
                mates = [(column, 0, 0.5), (-column, 1, 0.5)]
                if group == 0 and lane == 0:
                    mates = [(c, s, 0.25) for c in (0, length // 2) for s in (0, 1)]
                for mate, side, value in mates:
                    source, where = slot(group, mate, pack)
                    place[version, source, where, pack * 2 + side, lane] += value
            if group == 0:
                for mate, value in ((0, 0.25), (length // 2, -0.25)):
                    source, where = slot(group, mate, pack)
                    place[version, source, where, packs * 2, pack] += value
    flip = np.zeros((lanes, 2 * lanes))
    flip[np.arange(1, lanes), lanes - np.arange(1, lanes)] = 1.0
    flip[0, lanes] = 1.0
    as_half = lambda table: table.astype(np.float32).astype(ml_dtypes.bfloat16)
    return (
        as_half(pick.reshape(packs * width, count * lanes)),
        as_half(place.reshape(2, count * lanes, (packs * 2 + 1) * lanes)),
        as_half(flip),
    )


def busy(microseconds):
    return pl.CostEstimate(
        flops=0, bytes_accessed=int(microseconds * 3.5e6), transcendentals=0
    )


def whole_call(body, out_shapes, scratch, name, microseconds):
    return pl.pallas_call(
        body,
        out_shape=out_shapes,
        scratch_shapes=scratch,
        compiler_params=pltpu.CompilerParams(vmem_limit_bytes=vmem_bytes),
        name=name,
        cost_estimate=busy(microseconds),
    )


def row_forward_body(steps, x_ref, table_ref, out_ref, held):
    groups, _, height, lanes = out_ref.shape
    each = height // steps
    for start in range(0, height, 16):
        rows = pl.ds(start, 16)
        tiles = [x_ref[rows, pl.ds(lanes * t, lanes)] for t in range(2 * groups)]
        pairs = real_dft(tiles)
        pairs = [(pairs[0][0], pairs[groups][0])] + pairs[1:groups]
        for group in range(groups):
            high, low = split(jnp.concatenate(pairs[group], axis=1))
            held[0, group, rows, :] = high
            held[1, group, rows, :] = low
    for group in range(groups):
        done = (
            dot(held[0, group], table_ref[group, 0])
            + dot(held[1, group], table_ref[group, 0])
            + dot(held[0, group], table_ref[group, 1])
        )
        for start in range(0, height, 8):
            spread = pl.ds(start % steps * each + start // steps, 8, stride=each)
            out_ref[group, 0, spread, :] = done[start : start + 8, :lanes]
            out_ref[group, 1, spread, :] = done[start : start + 8, lanes:]


def row_inverse_body(
    steps, in_ref, table_ref, est_ref, dirty_ref, old_ref, res_ref, half_ref, held
):
    del old_ref
    groups, _, chunk, lanes = in_ref.shape
    parts, _, wide = half_ref.shape
    each = chunk // steps
    block = est_ref.shape[0]
    turn = pl.program_id(0)

    @pl.when(turn == 0)
    def _():
        for group in range(groups):
            halves = []
            for part in range(2):
                pieces = [
                    in_ref[
                        group,
                        part,
                        pl.ds(start % steps * each + start // steps, 8, stride=each),
                        :,
                    ]
                    for start in range(0, chunk, 8)
                ]
                halves.append(jnp.concatenate(pieces, axis=0))
            high, low = split(jnp.concatenate(halves, axis=1))
            held[group] = (
                dot(high, table_ref[group, 0])
                + dot(low, table_ref[group, 0])
                + dot(high, table_ref[group, 1])
            )

    per = wide // lanes
    lane_ids = lax.broadcasted_iota(jnp.int32, (8, lanes), 1)
    sides = [None] * parts
    for start in range(0, block, 8):
        rows = pl.ds(start, 8)
        chunk_rows = pl.ds(pl.multiple_of(turn * block + start, 8), 8)
        pairs = [
            (held[group, chunk_rows, pl.ds(0, lanes)], held[group, chunk_rows, pl.ds(lanes, lanes)])
            for group in range(groups)
        ]
        pairs = [(pairs[0][0], None)] + pairs[1:] + [(pairs[0][1], None)]
        tiles = real_inverse_dft(pairs)
        for t in range(2 * groups):
            where = pl.ds(lanes * t, lanes)
            residual = dirty_ref[rows, where] - tiles[t]
            res_ref[rows, where] = residual
            tiles[t] = est_ref[rows, where] + step_size * residual
            half_ref[t // per, chunk_rows, pl.ds(lanes * (t % per), lanes)] = tiles[t]
        offset = start // 8 * 2 * rim % lanes
        for part in range(parts):
            done = jnp.zeros_like(tiles[0]) if offset == 0 else sides[part]
            if part > 0:
                turned = pltpu.roll(tiles[part * per - 1], (offset + rim) % lanes, 1)
                done = jnp.where((lane_ids >= offset) & (lane_ids < offset + rim), turned, done)
            if part < parts - 1:
                turned = pltpu.roll(tiles[(part + 1) * per], (offset + rim) % lanes, 1)
                done = jnp.where(
                    (lane_ids >= offset + rim) & (lane_ids < offset + 2 * rim), turned, done
                )
            sides[part] = done
            if offset + 2 * rim == lanes:
                spot = turn * (block // 8 * 2 * rim // lanes) + start // 8 * 2 * rim // lanes
                where = pl.ds(pl.multiple_of(spot * lanes, lanes), lanes)
                half_ref[part, pl.ds(chunk, 8), where] = done


def starlet_body(chans, spans, fills, ends_ref, *refs):
    sources, (detail_ref, peak_ref, ping, pong) = refs[:-4], refs[-4:]
    part = detail_ref.shape[3]
    lanes = lane_count
    tiles = part // lanes
    total = part + lanes
    no_left, no_right = ends_ref[0] > 0, ends_ref[1] > 0
    no_top, no_bottom = ends_ref[2] > 0, ends_ref[3] > 0
    lane_ids = lax.broadcasted_iota(jnp.int32, (8, lanes), 1)
    outside = ((lane_ids >= lanes // 2) & no_left) | ((lane_ids < lanes // 2) & no_right)
    for chan in range(chans):
        for target, index, source_row, count, pack_row, group in fills:
            source = sources[index * chans + chan]
            to = pl.ds(8 + target, count)
            ping[chan, to, pl.ds(0, part)] = source[pl.ds(source_row, count), :]
            for i in range(count // 8):
                spot = (group + i) * 2 * rim
                tile = source[pl.ds(pack_row, 8), pl.ds(spot // lanes * lanes, lanes)]
                shift = (lanes - spot % lanes - rim) % lanes
                to = pl.ds(8 + target + 8 * i, 8)
                ping[chan, to, pl.ds(part, lanes)] = pltpu.roll(tile, shift, 1)

    skirt = halo_rows // 8
    peaks = [jnp.zeros((8, part), jnp.float32)] * 3
    for start, blocks, out_start, top, bottom in spans:
        for level in range(3):
            gap = 1 << level
            before, after = (ping, pong) if level % 2 == 0 else (pong, ping)

            def step(i, peak, level, gap, before, after):
                base = 8 + start + 8 * i
                if not isinstance(i, int):
                    base = pl.multiple_of(base, 8)
                inner = not isinstance(i, int)
                energy = 0.0
                for chan in range(chans):
                    window = before[chan, pl.ds(base - 8, 24), :]
                    near = window[8 - gap : 16 - gap] + window[8 + gap : 16 + gap]
                    far = window[8 - 2 * gap : 16 - 2 * gap] + window[8 + 2 * gap : 16 + 2 * gap]
                    row = (far + 4.0 * near) + 6.0 * window[8:16]
                    near = pltpu.roll(row, gap, 1) + pltpu.roll(row, total - gap, 1)
                    far = pltpu.roll(row, 2 * gap, 1) + pltpu.roll(row, total - 2 * gap, 1)
                    smooth = ((far + 4.0 * near) + 6.0 * row) * (1.0 / 256.0)
                    whole = smooth[:, :part]
                    if level < 2:
                        side = jnp.where(outside, 0.0, smooth[:, part:])
                        if not inner and (top if i < skirt else bottom):
                            gone = no_top if i < skirt else no_bottom
                            side = jnp.where(gone, 0.0, side)
                            after[chan, pl.ds(base, 8), pl.ds(0, part)] = jnp.where(
                                gone, 0.0, whole
                            )
                        else:
                            after[chan, pl.ds(base, 8), pl.ds(0, part)] = whole
                        after[chan, pl.ds(base, 8), pl.ds(part, lanes)] = side
                    if inner:
                        to = pl.ds(pl.multiple_of(out_start + 8 * i - halo_rows, 8), 8)
                        detail = window[8:16, :part] - whole
                        detail_ref[chan, level, to, :] = detail
                        if level == 2:
                            detail_ref[chan, 3, to, :] = whole
                        energy = energy + detail * detail
                return jnp.maximum(peak, energy) if inner else peak

            step = functools.partial(step, level=level, gap=gap, before=before, after=after)
            for i in range(level, skirt):
                step(i, None)
                step(blocks - 1 - i, None)
            peaks[level] = lax.fori_loop(skirt, blocks - skirt, step, peaks[level], unroll=unroll)
    for level in range(3):
        most = peaks[level][:, :lanes]
        for t in range(1, tiles):
            most = jnp.maximum(most, peaks[level][:, t * lanes : (t + 1) * lanes])
        peak_ref[level] = most


def shrink_body(chans, detail_ref, peak_ref, *out_refs):
    factors = []
    for level in range(3):
        energy = 0.0
        for chan in range(chans):
            detail = detail_ref[chan, level]
            energy = energy + detail * detail
        energy = jnp.sqrt(energy)
        threshold = fractions[level] * jnp.sqrt(jnp.max(peak_ref[level], keepdims=True))
        threshold = jnp.broadcast_to(threshold, energy.shape)
        factors.append(1.0 - threshold / jnp.maximum(energy, threshold))
    for chan in range(chans):
        total = detail_ref[chan, 3]
        for level in range(3):
            total = total + factors[level] * detail_ref[chan, level]
        out_refs[chan][...] = total


def join_body(me_ref, *refs):
    chans = (len(refs) - 1) // 2
    out_ref = refs[-1]
    part = refs[0].shape[1]
    outer_rows, inner_rows = refs[0].shape[0] // 2, refs[chans].shape[0]
    for chan in range(chans):
        outer, inner = refs[chan], refs[chans + chan]
        columns = pl.ds(pl.multiple_of((me_ref[0] ^ chan) * part, part), part)
        out_ref[pl.ds(0, outer_rows), columns] = outer[pl.ds(0, outer_rows), :]
        out_ref[pl.ds(outer_rows, inner_rows), columns] = inner[...]
        out_ref[pl.ds(outer_rows + inner_rows, outer_rows), columns] = outer[
            pl.ds(outer_rows, outer_rows), :
        ]


def column_body(
    steps, in_ref, there_ref, back_ref, weight_ref, mirror_ref, flip_ref, edge_ref, core_ref, held, made
):
    count, _, height, lanes = in_ref.shape
    each = height // steps
    size = each * count
    for step in range(steps):
        rows = pl.ds(step * each, each)
        block = jnp.concatenate(
            [in_ref[source, part, rows, :] for part in range(2) for source in range(count)],
            axis=0,
        )
        high, low = split(block)
        done = (
            dot(there_ref[step, 0], high)
            + dot(there_ref[step, 1], high)
            + dot(there_ref[step, 0], low)
        )
        held[0, step] = done[:size]
        held[1, step] = done[size:]

    def forward(chunk, carry):
        rows = pl.ds(pl.multiple_of(chunk * 8, 8), 8)
        pairs = [(held[0, step, rows, :], held[1, step, rows, :]) for step in range(steps)]
        for step, pair in enumerate(complex_dft(pairs, -1.0)):
            held[0, step, rows, :] = pair[0]
            held[1, step, rows, :] = pair[1]
        return carry

    lax.fori_loop(0, size // 8, forward, 0)
    for step in range(steps):
        facing = [
            jnp.concatenate([held[0, other], held[1, other]], axis=1)
            for other in (steps - 1 - step, (steps - step) % steps)
        ]
        high, low = split(jnp.concatenate(facing, axis=0))
        turned = dot(flip_ref[...], high) + dot(flip_ref[...], low)
        weight = weight_ref[step]
        mirror = mirror_ref[step]
        made[0, step] = weight * held[0, step] + mirror * turned[:, :lanes]
        made[1, step] = weight * held[1, step] - mirror * turned[:, lanes:]

    def backward(chunk, carry):
        rows = pl.ds(pl.multiple_of(chunk * 8, 8), 8)
        pairs = [(made[0, step, rows, :], made[1, step, rows, :]) for step in range(steps)]
        for step, pair in enumerate(complex_dft(pairs, 1.0)):
            made[0, step, rows, :] = pair[0]
            made[1, step, rows, :] = pair[1]
        return carry

    lax.fori_loop(0, size // 8, backward, 0)
    for step in range(steps):
        high, low = split(jnp.concatenate([made[0, step], made[1, step]], axis=0))
        done = (
            dot(back_ref[step, 0], high)
            + dot(back_ref[step, 1], high)
            + dot(back_ref[step, 0], low)
        )
        half = each // 2
        rows = pl.ds(step * half, half)
        for part in range(2):
            for target in range(count):
                start = part * size + target * each
                edge_ref[target, part, rows, :] = done[start : start + half]
                core_ref[target, part, rows, :] = done[start + half : start + each]


def weight_pick_body(w_ref, pick_ref, out_ref):
    count, _, lanes = out_ref.shape
    packs, _, width = w_ref.shape
    total = 0.0
    for pack in range(packs):
        high, low = split(w_ref[pack])
        chosen = pick_ref[pl.ds(pack * width, width), :]
        total = total + dot(high, chosen) + dot(low, chosen)
    for target in range(count):
        out_ref[target] = total[:, target * lanes : (target + 1) * lanes]


def weight_place_body(in_ref, place_ref, flip_ref, weight_ref, mirror_ref, held):
    count, depth, lanes = in_ref.shape
    steps, size, _ = weight_ref.shape
    packs = steps * size // depth
    total = 0.0
    for source in range(count):
        high, low = split(in_ref[source])
        chosen = place_ref[pl.ds(source * lanes, lanes), :]
        total = total + dot(high, chosen) + dot(low, chosen)
    inner = depth // size
    extra = total[:, 2 * packs * lanes :]
    first = lax.broadcasted_iota(jnp.int32, (size, lanes), 1) == 0
    for step in range(steps):
        pack, rest = divmod(step, inner)
        rows = slice(rest * size, (rest + 1) * size)
        lone = extra[rows]
        if pack:
            lone = pltpu.roll(lone, lanes - pack, 1)
        lone = jnp.where(first, lone, 0.0)
        mirror_ref[step] = lone
        weight_ref[step] = total[rows, 2 * pack * lanes : (2 * pack + 1) * lanes]
        held[step] = jnp.concatenate(
            [total[rows, (2 * pack + 1) * lanes : (2 * pack + 2) * lanes], lone], axis=1
        )
    for step in range(steps):
        high, low = split(
            jnp.concatenate([held[steps - 1 - step], held[(steps - step) % steps]], axis=0)
        )
        turned = dot(flip_ref[...], high) + dot(flip_ref[...], low)
        weight_ref[step] += turned[:, :lanes]
        mirror_ref[step] += turned[:, lanes:]


def filtered(values, dirty, weights):
    height, length = values.shape
    count = lax.axis_size("rows")
    lanes = length // (2 * count)
    steps = height // 16
    size = length // steps
    width = weights.shape[1]
    f32 = jnp.float32
    pick, place, flip = [jnp.asarray(table) for table in weight_tables(length, count)]
    there, back = [jnp.asarray(table) for table in row_tables(length, count)]
    down, up = [jnp.asarray(table) for table in column_tables(length, count, steps)]
    shape = lambda *dims: jax.ShapeDtypeStruct(dims, f32)
    packs = length * width // (count * lanes) // (length // count)
    packs = pick.shape[0] // width
    depth = length // packs

    sent = whole_call(weight_pick_body, shape(count, depth, lanes), [], "weight_pick", 6)(
        weights.reshape(packs, depth, width), pick
    )
    sent = lax.all_to_all(sent, "rows", 0, 0, tiled=True)
    ahead = whole_call(
        functools.partial(row_forward_body, steps),
        shape(count, 2, height, lanes),
        [pltpu.VMEM((2, count, height, 2 * lanes), jnp.bfloat16)],
        "row_forward",
        6,
    )(values, there)
    ahead = lax.all_to_all(ahead, "rows", 0, 0, tiled=True)
    mine = jnp.where(lax.axis_index("rows") == 0, place[0], place[1])
    weight, mirror = whole_call(
        weight_place_body,
        [shape(steps, size, lanes)] * 2,
        [pltpu.VMEM((steps, size, 2 * lanes), f32)],
        "weight_place",
        10,
    )(sent, mine, flip)
    half = height // 2
    edge, core = whole_call(
        functools.partial(column_body, steps),
        [shape(count, 2, half, lanes)] * 2,
        [pltpu.VMEM((2, steps, size, lanes), f32)] * 2,
        "column_filter",
        12,
    )(ahead, down, up, weight, mirror, flip)
    edge = lax.all_to_all(edge, "rows", 0, 0, tiled=True)
    core = lax.all_to_all(core, "rows", 0, 0, tiled=True)
    chans = lax.axis_size("chan")
    part = length // chans
    quarter = height // 4

    def row_inverse(cells, old, blocks):
        rows_spec = pl.BlockSpec((quarter, length), lambda i: (blocks[0] + i * blocks[1], 0))
        whole = lambda *dims: pl.BlockSpec(dims, lambda i: (0,) * len(dims))
        return pl.pallas_call(
            functools.partial(row_inverse_body, steps),
            grid=(2,),
            in_specs=[
                whole(*cells.shape),
                whole(*back.shape),
                rows_spec,
                rows_spec,
                pl.BlockSpec(memory_space=pl.ANY),
            ],
            out_specs=[rows_spec, whole(chans, half + 8, part)],
            out_shape=[shape(height, length), shape(chans, half + 8, part)],
            scratch_shapes=[pltpu.VMEM((count, half, 2 * lanes), f32)],
            input_output_aliases={4: 0} if old is not dirty else {},
            compiler_params=pltpu.CompilerParams(vmem_limit_bytes=vmem_bytes),
            name="row_inverse",
        cost_estimate=busy(5),
        )(cells, back, values, dirty, old)

    def pieces_for(cells):
        me = lax.axis_index("chan")
        return [
            lax.dynamic_index_in_dim(cells, me ^ turn, 0, keepdims=False) for turn in range(chans)
        ]

    def over_chans(pieces):
        return [pieces[0]] + [
            lax.ppermute(pieces[turn], "chan", [(i, i ^ turn) for i in range(chans)])
            for turn in range(1, chans)
        ]

    def in_order(earlier, later):
        both = lax.optimization_barrier((*earlier, *later))
        return list(both[: len(earlier)]), list(both[len(earlier) :])

    residual, outer = row_inverse(edge, dirty, (0, 3))
    outer = over_chans(pieces_for(outer))
    residual, inner = row_inverse(core, residual, (1, 1))
    outer, inner = in_order(outer, pieces_for(inner))
    inner = over_chans(inner)
    ahead_pairs = [(i, i + 1) for i in range(count - 1)]
    back_pairs = [(i + 1, i) for i in range(count - 1)]
    last = jnp.stack([cells[half - halo_rows :] for cells in outer])
    first = jnp.stack(
        [jnp.concatenate([cells[:halo_rows], cells[half:]], axis=0) for cells in outer]
    )
    last = lax.ppermute(last, "rows", ahead_pairs)
    first = lax.ppermute(first, "rows", back_pairs)
    above = [last[c] for c in range(chans)]
    below = [first[c] for c in range(chans)]
    chan_id, row_id = lax.axis_index("chan"), lax.axis_index("rows")
    at_end = jnp.stack(
        [chan_id == 0, chan_id == chans - 1, row_id == 0, row_id == count - 1]
    ).astype(jnp.int32)
    vmem = pl.BlockSpec(memory_space=pltpu.VMEM)

    def starlet(sources, rows, spans, fills, microseconds):
        extent = max(fill[0] + fill[3] for fill in fills) + 16
        cells = pltpu.VMEM((chans, extent, part + lanes), f32)
        return pl.pallas_call(
            functools.partial(starlet_body, chans, spans, fills),
            in_specs=[pl.BlockSpec(memory_space=pltpu.SMEM)] + [vmem] * len(sources),
            out_specs=[vmem] * 2,
            out_shape=[shape(chans, 4, rows, part), shape(3, 8, lanes)],
            scratch_shapes=[cells, cells],
            compiler_params=pltpu.CompilerParams(vmem_limit_bytes=vmem_bytes),
            name="starlet",
            cost_estimate=busy(microseconds),
        )(at_end, *sources)

    reach = quarter + halo_rows
    most = quarter - halo_rows
    skirt = halo_rows // 8
    outer_details, outer_peaks = starlet(
        outer + above + below,
        2 * most,
        (
            (0, reach // 8, 0, True, False),
            (reach + 16, reach // 8, most, False, True),
        ),
        (
            (0, 1, 0, halo_rows, halo_rows, (half - halo_rows) // 8),
            (halo_rows, 0, 0, quarter, half, 0),
            (reach + 16, 0, quarter, quarter, half, quarter // 8),
            (reach + 16 + quarter, 2, 0, halo_rows, halo_rows, 0),
        ),
        12,
    )
    inner_details, inner_peaks = starlet(
        outer + inner,
        half + 2 * halo_rows,
        ((0, half // 8 + 4 * skirt, 0, False, False),),
        (
            (0, 0, quarter - 2 * halo_rows, 2 * halo_rows, half, (quarter - 2 * halo_rows) // 8),
            (2 * halo_rows, 1, 0, half, half, 0),
            (2 * halo_rows + half, 0, quarter, 2 * halo_rows, half, quarter // 8),
        ),
        12,
    )
    peaks = jnp.maximum(outer_peaks, inner_peaks)
    peaks = max_over(peaks, "rows", range(1, 2))
    peaks = max_over(peaks, "rows", range(2, count, 2))
    peaks = max_over(peaks, "chan", range(1, chans))

    def shrink(details):
        rows = details.shape[2]
        thick = rows // 2
        return pl.pallas_call(
            functools.partial(shrink_body, chans),
            grid=(2,),
            in_specs=[
                pl.BlockSpec((chans, 4, thick, part), lambda i: (0, 0, i, 0)),
                pl.BlockSpec((3, 8, lanes), lambda i: (0, 0, 0)),
            ],
            out_specs=[pl.BlockSpec((thick, part), lambda i: (i, 0))] * chans,
            out_shape=[shape(rows, part)] * chans,
            compiler_params=pltpu.CompilerParams(vmem_limit_bytes=vmem_bytes),
            name="shrink",
            cost_estimate=busy(3),
        )(details, peaks)

    outer = over_chans(shrink(outer_details))
    outer, inner = in_order(outer, shrink(inner_details))
    inner = over_chans(inner)
    new_estimate = pl.pallas_call(
        join_body,
        in_specs=[pl.BlockSpec(memory_space=pltpu.SMEM)] + [vmem] * (2 * chans),
        out_specs=vmem,
        out_shape=shape(height, length),
        compiler_params=pltpu.CompilerParams(vmem_limit_bytes=vmem_bytes),
        name="join",
        cost_estimate=busy(4),
    )(jnp.reshape(chan_id, (1,)).astype(jnp.int32), *outer, *inner)
    return new_estimate, residual


def filtered_plain(values, dirty, weights):
    height, length = values.shape
    row_count = lax.axis_size("rows")
    narrow = length // row_count
    spec_real, spec_imag = dft_last(values, jnp.zeros_like(values), -1.0)
    spec_real = spec_real.reshape(height, row_count, narrow)
    spec_imag = spec_imag.reshape(height, row_count, narrow)
    col_real, col_imag = columns_forward(
        (
            lax.all_to_all(spec_real, "rows", split_axis=1, concat_axis=0, tiled=True),
            lax.all_to_all(spec_imag, "rows", split_axis=1, concat_axis=0, tiled=True),
        )
    )
    prod_real = weights * col_real[:, 0, :]
    prod_imag = weights * col_imag[:, 0, :]
    back_real, back_imag = dft_first(prod_real, prod_imag, 1.0)
    back_real = back_real.reshape(row_count, height, narrow)
    back_imag = back_imag.reshape(row_count, height, narrow)
    blurred = rows_inverse(
        (
            lax.all_to_all(back_real, "rows", split_axis=0, concat_axis=2, tiled=True),
            lax.all_to_all(back_imag, "rows", split_axis=0, concat_axis=2, tiled=True),
        )
    )[0]
    residual = dirty - blurred
    return residual, values + step_size * residual


def joined_plain(halfway):
    height, length = halfway.shape
    depth = 14
    chan_count = lax.axis_size("chan")
    part = length // chan_count
    padded = with_halo(halfway, (("rows", 0),), depth)
    padded = jnp.pad(padded, ((0, 0), (depth, depth)))
    pieces = jnp.stack(
        [padded[:, q * part : (q + 1) * part + 2 * depth] for q in range(chan_count)]
    )
    current = lax.all_to_all(pieces, "chan", split_axis=0, concat_axis=0, tiled=True)
    row_ids = lax.axis_index("rows") * height - depth + lax.iota(jnp.int32, height + 2 * depth)
    col_ids = lax.axis_index("chan") * part - depth + lax.iota(jnp.int32, part + 2 * depth)
    margin = depth
    details = []
    for scale_level in range(3):
        reach = 2 << scale_level
        smoother = smooth_both(current, 1 << scale_level)
        row_ids = row_ids[reach:-reach]
        col_ids = col_ids[reach:-reach]
        inside = ((row_ids >= 0) & (row_ids < length))[:, None] & (
            (col_ids >= 0) & (col_ids < length)
        )[None, :]
        smoother = jnp.where(inside[None], smoother, 0.0)
        new_margin = margin - reach
        details.append(
            current[:, margin : margin + height, margin : margin + part]
            - smoother[:, new_margin : new_margin + height, new_margin : new_margin + part]
        )
        current = smoother
        margin = new_margin
    energies = [jnp.sum(detail * detail, axis=0) for detail in details]
    peaks = jnp.stack([jnp.broadcast_to(jnp.max(energy), (128,)) for energy in energies])
    for axis in ("rows", "chan"):
        peaks = lax.pmax(peaks, axis)
    output = current
    for scale_level in range(3):
        threshold = fractions[scale_level] * jnp.sqrt(peaks[scale_level, 0])
        factor = 1.0 - threshold / jnp.maximum(jnp.sqrt(energies[scale_level]), threshold)
        output = output + factor[None] * details[scale_level]
    output = lax.all_to_all(output, "chan", split_axis=0, concat_axis=2, tiled=True)[0]
    return output


def shards(estimate, dirty_image, psf_weights):
    values, dirty, weights = estimate[0], dirty_image[0], psf_weights[0]
    height, length = values.shape
    row_count, chan_count = lax.axis_size("rows"), lax.axis_size("chan")
    whole_tiles = length == 2 * row_count * lane_count and length % (chan_count * lane_count) == 0
    if whole_tiles and chan_count & (chan_count - 1) == 0:
        new_estimate, residual = filtered(values, dirty, weights)
    else:
        residual, halfway = filtered_plain(values, dirty, weights)
        new_estimate = joined_plain(halfway)
    return (new_estimate[None], residual[None])


def solution(mesh):
    return jax.shard_map(
        shards,
        mesh=mesh,
        in_specs=(P("chan", "rows", None), P("chan", "rows", None), P("chan", None, "rows")),
        out_specs=(P("chan", "rows", None), P("chan", "rows", None)),
        check_vma=False,
    )
```

```python
import functools
import math

import jax
import jax.numpy as jnp
import ml_dtypes
import numpy as np
from jax import lax
from jax.experimental import pallas as pl
from jax.experimental.pallas import tpu as pltpu
from jax.sharding import PartitionSpec as P

fractions = (0.03, 0.02, 0.015)
taps = (0.0625, 0.25, 0.375, 0.25, 0.0625)
step_size = 0.9
inner_length = 128
highest = lax.Precision.HIGHEST
lane_count = 128
vmem_bytes = 56 * 1024 * 1024
rim = 16
halo_rows = 16
unroll = 2


def with_halo(cells, sides, width):
    for axis, dim in sides:
        count = lax.axis_size(axis)
        ends = count - 1
        head = lax.slice_in_dim(cells, 0, width, axis=dim)
        tail = lax.slice_in_dim(cells, cells.shape[dim] - width, cells.shape[dim], axis=dim)
        cells = jnp.concatenate(
            [
                lax.ppermute(tail, axis, [(i, (i + 1) % count) for i in range(ends)]),
                cells,
                lax.ppermute(head, axis, [((i + 1) % count, i) for i in range(ends)]),
            ],
            axis=dim,
        )
    return cells


def phase_table(first_count, second_count, length, sign):
    first_ids = lax.iota(jnp.int32, first_count)
    second_ids = lax.iota(jnp.int32, second_count)
    angles = (first_ids[:, None] * second_ids[None, :] % length).astype(jnp.float32) * (
        2.0 * math.pi / length
    )
    return (jnp.cos(angles), sign * jnp.sin(angles))


def dft_last(real_in, imag_in, sign):
    batch, length = real_in.shape
    outer = length // inner_length
    real_part = real_in.reshape(batch, outer, inner_length)
    imag_part = imag_in.reshape(batch, outer, inner_length)
    cos_small, sin_small = phase_table(outer, outer, outer, sign)
    first_real = jnp.einsum("kn,bnm->bkm", cos_small, real_part, precision=highest) - jnp.einsum(
        "kn,bnm->bkm", sin_small, imag_part, precision=highest
    )
    first_imag = jnp.einsum("kn,bnm->bkm", cos_small, imag_part, precision=highest) + jnp.einsum(
        "kn,bnm->bkm", sin_small, real_part, precision=highest
    )
    cos_twist, sin_twist = phase_table(outer, inner_length, length, sign)
    twist_real = first_real * cos_twist - first_imag * sin_twist
    twist_imag = first_imag * cos_twist + first_real * sin_twist
    cos_large, sin_large = phase_table(inner_length, inner_length, inner_length, sign)
    last_real = jnp.einsum("bkm,mj->bkj", twist_real, cos_large, precision=highest) - jnp.einsum(
        "bkm,mj->bkj", twist_imag, sin_large, precision=highest
    )
    last_imag = jnp.einsum("bkm,mj->bkj", twist_imag, cos_large, precision=highest) + jnp.einsum(
        "bkm,mj->bkj", twist_real, sin_large, precision=highest
    )
    return (
        jnp.transpose(last_real, (0, 2, 1)).reshape(batch, length),
        jnp.transpose(last_imag, (0, 2, 1)).reshape(batch, length),
    )


def dft_first(real_in, imag_in, sign):
    length, width = real_in.shape
    outer = length // inner_length
    real_part = real_in.reshape(outer, inner_length, width)
    imag_part = imag_in.reshape(outer, inner_length, width)
    cos_small, sin_small = phase_table(outer, outer, outer, sign)
    first_real = jnp.einsum("kn,nmw->kmw", cos_small, real_part, precision=highest) - jnp.einsum(
        "kn,nmw->kmw", sin_small, imag_part, precision=highest
    )
    first_imag = jnp.einsum("kn,nmw->kmw", cos_small, imag_part, precision=highest) + jnp.einsum(
        "kn,nmw->kmw", sin_small, real_part, precision=highest
    )
    cos_twist, sin_twist = phase_table(outer, inner_length, length, sign)
    cos_twist = cos_twist[:, :, None]
    sin_twist = sin_twist[:, :, None]
    twist_real = first_real * cos_twist - first_imag * sin_twist
    twist_imag = first_imag * cos_twist + first_real * sin_twist
    cos_large, sin_large = phase_table(inner_length, inner_length, inner_length, sign)
    last_real = jnp.einsum("kmw,mj->kjw", twist_real, cos_large, precision=highest) - jnp.einsum(
        "kmw,mj->kjw", twist_imag, sin_large, precision=highest
    )
    last_imag = jnp.einsum("kmw,mj->kjw", twist_imag, cos_large, precision=highest) + jnp.einsum(
        "kmw,mj->kjw", twist_real, sin_large, precision=highest
    )
    return (
        jnp.transpose(last_real, (1, 0, 2)).reshape(length, width),
        jnp.transpose(last_imag, (1, 0, 2)).reshape(length, width),
    )


def columns_forward(pieces):
    real_out, imag_out = dft_first(pieces[0][:, 0, :], pieces[1][:, 0, :], -1.0)
    return (real_out[:, None, :], imag_out[:, None, :])


def rows_inverse(pieces):
    real_in = pieces[0][0]
    imag_in = pieces[1][0]
    length = real_in.shape[1]
    real_out, imag_out = dft_last(real_in, imag_in, 1.0)
    return (real_out * (1.0 / (length * length)))[None]


def max_over(cells, axis, distances):
    count = lax.axis_size(axis)
    others = [
        lax.ppermute(cells, axis, [(i, i ^ distance) for i in range(count)])
        for distance in distances
    ]
    for other in others:
        cells = jnp.maximum(cells, other)
    return cells


def smooth_both(values, spacing):
    for dim in (2, 1):
        count = values.shape[dim] - 4 * spacing
        total = taps[0] * lax.slice_in_dim(values, 0, count, axis=dim)
        for tap_index in range(1, 5):
            start = tap_index * spacing
            total = total + taps[tap_index] * lax.slice_in_dim(
                values, start, start + count, axis=dim
            )
        values = total
    return values


def real_dft(parts):
    count = len(parts)
    if count == 1:
        return [(parts[0], None)]
    if count == 2:
        return [(parts[0] + parts[1], None), (parts[0] - parts[1], None)]
    even = real_dft(parts[0::2])
    odd = real_dft(parts[1::2])
    out = [None] * (count // 2 + 1)
    for k in range(count // 4 + 1):
        turned = spin(odd[k], -2.0 * math.pi * k / count)
        out[k] = pair_add(even[k], turned)
        low = pair_sub(even[k], turned)
        out[count // 2 - k] = (low[0], None if low[1] is None else -low[1])
    out[0] = (out[0][0], None)
    out[count // 2] = (out[count // 2][0], None)
    return out


def real_inverse_dft(pairs):
    count = 2 * (len(pairs) - 1)
    if count == 2:
        return [pairs[0][0] + pairs[1][0], pairs[0][0] - pairs[1][0]]
    even, odd = [], []
    for k in range(count // 4 + 1):
        low = pairs[k]
        high = pairs[count // 2 - k]
        high = (high[0], None if high[1] is None else -high[1])
        even.append(pair_add(low, high))
        odd.append(spin(pair_sub(low, high), 2.0 * math.pi * k / count))
    for half in (even, odd):
        half[0] = (half[0][0], None)
        half[-1] = (half[-1][0], None)
    even = real_inverse_dft(even)
    odd = real_inverse_dft(odd)
    return [cells for both in zip(even, odd) for cells in both]


def complex_dft(pairs, sign):
    count = len(pairs)
    if count == 1:
        return pairs
    even = complex_dft(pairs[0::2], sign)
    odd = complex_dft(pairs[1::2], sign)
    turned = [spin(odd[k], sign * 2.0 * math.pi * k / count) for k in range(count // 2)]
    return [pair_add(a, b) for a, b in zip(even, turned)] + [
        pair_sub(a, b) for a, b in zip(even, turned)
    ]


def pair_add(a, b):
    if a[1] is None or b[1] is None:
        return (a[0] + b[0], a[1] if b[1] is None else b[1])
    return (a[0] + b[0], a[1] + b[1])


def pair_sub(a, b):
    if b[1] is None:
        return (a[0] - b[0], a[1])
    return (a[0] - b[0], -b[1] if a[1] is None else a[1] - b[1])


def spin(pair, angle):
    quarter = angle / (0.5 * math.pi)
    turns = round(quarter)
    real, imag = pair
    if abs(quarter - turns) < 1e-9:
        turns %= 4
        if turns == 0:
            return pair
        if turns == 2:
            return (-real, None if imag is None else -imag)
        if imag is None:
            return (jnp.zeros_like(real), real if turns == 1 else -real)
        return (-imag, real) if turns == 1 else (imag, -real)
    cosine, sine = math.cos(angle), math.sin(angle)
    if imag is None:
        return (real * cosine, real * sine)
    if abs(abs(cosine) - abs(sine)) < 1e-9:
        a, b = math.copysign(1.0, cosine), math.copysign(1.0, sine)
        root = abs(cosine)
        first = real if a > 0 else -real
        second = imag if b > 0 else -imag
        third = real if b > 0 else -real
        fourth = imag if a > 0 else -imag
        return ((first - second) * root, (third + fourth) * root)
    return (real * cosine - imag * sine, real * sine + imag * cosine)


def split(cells):
    high = cells.astype(jnp.bfloat16)
    return high, (cells - high.astype(jnp.float32)).astype(jnp.bfloat16)


def dot(a, b):
    return jnp.dot(a, b, preferred_element_type=jnp.float32)


def split_table(table):
    high = table.astype(np.float32).astype(ml_dtypes.bfloat16)
    low = (table - high.astype(np.float64)).astype(np.float32).astype(ml_dtypes.bfloat16)
    return np.stack([high, low], axis=-3)


def group_columns(length, count, group):
    radix = 2 * count
    lanes = length // radix
    spots = np.arange(lanes)
    if group:
        return group + radix * spots
    half = lanes // 2
    return np.where(spots < half, radix * spots, count + radix * (spots - half))


def row_tables(length, count):
    radix = 2 * count
    lanes = length // radix
    half = lanes // 2
    spots = np.arange(lanes)
    there, back = [], []
    for group in range(count):
        columns = group_columns(length, count, group)
        angles = 2.0 * np.pi * (np.outer(spots, columns) % length) / length
        cosine, sine = np.cos(angles), np.sin(angles)
        ahead = np.zeros((2, lanes, 2, lanes))
        behind = np.zeros((2, lanes, 2, lanes))
        if group:
            ahead[0, :, 0], ahead[0, :, 1] = cosine, -sine
            ahead[1, :, 0], ahead[1, :, 1] = sine, cosine
            behind[0, :, 0], behind[0, :, 1] = cosine.T, sine.T
            behind[1, :, 0], behind[1, :, 1] = -sine.T, cosine.T
        else:
            for part, where in enumerate((slice(0, half), slice(half, lanes))):
                ahead[part, :, 0, where] = cosine[:, where]
                ahead[part, :, 1, where] = -sine[:, where]
                behind[0, where, part] = 2.0 * cosine[:, where].T
                behind[1, where, part] = -2.0 * sine[:, where].T
            ahead[0, :, 1, 0] = (-1.0) ** spots
            behind[0, 0, 0] = 1.0
            behind[1, 0, 0] = (-1.0) ** spots
        there.append(ahead.reshape(2 * lanes, 2 * lanes))
        back.append(behind.reshape(2 * lanes, 2 * lanes) / float(length) ** 2)
    return split_table(np.stack(there)), split_table(np.stack(back))


def column_tables(length, count, steps):
    size = length // steps
    each = size // count
    quarter = each // 4
    order = np.r_[0:quarter, each - quarter : each, quarter : each - quarter]
    order = (np.arange(count)[:, None] * each + order[None]).reshape(-1)
    order = np.concatenate([order, size + order])
    spots = np.arange(size)
    angles = 2.0 * np.pi * (np.outer(spots, spots) % size) / size
    cosine, sine = np.cos(angles), np.sin(angles)
    there = np.block([[cosine, sine], [-sine, cosine]])
    turns = np.zeros((2, size, lane_count), np.float32)
    angles = 2.0 * np.pi * np.outer(spots, np.arange(steps)) / length
    turns[0, :, :steps], turns[1, :, :steps] = np.cos(angles), np.sin(angles)
    return split_table(there), split_table(there.T[order]), turns


def weight_tables(length, count, steps):
    width = length // count
    lanes = length // (2 * count)
    per_class = width // (2 * count)
    packs = lanes // (2 * per_class)
    radix = 2 * count

    def classes(group):
        return (group, radix - group) if group else (0, count)

    pick = np.zeros((width, count, 2, per_class))
    for group in range(count):
        for which, kind in enumerate(classes(group)):
            for q in range(per_class):
                pick[radix * q + kind, group, which, q] = 1.0
    place = np.zeros((2, count, lanes, packs * 2 + 1, lanes))

    def slot(group, column, pack):
        column %= length
        source, rest = divmod(column, width)
        which = classes(group).index(rest % radix)
        return source, pack * 2 * per_class + which * per_class + rest // radix

    for version, group in ((0, 0), (1, 1)):
        columns = group_columns(length, count, group)
        for pack in range(packs):
            for lane in range(lanes):
                column = int(columns[lane])
                mates = [(column, 0, 0.5), (-column, 1, 0.5)]
                if group == 0 and lane == 0:
                    mates = [(c, s, 0.25) for c in (0, length // 2) for s in (0, 1)]
                for mate, side, value in mates:
                    source, where = slot(group, mate, pack)
                    place[version, source, where, pack * 2 + side, lane] += value
            if group == 0:
                for mate, value in ((0, 0.25), (length // 2, -0.25)):
                    source, where = slot(group, mate, pack)
                    place[version, source, where, packs * 2, pack] += value
    flip = np.zeros((length // steps, length // steps))
    flip[np.arange(len(flip)), -np.arange(len(flip))] = 1.0
    as_half = lambda table: table.astype(np.float32).astype(ml_dtypes.bfloat16)
    return (
        as_half(pick.reshape(width, width)),
        as_half(place.reshape(2, count * lanes, (packs * 2 + 1) * lanes)),
        as_half(flip),
    )


def busy(microseconds):
    return pl.CostEstimate(
        flops=0, bytes_accessed=int(microseconds * 3.5e6), transcendentals=0
    )


def whole_call(body, out_shapes, scratch, name, microseconds):
    return pl.pallas_call(
        body,
        out_shape=out_shapes,
        scratch_shapes=scratch,
        compiler_params=pltpu.CompilerParams(vmem_limit_bytes=vmem_bytes),
        name=name,
        cost_estimate=busy(microseconds),
    )


def row_forward_body(steps, me_ref, x_ref, table_ref, *refs):
    out_refs, held = refs[:-1], refs[-1]
    groups = len(out_refs)
    _, height, lanes = out_refs[0].shape
    each = height // steps
    for start in range(0, height, 16):
        rows = pl.ds(start, 16)
        tiles = [x_ref[rows, pl.ds(lanes * t, lanes)] for t in range(2 * groups)]
        pairs = real_dft(tiles)
        pairs = [(pairs[0][0], pairs[groups][0])] + pairs[1:groups]
        for group in range(groups):
            high, low = split(jnp.concatenate(pairs[group], axis=1))
            held[0, group, rows, :] = high
            held[1, group, rows, :] = low
    for turn, out_ref in enumerate(out_refs):
        group = me_ref[0] ^ turn
        done = (
            dot(held[0, group], table_ref[group, 0])
            + dot(held[1, group], table_ref[group, 0])
            + dot(held[0, group], table_ref[group, 1])
        )
        for start in range(0, height, 8):
            spread = pl.ds(start % steps * each + start // steps, 8, stride=each)
            out_ref[0, spread, :] = done[start : start + 8, :lanes]
            out_ref[1, spread, :] = done[start : start + 8, lanes:]


def row_inverse_body(
    steps, in_ref, table_ref, est_ref, dirty_ref, old_ref, res_ref, half_ref, held
):
    del old_ref
    groups, _, chunk, lanes = in_ref.shape
    parts, _, wide = half_ref.shape
    each = chunk // steps
    block = est_ref.shape[0]
    turn = pl.program_id(0)

    @pl.when(turn == 0)
    def _():
        for group in range(groups):
            halves = []
            for part in range(2):
                pieces = [
                    in_ref[
                        group,
                        part,
                        pl.ds(start % steps * each + start // steps, 8, stride=each),
                        :,
                    ]
                    for start in range(0, chunk, 8)
                ]
                halves.append(jnp.concatenate(pieces, axis=0))
            high, low = split(jnp.concatenate(halves, axis=1))
            held[group] = (
                dot(high, table_ref[group, 0])
                + dot(low, table_ref[group, 0])
                + dot(high, table_ref[group, 1])
            )

    per = wide // lanes
    lane_ids = lax.broadcasted_iota(jnp.int32, (8, lanes), 1)
    sides = [None] * parts
    for start in range(0, block, 8):
        rows = pl.ds(start, 8)
        chunk_rows = pl.ds(pl.multiple_of(turn * block + start, 8), 8)
        pairs = [
            (held[group, chunk_rows, pl.ds(0, lanes)], held[group, chunk_rows, pl.ds(lanes, lanes)])
            for group in range(groups)
        ]
        pairs = [(pairs[0][0], None)] + pairs[1:] + [(pairs[0][1], None)]
        tiles = real_inverse_dft(pairs)
        for t in range(2 * groups):
            where = pl.ds(lanes * t, lanes)
            residual = dirty_ref[rows, where] - tiles[t]
            res_ref[rows, where] = residual
            tiles[t] = est_ref[rows, where] + step_size * residual
            half_ref[t // per, chunk_rows, pl.ds(lanes * (t % per), lanes)] = tiles[t]
        offset = start // 8 * 2 * rim % lanes
        for part in range(parts):
            done = jnp.zeros_like(tiles[0]) if offset == 0 else sides[part]
            if part > 0:
                turned = pltpu.roll(tiles[part * per - 1], (offset + rim) % lanes, 1)
                done = jnp.where((lane_ids >= offset) & (lane_ids < offset + rim), turned, done)
            if part < parts - 1:
                turned = pltpu.roll(tiles[(part + 1) * per], (offset + rim) % lanes, 1)
                done = jnp.where(
                    (lane_ids >= offset + rim) & (lane_ids < offset + 2 * rim), turned, done
                )
            sides[part] = done
            if offset + 2 * rim == lanes:
                spot = turn * (block // 8 * 2 * rim // lanes) + start // 8 * 2 * rim // lanes
                where = pl.ds(pl.multiple_of(spot * lanes, lanes), lanes)
                half_ref[part, pl.ds(chunk, 8), where] = done


def starlet_body(chans, spans, fills, ends_ref, *refs):
    sources, (detail_ref, peak_ref, ping, pong) = refs[:-4], refs[-4:]
    part = detail_ref.shape[3]
    lanes = lane_count
    tiles = part // lanes
    total = part + lanes
    no_left, no_right = ends_ref[0] > 0, ends_ref[1] > 0
    no_top, no_bottom = ends_ref[2] > 0, ends_ref[3] > 0
    lane_ids = lax.broadcasted_iota(jnp.int32, (8, lanes), 1)
    outside = ((lane_ids >= lanes // 2) & no_left) | ((lane_ids < lanes // 2) & no_right)
    for chan in range(chans):
        for target, index, source_row, count, pack_row, group in fills:
            source = sources[index * chans + chan]
            to = pl.ds(8 + target, count)
            ping[chan, to, pl.ds(0, part)] = source[pl.ds(source_row, count), :]
            for i in range(count // 8):
                spot = (group + i) * 2 * rim
                tile = source[pl.ds(pack_row, 8), pl.ds(spot // lanes * lanes, lanes)]
                shift = (lanes - spot % lanes - rim) % lanes
                to = pl.ds(8 + target + 8 * i, 8)
                ping[chan, to, pl.ds(part, lanes)] = pltpu.roll(tile, shift, 1)

    skirt = halo_rows // 8
    peaks = [jnp.zeros((8, part), jnp.float32)] * 3
    for start, blocks, out_start, top, bottom in spans:
        for level in range(3):
            gap = 1 << level
            before, after = (ping, pong) if level % 2 == 0 else (pong, ping)

            def step(i, peak, level, gap, before, after):
                base = 8 + start + 8 * i
                if not isinstance(i, int):
                    base = pl.multiple_of(base, 8)
                inner = not isinstance(i, int)
                energy = 0.0
                for chan in range(chans):
                    window = before[chan, pl.ds(base - 8, 24), :]
                    near = window[8 - gap : 16 - gap] + window[8 + gap : 16 + gap]
                    far = window[8 - 2 * gap : 16 - 2 * gap] + window[8 + 2 * gap : 16 + 2 * gap]
                    row = (far + 4.0 * near) + 6.0 * window[8:16]
                    near = pltpu.roll(row, gap, 1) + pltpu.roll(row, total - gap, 1)
                    far = pltpu.roll(row, 2 * gap, 1) + pltpu.roll(row, total - 2 * gap, 1)
                    smooth = ((far + 4.0 * near) + 6.0 * row) * (1.0 / 256.0)
                    whole = smooth[:, :part]
                    if level < 2:
                        side = jnp.where(outside, 0.0, smooth[:, part:])
                        if not inner and (top if i < skirt else bottom):
                            gone = no_top if i < skirt else no_bottom
                            side = jnp.where(gone, 0.0, side)
                            after[chan, pl.ds(base, 8), pl.ds(0, part)] = jnp.where(
                                gone, 0.0, whole
                            )
                        else:
                            after[chan, pl.ds(base, 8), pl.ds(0, part)] = whole
                        after[chan, pl.ds(base, 8), pl.ds(part, lanes)] = side
                    if inner:
                        to = pl.ds(pl.multiple_of(out_start + 8 * i - halo_rows, 8), 8)
                        detail = window[8:16, :part] - whole
                        detail_ref[chan, level, to, :] = detail
                        if level == 2:
                            detail_ref[chan, 3, to, :] = whole
                        energy = energy + detail * detail
                return jnp.maximum(peak, energy) if inner else peak

            step = functools.partial(step, level=level, gap=gap, before=before, after=after)
            for i in range(level, skirt):
                step(i, None)
                step(blocks - 1 - i, None)
            peaks[level] = lax.fori_loop(skirt, blocks - skirt, step, peaks[level], unroll=unroll)
    for level in range(3):
        most = peaks[level][:, :lanes]
        for t in range(1, tiles):
            most = jnp.maximum(most, peaks[level][:, t * lanes : (t + 1) * lanes])
        peak_ref[level] = most


def shrink_body(chans, detail_ref, peak_ref, *out_refs):
    factors = []
    for level in range(3):
        energy = 0.0
        for chan in range(chans):
            detail = detail_ref[chan, level]
            energy = energy + detail * detail
        energy = jnp.sqrt(energy)
        threshold = fractions[level] * jnp.sqrt(jnp.max(peak_ref[level], keepdims=True))
        threshold = jnp.broadcast_to(threshold, energy.shape)
        factors.append(1.0 - threshold / jnp.maximum(energy, threshold))
    for chan in range(chans):
        total = detail_ref[chan, 3]
        for level in range(3):
            total = total + factors[level] * detail_ref[chan, level]
        out_refs[chan][...] = total


def join_body(me_ref, *refs):
    chans = (len(refs) - 1) // 2
    out_ref = refs[-1]
    part = refs[0].shape[1]
    outer_rows, inner_rows = refs[0].shape[0] // 2, refs[chans].shape[0]
    for chan in range(chans):
        outer, inner = refs[chan], refs[chans + chan]
        columns = pl.ds(pl.multiple_of((me_ref[0] ^ chan) * part, part), part)
        out_ref[pl.ds(0, outer_rows), columns] = outer[pl.ds(0, outer_rows), :]
        out_ref[pl.ds(outer_rows, inner_rows), columns] = inner[...]
        out_ref[pl.ds(outer_rows + inner_rows, outer_rows), columns] = outer[
            pl.ds(outer_rows, outer_rows), :
        ]


def facing(blocks, step):
    rows = lax.broadcasted_iota(jnp.int32, blocks[0].shape, 0)
    return jnp.where(rows == 0, blocks[-step % len(blocks)], blocks[len(blocks) - 1 - step])


def column_body(steps, count, me_ref, *refs):
    in_refs = refs[:count]
    there_ref, back_ref, turn_ref, weight_ref, mirror_ref, flip_ref = refs[count : count + 6]
    edge_ref, core_ref, gathered, held, made = refs[count + 6 :]
    _, height, lanes = in_refs[0].shape
    each = height // steps
    size = each * count
    for turn, in_ref in enumerate(in_refs):
        source = me_ref[0] ^ turn
        for part in range(2):
            to = pl.ds(pl.multiple_of(part * size + source * each, 8), each)
            for step in range(steps):
                gathered[to, pl.ds(step * lanes, lanes)] = in_ref[part, pl.ds(step * each, each), :]
    for step in range(0, steps, 2):
        high, low = split(gathered[:, pl.ds(step * lanes, 2 * lanes)])
        done = dot(there_ref[0], high) + dot(there_ref[1], high) + dot(there_ref[0], low)
        for k in range(2):
            held[0, step + k] = done[:size, k * lanes : (k + 1) * lanes]
            held[1, step + k] = done[size:, k * lanes : (k + 1) * lanes]

    def turned(pairs, rows, sign):
        cosines, sines = turn_ref[0, rows, :], turn_ref[1, rows, :]
        out = [pairs[0]]
        for step in range(1, steps):
            real, imag = pairs[step]
            cosine = jnp.broadcast_to(cosines[:, step : step + 1], real.shape)
            sine = sign * jnp.broadcast_to(sines[:, step : step + 1], real.shape)
            out.append((real * cosine - imag * sine, imag * cosine + real * sine))
        return out

    def forward(chunk, carry):
        rows = pl.ds(pl.multiple_of(chunk * 8, 8), 8)
        pairs = [(held[0, step, rows, :], held[1, step, rows, :]) for step in range(steps)]
        for step, pair in enumerate(complex_dft(turned(pairs, rows, -1.0), -1.0)):
            held[0, step, rows, :] = pair[0]
            held[1, step, rows, :] = pair[1]
        return carry

    lax.fori_loop(0, size // 8, forward, 0)
    lane_ids = lax.broadcasted_iota(jnp.int32, (size, lanes), 1)
    lone = jnp.zeros((size, lanes), jnp.float32)
    for step in range(steps):
        for part in range(2):
            spot = 2 * step + part
            moved = facing([held[part, other] for other in range(steps)], step)
            if spot:
                moved = pltpu.roll(moved, spot, 1)
            lone = jnp.where(lane_ids == spot, moved, lone)
    high, low = split(lone)
    lone = (dot(flip_ref[...], high) + dot(flip_ref[...], low)) * mirror_ref[...]
    for step in range(steps):
        weight = weight_ref[step]
        for part in range(2):
            spot = 2 * step + part
            moved = pltpu.roll(lone, lanes - spot, 1) if spot else lone
            made[part, step] = weight * held[part, step] + jnp.where(lane_ids == 0, moved, 0.0)

    def backward(chunk, carry):
        rows = pl.ds(pl.multiple_of(chunk * 8, 8), 8)
        pairs = [(made[0, step, rows, :], made[1, step, rows, :]) for step in range(steps)]
        for step, pair in enumerate(turned(complex_dft(pairs, 1.0), rows, 1.0)):
            made[0, step, rows, :] = pair[0]
            made[1, step, rows, :] = pair[1]
        return carry

    lax.fori_loop(0, size // 8, backward, 0)
    half = each // 2
    for step in range(0, steps, 2):
        block = [
            jnp.concatenate([made[part, step + k] for k in range(2)], axis=1) for part in range(2)
        ]
        high, low = split(jnp.concatenate(block, axis=0))
        done = dot(back_ref[0], high) + dot(back_ref[1], high) + dot(back_ref[0], low)
        for k in range(2):
            rows = pl.ds((step + k) * half, half)
            columns = slice(k * lanes, (k + 1) * lanes)
            for part in range(2):
                for target in range(count):
                    start = part * size + target * each
                    edge_ref[target, part, rows, :] = done[start : start + half, columns]
                    core_ref[target, part, rows, :] = done[start + half : start + each, columns]


def weight_pick_body(w_ref, pick_ref, out_ref):
    count, thick, lanes = out_ref.shape
    packs, _, width = w_ref.shape
    piece = lanes // packs
    chosen = []
    for pack in range(packs):
        high, low = split(w_ref[pack])
        chosen.append(dot(high, pick_ref[...]) + dot(low, pick_ref[...]))
    lane_ids = lax.broadcasted_iota(jnp.int32, (thick, lanes), 1)
    for target in range(count):
        start = target * piece // lanes * lanes
        total = None
        for pack in range(packs):
            moved = chosen[pack][:, start : start + lanes]
            shift = (pack - target) % packs * piece
            if shift:
                moved = pltpu.roll(moved, shift, 1)
            total = moved if pack == 0 else jnp.where(lane_ids >= pack * piece, moved, total)
        out_ref[target] = total


def weight_place_body(in_ref, place_ref, flip_ref, weight_ref, mirror_ref):
    count, depth, lanes = in_ref.shape
    steps, size, _ = weight_ref.shape
    packs = steps * size // depth
    inner = depth // size
    total = 0.0
    for source in range(count):
        high, low = split(in_ref[source])
        chosen = place_ref[pl.ds(source * lanes, lanes), :]
        total = total + dot(high, chosen) + dot(low, chosen)

    def block(step, side):
        pack, rest = divmod(step, inner)
        start = (2 * pack + side) * lanes if side < 2 else 2 * packs * lanes
        return total[rest * size : (rest + 1) * size, start : start + lanes]

    def flipped(cells):
        high, low = split(cells)
        return dot(flip_ref[...], high) + dot(flip_ref[...], low)

    lane_ids = lax.broadcasted_iota(jnp.int32, (size, lanes), 1)
    extra = [block(step, 2) for step in range(steps)]
    extra = [
        pltpu.roll(cells, lanes - step // inner, 1) if step // inner else cells
        for step, cells in enumerate(extra)
    ]
    straight = jnp.zeros((size, lanes), jnp.float32)
    opposite = straight
    for step in range(steps):
        against = facing(extra, step)
        for part in range(2):
            spot = 2 * step + part
            sign = 1.0 - 2.0 * part
            straight = jnp.where(lane_ids == spot, sign * roll_to(extra[step], spot), straight)
            opposite = jnp.where(lane_ids == spot, sign * roll_to(against, spot), opposite)
    mirror_ref[...] = straight + flipped(opposite)
    backs = [block(step, 1) for step in range(steps)]
    for step in range(0, steps, 2):
        both = jnp.concatenate([facing(backs, step), facing(backs, step + 1)], axis=1)
        both = flipped(both)
        weight_ref[step] = block(step, 0) + both[:, :lanes]
        weight_ref[step + 1] = block(step + 1, 0) + both[:, lanes:]


def roll_to(cells, spot):
    return pltpu.roll(cells, spot, 1) if spot else cells


def filtered(values, dirty, weights):
    height, length = values.shape
    count = lax.axis_size("rows")
    lanes = length // (2 * count)
    steps = height // 16
    size = length // steps
    width = weights.shape[1]
    f32 = jnp.float32
    pick, place, flip = [jnp.asarray(table) for table in weight_tables(length, count, steps)]
    there, back = [jnp.asarray(table) for table in row_tables(length, count)]
    down, up, turns = [jnp.asarray(table) for table in column_tables(length, count, steps)]
    shape = lambda *dims: jax.ShapeDtypeStruct(dims, f32)
    packs = lanes * count // width
    depth = length // packs
    half = height // 2
    vmem = pl.BlockSpec(memory_space=pltpu.VMEM)
    smem = pl.BlockSpec(memory_space=pltpu.SMEM)
    me = jnp.reshape(lax.axis_index("rows"), (1,)).astype(jnp.int32)

    thick = depth // 2
    sent = pl.pallas_call(
        weight_pick_body,
        grid=(2,),
        in_specs=[
            pl.BlockSpec((packs, thick, width), lambda i: (0, i, 0)),
            pl.BlockSpec((width, width), lambda i: (0, 0)),
        ],
        out_specs=pl.BlockSpec((count, thick, lanes), lambda i: (0, i, 0)),
        out_shape=shape(count, depth, lanes),
        compiler_params=pltpu.CompilerParams(vmem_limit_bytes=vmem_bytes),
        name="weight_pick",
        cost_estimate=busy(4),
    )(weights.reshape(packs, depth, width), pick)
    sent = lax.all_to_all(sent, "rows", 0, 0, tiled=True)
    ahead = pl.pallas_call(
        functools.partial(row_forward_body, steps),
        in_specs=[smem, vmem, vmem],
        out_specs=[vmem] * count,
        out_shape=[shape(2, height, lanes)] * count,
        scratch_shapes=[pltpu.VMEM((2, count, height, 2 * lanes), jnp.bfloat16)],
        compiler_params=pltpu.CompilerParams(vmem_limit_bytes=vmem_bytes),
        name="row_forward",
        cost_estimate=busy(6),
    )(me, values, there)
    ahead = [ahead[0]] + [
        lax.ppermute(ahead[turn], "rows", [(i, i ^ turn) for i in range(count)])
        for turn in range(1, count)
    ]
    mine = jnp.where(lax.axis_index("rows") == 0, place[0], place[1])
    weight, mirror = whole_call(
        weight_place_body,
        [shape(steps, size, lanes), shape(size, lanes)],
        [],
        "weight_place",
        10,
    )(sent, mine, flip)
    edge, core = pl.pallas_call(
        functools.partial(column_body, steps, count),
        in_specs=[smem] + [vmem] * (count + 6),
        out_specs=[vmem] * 2,
        out_shape=[shape(count, 2, half, lanes)] * 2,
        scratch_shapes=[
            pltpu.VMEM((2 * size, steps * lanes), f32),
            pltpu.VMEM((2, steps, size, lanes), f32),
            pltpu.VMEM((2, steps, size, lanes), f32),
        ],
        compiler_params=pltpu.CompilerParams(vmem_limit_bytes=vmem_bytes),
        name="column_filter",
        cost_estimate=busy(10),
    )(me, *ahead, down, up, turns, weight, mirror, flip)
    edge = lax.all_to_all(edge, "rows", 0, 0, tiled=True)
    core = lax.all_to_all(core, "rows", 0, 0, tiled=True)
    chans = lax.axis_size("chan")
    part = length // chans
    quarter = height // 4

    def row_inverse(cells, old, blocks):
        rows_spec = pl.BlockSpec((quarter, length), lambda i: (blocks[0] + i * blocks[1], 0))
        whole = lambda *dims: pl.BlockSpec(dims, lambda i: (0,) * len(dims))
        return pl.pallas_call(
            functools.partial(row_inverse_body, steps),
            grid=(2,),
            in_specs=[
                whole(*cells.shape),
                whole(*back.shape),
                rows_spec,
                rows_spec,
                pl.BlockSpec(memory_space=pl.ANY),
            ],
            out_specs=[rows_spec, whole(chans, half + 8, part)],
            out_shape=[shape(height, length), shape(chans, half + 8, part)],
            scratch_shapes=[pltpu.VMEM((count, half, 2 * lanes), f32)],
            input_output_aliases={4: 0} if old is not dirty else {},
            compiler_params=pltpu.CompilerParams(vmem_limit_bytes=vmem_bytes),
            name="row_inverse",
        cost_estimate=busy(5),
        )(cells, back, values, dirty, old)

    def pieces_for(cells):
        me = lax.axis_index("chan")
        return [
            lax.dynamic_index_in_dim(cells, me ^ turn, 0, keepdims=False) for turn in range(chans)
        ]

    def over_chans(pieces):
        return [pieces[0]] + [
            lax.ppermute(pieces[turn], "chan", [(i, i ^ turn) for i in range(chans)])
            for turn in range(1, chans)
        ]

    def in_order(earlier, later):
        both = lax.optimization_barrier((*earlier, *later))
        return list(both[: len(earlier)]), list(both[len(earlier) :])

    residual, outer = row_inverse(edge, dirty, (0, 3))
    outer = over_chans(pieces_for(outer))
    residual, inner = row_inverse(core, residual, (1, 1))
    outer, inner = in_order(outer, pieces_for(inner))
    inner = over_chans(inner)
    ahead_pairs = [(i, i + 1) for i in range(count - 1)]
    back_pairs = [(i + 1, i) for i in range(count - 1)]
    last = jnp.stack([cells[half - halo_rows :] for cells in outer])
    first = jnp.stack(
        [jnp.concatenate([cells[:halo_rows], cells[half:]], axis=0) for cells in outer]
    )
    last = lax.ppermute(last, "rows", ahead_pairs)
    first = lax.ppermute(first, "rows", back_pairs)
    above = [last[c] for c in range(chans)]
    below = [first[c] for c in range(chans)]
    chan_id, row_id = lax.axis_index("chan"), lax.axis_index("rows")
    at_end = jnp.stack(
        [chan_id == 0, chan_id == chans - 1, row_id == 0, row_id == count - 1]
    ).astype(jnp.int32)
    vmem = pl.BlockSpec(memory_space=pltpu.VMEM)

    def starlet(sources, rows, spans, fills, microseconds):
        extent = max(fill[0] + fill[3] for fill in fills) + 16
        cells = pltpu.VMEM((chans, extent, part + lanes), f32)
        return pl.pallas_call(
            functools.partial(starlet_body, chans, spans, fills),
            in_specs=[pl.BlockSpec(memory_space=pltpu.SMEM)] + [vmem] * len(sources),
            out_specs=[vmem] * 2,
            out_shape=[shape(chans, 4, rows, part), shape(3, 8, lanes)],
            scratch_shapes=[cells, cells],
            compiler_params=pltpu.CompilerParams(vmem_limit_bytes=vmem_bytes),
            name="starlet",
            cost_estimate=busy(microseconds),
        )(at_end, *sources)

    reach = quarter + halo_rows
    most = quarter - halo_rows
    skirt = halo_rows // 8
    outer_details, outer_peaks = starlet(
        outer + above + below,
        2 * most,
        (
            (0, reach // 8, 0, True, False),
            (reach + 16, reach // 8, most, False, True),
        ),
        (
            (0, 1, 0, halo_rows, halo_rows, (half - halo_rows) // 8),
            (halo_rows, 0, 0, quarter, half, 0),
            (reach + 16, 0, quarter, quarter, half, quarter // 8),
            (reach + 16 + quarter, 2, 0, halo_rows, halo_rows, 0),
        ),
        12,
    )
    inner_details, inner_peaks = starlet(
        outer + inner,
        half + 2 * halo_rows,
        ((0, half // 8 + 4 * skirt, 0, False, False),),
        (
            (0, 0, quarter - 2 * halo_rows, 2 * halo_rows, half, (quarter - 2 * halo_rows) // 8),
            (2 * halo_rows, 1, 0, half, half, 0),
            (2 * halo_rows + half, 0, quarter, 2 * halo_rows, half, quarter // 8),
        ),
        12,
    )
    peaks = jnp.maximum(outer_peaks, inner_peaks)
    peaks = max_over(peaks, "rows", range(1, 2))
    peaks = max_over(peaks, "rows", range(2, count, 2))
    peaks = max_over(peaks, "chan", range(1, chans))

    def shrink(details):
        rows = details.shape[2]
        thick = rows // 2
        return pl.pallas_call(
            functools.partial(shrink_body, chans),
            grid=(2,),
            in_specs=[
                pl.BlockSpec((chans, 4, thick, part), lambda i: (0, 0, i, 0)),
                pl.BlockSpec((3, 8, lanes), lambda i: (0, 0, 0)),
            ],
            out_specs=[pl.BlockSpec((thick, part), lambda i: (i, 0))] * chans,
            out_shape=[shape(rows, part)] * chans,
            compiler_params=pltpu.CompilerParams(vmem_limit_bytes=vmem_bytes),
            name="shrink",
            cost_estimate=busy(3),
        )(details, peaks)

    outer = over_chans(shrink(outer_details))
    outer, inner = in_order(outer, shrink(inner_details))
    inner = over_chans(inner)
    new_estimate = pl.pallas_call(
        join_body,
        in_specs=[pl.BlockSpec(memory_space=pltpu.SMEM)] + [vmem] * (2 * chans),
        out_specs=vmem,
        out_shape=shape(height, length),
        compiler_params=pltpu.CompilerParams(vmem_limit_bytes=vmem_bytes),
        name="join",
        cost_estimate=busy(4),
    )(jnp.reshape(chan_id, (1,)).astype(jnp.int32), *outer, *inner)
    return new_estimate, residual


def filtered_plain(values, dirty, weights):
    height, length = values.shape
    row_count = lax.axis_size("rows")
    narrow = length // row_count
    spec_real, spec_imag = dft_last(values, jnp.zeros_like(values), -1.0)
    spec_real = spec_real.reshape(height, row_count, narrow)
    spec_imag = spec_imag.reshape(height, row_count, narrow)
    col_real, col_imag = columns_forward(
        (
            lax.all_to_all(spec_real, "rows", split_axis=1, concat_axis=0, tiled=True),
            lax.all_to_all(spec_imag, "rows", split_axis=1, concat_axis=0, tiled=True),
        )
    )
    prod_real = weights * col_real[:, 0, :]
    prod_imag = weights * col_imag[:, 0, :]
    back_real, back_imag = dft_first(prod_real, prod_imag, 1.0)
    back_real = back_real.reshape(row_count, height, narrow)
    back_imag = back_imag.reshape(row_count, height, narrow)
    blurred = rows_inverse(
        (
            lax.all_to_all(back_real, "rows", split_axis=0, concat_axis=2, tiled=True),
            lax.all_to_all(back_imag, "rows", split_axis=0, concat_axis=2, tiled=True),
        )
    )[0]
    residual = dirty - blurred
    return residual, values + step_size * residual


def joined_plain(halfway):
    height, length = halfway.shape
    depth = 14
    chan_count = lax.axis_size("chan")
    part = length // chan_count
    padded = with_halo(halfway, (("rows", 0),), depth)
    padded = jnp.pad(padded, ((0, 0), (depth, depth)))
    pieces = jnp.stack(
        [padded[:, q * part : (q + 1) * part + 2 * depth] for q in range(chan_count)]
    )
    current = lax.all_to_all(pieces, "chan", split_axis=0, concat_axis=0, tiled=True)
    row_ids = lax.axis_index("rows") * height - depth + lax.iota(jnp.int32, height + 2 * depth)
    col_ids = lax.axis_index("chan") * part - depth + lax.iota(jnp.int32, part + 2 * depth)
    margin = depth
    details = []
    for scale_level in range(3):
        reach = 2 << scale_level
        smoother = smooth_both(current, 1 << scale_level)
        row_ids = row_ids[reach:-reach]
        col_ids = col_ids[reach:-reach]
        inside = ((row_ids >= 0) & (row_ids < length))[:, None] & (
            (col_ids >= 0) & (col_ids < length)
        )[None, :]
        smoother = jnp.where(inside[None], smoother, 0.0)
        new_margin = margin - reach
        details.append(
            current[:, margin : margin + height, margin : margin + part]
            - smoother[:, new_margin : new_margin + height, new_margin : new_margin + part]
        )
        current = smoother
        margin = new_margin
    energies = [jnp.sum(detail * detail, axis=0) for detail in details]
    peaks = jnp.stack([jnp.broadcast_to(jnp.max(energy), (128,)) for energy in energies])
    for axis in ("rows", "chan"):
        peaks = lax.pmax(peaks, axis)
    output = current
    for scale_level in range(3):
        threshold = fractions[scale_level] * jnp.sqrt(peaks[scale_level, 0])
        factor = 1.0 - threshold / jnp.maximum(jnp.sqrt(energies[scale_level]), threshold)
        output = output + factor[None] * details[scale_level]
    output = lax.all_to_all(output, "chan", split_axis=0, concat_axis=2, tiled=True)[0]
    return output


def shards(estimate, dirty_image, psf_weights):
    values, dirty, weights = estimate[0], dirty_image[0], psf_weights[0]
    height, length = values.shape
    row_count, chan_count = lax.axis_size("rows"), lax.axis_size("chan")
    whole_tiles = length == 2 * row_count * lane_count and length % (chan_count * lane_count) == 0
    if whole_tiles and chan_count & (chan_count - 1) == 0:
        new_estimate, residual = filtered(values, dirty, weights)
    else:
        residual, halfway = filtered_plain(values, dirty, weights)
        new_estimate = joined_plain(halfway)
    return (new_estimate[None], residual[None])


def solution(mesh):
    return jax.shard_map(
        shards,
        mesh=mesh,
        in_specs=(P("chan", "rows", None), P("chan", "rows", None), P("chan", None, "rows")),
        out_specs=(P("chan", "rows", None), P("chan", "rows", None)),
        check_vma=False,
    )
```

```python
import functools
import math

import jax
import jax.numpy as jnp
import ml_dtypes
import numpy as np
from jax import lax
from jax.experimental import pallas as pl
from jax.experimental.pallas import tpu as pltpu
from jax.sharding import PartitionSpec as P

fractions = (0.03, 0.02, 0.015)
taps = (0.0625, 0.25, 0.375, 0.25, 0.0625)
step_size = 0.9
inner_length = 128
highest = lax.Precision.HIGHEST
lane_count = 128
mebibyte = 1024 * 1024
rim = 16
halo_rows = 16
unroll = 2


def with_halo(cells, sides, width):
    for axis, dim in sides:
        count = lax.axis_size(axis)
        ends = count - 1
        head = lax.slice_in_dim(cells, 0, width, axis=dim)
        tail = lax.slice_in_dim(cells, cells.shape[dim] - width, cells.shape[dim], axis=dim)
        cells = jnp.concatenate(
            [
                lax.ppermute(tail, axis, [(i, (i + 1) % count) for i in range(ends)]),
                cells,
                lax.ppermute(head, axis, [((i + 1) % count, i) for i in range(ends)]),
            ],
            axis=dim,
        )
    return cells


def phase_table(first_count, second_count, length, sign):
    first_ids = lax.iota(jnp.int32, first_count)
    second_ids = lax.iota(jnp.int32, second_count)
    angles = (first_ids[:, None] * second_ids[None, :] % length).astype(jnp.float32) * (
        2.0 * math.pi / length
    )
    return (jnp.cos(angles), sign * jnp.sin(angles))


def dft_last(real_in, imag_in, sign):
    batch, length = real_in.shape
    outer = length // inner_length
    real_part = real_in.reshape(batch, outer, inner_length)
    imag_part = imag_in.reshape(batch, outer, inner_length)
    cos_small, sin_small = phase_table(outer, outer, outer, sign)
    first_real = jnp.einsum("kn,bnm->bkm", cos_small, real_part, precision=highest) - jnp.einsum(
        "kn,bnm->bkm", sin_small, imag_part, precision=highest
    )
    first_imag = jnp.einsum("kn,bnm->bkm", cos_small, imag_part, precision=highest) + jnp.einsum(
        "kn,bnm->bkm", sin_small, real_part, precision=highest
    )
    cos_twist, sin_twist = phase_table(outer, inner_length, length, sign)
    twist_real = first_real * cos_twist - first_imag * sin_twist
    twist_imag = first_imag * cos_twist + first_real * sin_twist
    cos_large, sin_large = phase_table(inner_length, inner_length, inner_length, sign)
    last_real = jnp.einsum("bkm,mj->bkj", twist_real, cos_large, precision=highest) - jnp.einsum(
        "bkm,mj->bkj", twist_imag, sin_large, precision=highest
    )
    last_imag = jnp.einsum("bkm,mj->bkj", twist_imag, cos_large, precision=highest) + jnp.einsum(
        "bkm,mj->bkj", twist_real, sin_large, precision=highest
    )
    return (
        jnp.transpose(last_real, (0, 2, 1)).reshape(batch, length),
        jnp.transpose(last_imag, (0, 2, 1)).reshape(batch, length),
    )


def dft_first(real_in, imag_in, sign):
    length, width = real_in.shape
    outer = length // inner_length
    real_part = real_in.reshape(outer, inner_length, width)
    imag_part = imag_in.reshape(outer, inner_length, width)
    cos_small, sin_small = phase_table(outer, outer, outer, sign)
    first_real = jnp.einsum("kn,nmw->kmw", cos_small, real_part, precision=highest) - jnp.einsum(
        "kn,nmw->kmw", sin_small, imag_part, precision=highest
    )
    first_imag = jnp.einsum("kn,nmw->kmw", cos_small, imag_part, precision=highest) + jnp.einsum(
        "kn,nmw->kmw", sin_small, real_part, precision=highest
    )
    cos_twist, sin_twist = phase_table(outer, inner_length, length, sign)
    cos_twist = cos_twist[:, :, None]
    sin_twist = sin_twist[:, :, None]
    twist_real = first_real * cos_twist - first_imag * sin_twist
    twist_imag = first_imag * cos_twist + first_real * sin_twist
    cos_large, sin_large = phase_table(inner_length, inner_length, inner_length, sign)
    last_real = jnp.einsum("kmw,mj->kjw", twist_real, cos_large, precision=highest) - jnp.einsum(
        "kmw,mj->kjw", twist_imag, sin_large, precision=highest
    )
    last_imag = jnp.einsum("kmw,mj->kjw", twist_imag, cos_large, precision=highest) + jnp.einsum(
        "kmw,mj->kjw", twist_real, sin_large, precision=highest
    )
    return (
        jnp.transpose(last_real, (1, 0, 2)).reshape(length, width),
        jnp.transpose(last_imag, (1, 0, 2)).reshape(length, width),
    )


def columns_forward(pieces):
    real_out, imag_out = dft_first(pieces[0][:, 0, :], pieces[1][:, 0, :], -1.0)
    return (real_out[:, None, :], imag_out[:, None, :])


def rows_inverse(pieces):
    real_in = pieces[0][0]
    imag_in = pieces[1][0]
    length = real_in.shape[1]
    real_out, imag_out = dft_last(real_in, imag_in, 1.0)
    return (real_out * (1.0 / (length * length)))[None]


def max_over(cells, axis, distances):
    count = lax.axis_size(axis)
    others = [
        lax.ppermute(cells, axis, [(i, i ^ distance) for i in range(count)])
        for distance in distances
    ]
    for other in others:
        cells = jnp.maximum(cells, other)
    return cells


def smooth_both(values, spacing):
    for dim in (2, 1):
        count = values.shape[dim] - 4 * spacing
        total = taps[0] * lax.slice_in_dim(values, 0, count, axis=dim)
        for tap_index in range(1, 5):
            start = tap_index * spacing
            total = total + taps[tap_index] * lax.slice_in_dim(
                values, start, start + count, axis=dim
            )
        values = total
    return values


def real_dft(parts):
    count = len(parts)
    if count == 1:
        return [(parts[0], None)]
    if count == 2:
        return [(parts[0] + parts[1], None), (parts[0] - parts[1], None)]
    even = real_dft(parts[0::2])
    odd = real_dft(parts[1::2])
    out = [None] * (count // 2 + 1)
    for k in range(count // 4 + 1):
        turned = spin(odd[k], -2.0 * math.pi * k / count)
        out[k] = pair_add(even[k], turned)
        low = pair_sub(even[k], turned)
        out[count // 2 - k] = (low[0], None if low[1] is None else -low[1])
    out[0] = (out[0][0], None)
    out[count // 2] = (out[count // 2][0], None)
    return out


def real_inverse_dft(pairs):
    count = 2 * (len(pairs) - 1)
    if count == 2:
        return [pairs[0][0] + pairs[1][0], pairs[0][0] - pairs[1][0]]
    even, odd = [], []
    for k in range(count // 4 + 1):
        low = pairs[k]
        high = pairs[count // 2 - k]
        high = (high[0], None if high[1] is None else -high[1])
        even.append(pair_add(low, high))
        odd.append(spin(pair_sub(low, high), 2.0 * math.pi * k / count))
    for half in (even, odd):
        half[0] = (half[0][0], None)
        half[-1] = (half[-1][0], None)
    even = real_inverse_dft(even)
    odd = real_inverse_dft(odd)
    return [cells for both in zip(even, odd) for cells in both]


def complex_dft(pairs, sign):
    count = len(pairs)
    if count == 1:
        return pairs
    even = complex_dft(pairs[0::2], sign)
    odd = complex_dft(pairs[1::2], sign)
    turned = [spin(odd[k], sign * 2.0 * math.pi * k / count) for k in range(count // 2)]
    return [pair_add(a, b) for a, b in zip(even, turned)] + [
        pair_sub(a, b) for a, b in zip(even, turned)
    ]


def pair_add(a, b):
    if a[1] is None or b[1] is None:
        return (a[0] + b[0], a[1] if b[1] is None else b[1])
    return (a[0] + b[0], a[1] + b[1])


def pair_sub(a, b):
    if b[1] is None:
        return (a[0] - b[0], a[1])
    return (a[0] - b[0], -b[1] if a[1] is None else a[1] - b[1])


def spin(pair, angle):
    quarter = angle / (0.5 * math.pi)
    turns = round(quarter)
    real, imag = pair
    if abs(quarter - turns) < 1e-9:
        turns %= 4
        if turns == 0:
            return pair
        if turns == 2:
            return (-real, None if imag is None else -imag)
        if imag is None:
            return (jnp.zeros_like(real), real if turns == 1 else -real)
        return (-imag, real) if turns == 1 else (imag, -real)
    cosine, sine = math.cos(angle), math.sin(angle)
    if imag is None:
        return (real * cosine, real * sine)
    if abs(abs(cosine) - abs(sine)) < 1e-9:
        a, b = math.copysign(1.0, cosine), math.copysign(1.0, sine)
        root = abs(cosine)
        first = real if a > 0 else -real
        second = imag if b > 0 else -imag
        third = real if b > 0 else -real
        fourth = imag if a > 0 else -imag
        return ((first - second) * root, (third + fourth) * root)
    return (real * cosine - imag * sine, real * sine + imag * cosine)


def split(cells):
    high = cells.astype(jnp.bfloat16)
    return high, (cells - high.astype(jnp.float32)).astype(jnp.bfloat16)


def dot(a, b):
    return jnp.dot(a, b, preferred_element_type=jnp.float32)


def split_table(table):
    high = table.astype(np.float32).astype(ml_dtypes.bfloat16)
    low = (table - high.astype(np.float64)).astype(np.float32).astype(ml_dtypes.bfloat16)
    return np.stack([high, low], axis=-3)


def group_columns(length, count, group):
    radix = 2 * count
    lanes = length // radix
    spots = np.arange(lanes)
    if group:
        return group + radix * spots
    half = lanes // 2
    return np.where(spots < half, radix * spots, count + radix * (spots - half))


def row_tables(length, count):
    radix = 2 * count
    lanes = length // radix
    half = lanes // 2
    spots = np.arange(lanes)
    there, back = [], []
    for group in range(count):
        columns = group_columns(length, count, group)
        angles = 2.0 * np.pi * (np.outer(spots, columns) % length) / length
        cosine, sine = np.cos(angles), np.sin(angles)
        ahead = np.zeros((2, lanes, 2, lanes))
        behind = np.zeros((2, lanes, 2, lanes))
        if group:
            ahead[0, :, 0], ahead[0, :, 1] = cosine, -sine
            ahead[1, :, 0], ahead[1, :, 1] = sine, cosine
            behind[0, :, 0], behind[0, :, 1] = cosine.T, sine.T
            behind[1, :, 0], behind[1, :, 1] = -sine.T, cosine.T
        else:
            for part, where in enumerate((slice(0, half), slice(half, lanes))):
                ahead[part, :, 0, where] = cosine[:, where]
                ahead[part, :, 1, where] = -sine[:, where]
                behind[0, where, part] = 2.0 * cosine[:, where].T
                behind[1, where, part] = -2.0 * sine[:, where].T
            ahead[0, :, 1, 0] = (-1.0) ** spots
            behind[0, 0, 0] = 1.0
            behind[1, 0, 0] = (-1.0) ** spots
        there.append(ahead.reshape(2 * lanes, 2 * lanes))
        back.append(behind.reshape(2 * lanes, 2 * lanes) / float(length) ** 2)
    return split_table(np.stack(there)), split_table(np.stack(back))


def column_tables(length, count, steps):
    size = length // steps
    each = size // count
    quarter = each // 4
    order = np.r_[0:quarter, each - quarter : each, quarter : each - quarter]
    order = (np.arange(count)[:, None] * each + order[None]).reshape(-1)
    order = np.concatenate([order, size + order])
    spots = np.arange(size)
    angles = 2.0 * np.pi * (np.outer(spots, spots) % size) / size
    cosine, sine = np.cos(angles), np.sin(angles)
    there = np.block([[cosine, sine], [-sine, cosine]])
    turns = np.zeros((2, size, lane_count), np.float32)
    angles = 2.0 * np.pi * np.outer(spots, np.arange(steps)) / length
    turns[0, :, :steps], turns[1, :, :steps] = np.cos(angles), np.sin(angles)
    return split_table(there), split_table(there.T[order]), turns


def weight_tables(length, count, steps):
    width = length // count
    lanes = length // (2 * count)
    per_class = width // (2 * count)
    packs = lanes // (2 * per_class)
    radix = 2 * count

    def classes(group):
        return (group, radix - group) if group else (0, count)

    pick = np.zeros((width, count, 2, per_class))
    for group in range(count):
        for which, kind in enumerate(classes(group)):
            for q in range(per_class):
                pick[radix * q + kind, group, which, q] = 1.0
    place = np.zeros((2, count, lanes, packs * 2 + 1, lanes))

    def slot(group, column, pack):
        column %= length
        source, rest = divmod(column, width)
        which = classes(group).index(rest % radix)
        return source, pack * 2 * per_class + which * per_class + rest // radix

    for version, group in ((0, 0), (1, 1)):
        columns = group_columns(length, count, group)
        for pack in range(packs):
            for lane in range(lanes):
                column = int(columns[lane])
                mates = [(column, 0, 0.5), (-column, 1, 0.5)]
                if group == 0 and lane == 0:
                    mates = [(c, s, 0.25) for c in (0, length // 2) for s in (0, 1)]
                for mate, side, value in mates:
                    source, where = slot(group, mate, pack)
                    place[version, source, where, pack * 2 + side, lane] += value
            if group == 0:
                for mate, value in ((0, 0.25), (length // 2, -0.25)):
                    source, where = slot(group, mate, pack)
                    place[version, source, where, packs * 2, pack] += value
    flip = np.zeros((length // steps, length // steps))
    flip[np.arange(len(flip)), -np.arange(len(flip))] = 1.0
    as_half = lambda table: table.astype(np.float32).astype(ml_dtypes.bfloat16)
    return (
        as_half(pick.reshape(width, width)),
        as_half(place.reshape(2, count * lanes, (packs * 2 + 1) * lanes)),
        as_half(flip),
    )


def busy(microseconds):
    return pl.CostEstimate(
        flops=0, bytes_accessed=int(microseconds * 3.5e6), transcendentals=0
    )


def whole_call(body, out_shapes, scratch, name, microseconds):
    return pl.pallas_call(
        body,
        out_shape=out_shapes,
        scratch_shapes=scratch,
        compiler_params=pltpu.CompilerParams(vmem_limit_bytes=24 * mebibyte),
        name=name,
        cost_estimate=busy(microseconds),
    )


def row_forward_body(steps, me_ref, x_ref, table_ref, *refs):
    out_refs, held = refs[:-1], refs[-1]
    groups = len(out_refs)
    _, height, lanes = out_refs[0].shape
    each = height // steps
    for start in range(0, height, 16):
        rows = pl.ds(start, 16)
        tiles = [x_ref[rows, pl.ds(lanes * t, lanes)] for t in range(2 * groups)]
        pairs = real_dft(tiles)
        pairs = [(pairs[0][0], pairs[groups][0])] + pairs[1:groups]
        for group in range(groups):
            high, low = split(jnp.concatenate(pairs[group], axis=1))
            held[0, group, rows, :] = high
            held[1, group, rows, :] = low
    for turn, out_ref in enumerate(out_refs):
        group = me_ref[0] ^ turn
        done = (
            dot(held[0, group], table_ref[group, 0])
            + dot(held[1, group], table_ref[group, 0])
            + dot(held[0, group], table_ref[group, 1])
        )
        for start in range(0, height, 8):
            spread = pl.ds(start % steps * each + start // steps, 8, stride=each)
            out_ref[0, spread, :] = done[start : start + 8, :lanes]
            out_ref[1, spread, :] = done[start : start + 8, lanes:]


def row_inverse_body(steps, groups, me_ref, *refs):
    in_refs = refs[:groups]
    table_ref, est_ref, dirty_ref, _, res_ref, half_ref, held = refs[groups:]
    _, chunk, lanes = in_refs[0].shape
    parts, _, wide = half_ref.shape
    each = chunk // steps
    block = est_ref.shape[0]
    turn = pl.program_id(0)

    @pl.when(turn == 0)
    def _():
        for partner, in_ref in enumerate(in_refs):
            group = me_ref[0] ^ partner
            halves = []
            for part in range(2):
                pieces = [
                    in_ref[part, pl.ds(start % steps * each + start // steps, 8, stride=each), :]
                    for start in range(0, chunk, 8)
                ]
                halves.append(jnp.concatenate(pieces, axis=0))
            high, low = split(jnp.concatenate(halves, axis=1))
            held[group] = (
                dot(high, table_ref[group, 0])
                + dot(low, table_ref[group, 0])
                + dot(high, table_ref[group, 1])
            )

    per = wide // lanes
    lane_ids = lax.broadcasted_iota(jnp.int32, (8, lanes), 1)
    sides = [None] * parts
    for start in range(0, block, 8):
        rows = pl.ds(start, 8)
        chunk_rows = pl.ds(pl.multiple_of(turn * block + start, 8), 8)
        pairs = [
            (held[group, chunk_rows, pl.ds(0, lanes)], held[group, chunk_rows, pl.ds(lanes, lanes)])
            for group in range(groups)
        ]
        pairs = [(pairs[0][0], None)] + pairs[1:] + [(pairs[0][1], None)]
        tiles = real_inverse_dft(pairs)
        for t in range(2 * groups):
            where = pl.ds(lanes * t, lanes)
            residual = dirty_ref[rows, where] - tiles[t]
            res_ref[rows, where] = residual
            tiles[t] = est_ref[rows, where] + step_size * residual
            half_ref[t // per, chunk_rows, pl.ds(lanes * (t % per), lanes)] = tiles[t]
        offset = start // 8 * 2 * rim % lanes
        for part in range(parts):
            done = jnp.zeros_like(tiles[0]) if offset == 0 else sides[part]
            if part > 0:
                turned = pltpu.roll(tiles[part * per - 1], (offset + rim) % lanes, 1)
                done = jnp.where((lane_ids >= offset) & (lane_ids < offset + rim), turned, done)
            if part < parts - 1:
                turned = pltpu.roll(tiles[(part + 1) * per], (offset + rim) % lanes, 1)
                done = jnp.where(
                    (lane_ids >= offset + rim) & (lane_ids < offset + 2 * rim), turned, done
                )
            sides[part] = done
            if offset + 2 * rim == lanes:
                spot = turn * (block // 8 * 2 * rim // lanes) + start // 8 * 2 * rim // lanes
                where = pl.ds(pl.multiple_of(spot * lanes, lanes), lanes)
                half_ref[part, pl.ds(chunk, 8), where] = done


def starlet_body(chans, spans, fills, ends_ref, before_ref, *refs):
    sources, (detail_ref, peak_ref, ping, pong) = refs[:-4], refs[-4:]
    part = detail_ref.shape[3]
    lanes = lane_count
    tiles = part // lanes
    total = part + lanes
    no_left, no_right = ends_ref[0] > 0, ends_ref[1] > 0
    no_top, no_bottom = ends_ref[2] > 0, ends_ref[3] > 0
    lane_ids = lax.broadcasted_iota(jnp.int32, (8, lanes), 1)
    outside = ((lane_ids >= lanes // 2) & no_left) | ((lane_ids < lanes // 2) & no_right)
    for chan in range(chans):
        for target, index, source_row, count, pack_row, group in fills:
            source = sources[index * chans + chan]
            to = pl.ds(8 + target, count)
            ping[chan, to, pl.ds(0, part)] = source[pl.ds(source_row, count), :]
            for i in range(count // 8):
                spot = (group + i) * 2 * rim
                tile = source[pl.ds(pack_row, 8), pl.ds(spot // lanes * lanes, lanes)]
                shift = (lanes - spot % lanes - rim) % lanes
                to = pl.ds(8 + target + 8 * i, 8)
                ping[chan, to, pl.ds(part, lanes)] = pltpu.roll(tile, shift, 1)

    skirt = halo_rows // 8
    peaks = [jnp.zeros((8, part), jnp.float32)] * 3
    for start, blocks, out_start, top, bottom in spans:
        for level in range(3):
            gap = 1 << level
            before, after = (ping, pong) if level % 2 == 0 else (pong, ping)

            def step(i, peak, level, gap, before, after):
                base = 8 + start + 8 * i
                if not isinstance(i, int):
                    base = pl.multiple_of(base, 8)
                inner = not isinstance(i, int)
                energy = 0.0
                for chan in range(chans):
                    window = before[chan, pl.ds(base - 8, 24), :]
                    near = window[8 - gap : 16 - gap] + window[8 + gap : 16 + gap]
                    far = window[8 - 2 * gap : 16 - 2 * gap] + window[8 + 2 * gap : 16 + 2 * gap]
                    row = (far + 4.0 * near) + 6.0 * window[8:16]
                    near = pltpu.roll(row, gap, 1) + pltpu.roll(row, total - gap, 1)
                    far = pltpu.roll(row, 2 * gap, 1) + pltpu.roll(row, total - 2 * gap, 1)
                    smooth = ((far + 4.0 * near) + 6.0 * row) * (1.0 / 256.0)
                    whole = smooth[:, :part]
                    if level < 2:
                        side = jnp.where(outside, 0.0, smooth[:, part:])
                        if not inner and (top if i < skirt else bottom):
                            gone = no_top if i < skirt else no_bottom
                            side = jnp.where(gone, 0.0, side)
                            after[chan, pl.ds(base, 8), pl.ds(0, part)] = jnp.where(
                                gone, 0.0, whole
                            )
                        else:
                            after[chan, pl.ds(base, 8), pl.ds(0, part)] = whole
                        after[chan, pl.ds(base, 8), pl.ds(part, lanes)] = side
                    if inner:
                        to = pl.ds(pl.multiple_of(out_start + 8 * i - halo_rows, 8), 8)
                        detail = window[8:16, :part] - whole
                        detail_ref[chan, level, to, :] = detail
                        if level == 2:
                            detail_ref[chan, 3, to, :] = whole
                        energy = energy + detail * detail
                return jnp.maximum(peak, energy) if inner else peak

            step = functools.partial(step, level=level, gap=gap, before=before, after=after)
            for i in range(level, skirt):
                step(i, None)
                step(blocks - 1 - i, None)
            peaks[level] = lax.fori_loop(skirt, blocks - skirt, step, peaks[level], unroll=unroll)
    for level in range(3):
        most = before_ref[level]
        for t in range(tiles):
            most = jnp.maximum(most, peaks[level][:, t * lanes : (t + 1) * lanes])
        peak_ref[level] = most


def shrink_body(chans, detail_ref, peak_ref, *out_refs):
    factors = []
    for level in range(3):
        energy = 0.0
        for chan in range(chans):
            detail = detail_ref[chan, level]
            energy = energy + detail * detail
        energy = jnp.sqrt(energy)
        threshold = fractions[level] * jnp.sqrt(jnp.max(peak_ref[level], keepdims=True))
        threshold = jnp.broadcast_to(threshold, energy.shape)
        factors.append(1.0 - threshold / jnp.maximum(energy, threshold))
    for chan in range(chans):
        total = detail_ref[chan, 3]
        for level in range(3):
            total = total + factors[level] * detail_ref[chan, level]
        out_refs[chan][...] = total


def join_body(me_ref, *refs):
    chans = (len(refs) - 1) // 2
    out_ref = refs[-1]
    part = refs[0].shape[1]
    outer_rows, inner_rows = refs[0].shape[0] // 2, refs[chans].shape[0]
    for chan in range(chans):
        outer, inner = refs[chan], refs[chans + chan]
        columns = pl.ds(pl.multiple_of((me_ref[0] ^ chan) * part, part), part)
        out_ref[pl.ds(0, outer_rows), columns] = outer[pl.ds(0, outer_rows), :]
        out_ref[pl.ds(outer_rows, inner_rows), columns] = inner[...]
        out_ref[pl.ds(outer_rows + inner_rows, outer_rows), columns] = outer[
            pl.ds(outer_rows, outer_rows), :
        ]


def facing(blocks, step):
    rows = lax.broadcasted_iota(jnp.int32, blocks[0].shape, 0)
    return jnp.where(rows == 0, blocks[-step % len(blocks)], blocks[len(blocks) - 1 - step])


def column_body(steps, count, me_ref, *refs):
    in_refs = refs[:count]
    there_ref, back_ref, turn_ref, weight_ref, mirror_ref, flip_ref = refs[count : count + 6]
    out_refs, (gathered, held, made, ready) = refs[count + 6 : 3 * count + 6], refs[3 * count + 6 :]
    _, height, lanes = in_refs[0].shape
    each = height // steps
    size = each * count
    for turn, in_ref in enumerate(in_refs):
        source = me_ref[0] ^ turn
        for part in range(2):
            to = pl.ds(pl.multiple_of(part * size + source * each, 8), each)
            for step in range(steps):
                gathered[to, pl.ds(step * lanes, lanes)] = in_ref[part, pl.ds(step * each, each), :]
    for step in range(0, steps, 2):
        high, low = split(gathered[:, pl.ds(step * lanes, 2 * lanes)])
        done = dot(there_ref[0], high) + dot(there_ref[1], high) + dot(there_ref[0], low)
        for k in range(2):
            held[0, step + k] = done[:size, k * lanes : (k + 1) * lanes]
            held[1, step + k] = done[size:, k * lanes : (k + 1) * lanes]

    def turned(pairs, rows, sign):
        cosines, sines = turn_ref[0, rows, :], turn_ref[1, rows, :]
        out = [pairs[0]]
        for step in range(1, steps):
            real, imag = pairs[step]
            cosine = jnp.broadcast_to(cosines[:, step : step + 1], real.shape)
            sine = sign * jnp.broadcast_to(sines[:, step : step + 1], real.shape)
            out.append((real * cosine - imag * sine, imag * cosine + real * sine))
        return out

    def forward(chunk, carry):
        rows = pl.ds(pl.multiple_of(chunk * 8, 8), 8)
        pairs = [(held[0, step, rows, :], held[1, step, rows, :]) for step in range(steps)]
        for step, pair in enumerate(complex_dft(turned(pairs, rows, -1.0), -1.0)):
            held[0, step, rows, :] = pair[0]
            held[1, step, rows, :] = pair[1]
        return carry

    lax.fori_loop(0, size // 8, forward, 0)
    lane_ids = lax.broadcasted_iota(jnp.int32, (size, lanes), 1)
    lone = jnp.zeros((size, lanes), jnp.float32)
    for step in range(steps):
        for part in range(2):
            spot = 2 * step + part
            moved = facing([held[part, other] for other in range(steps)], step)
            if spot:
                moved = pltpu.roll(moved, spot, 1)
            lone = jnp.where(lane_ids == spot, moved, lone)
    high, low = split(lone)
    lone = (dot(flip_ref[...], high) + dot(flip_ref[...], low)) * mirror_ref[...]
    for step in range(steps):
        weight = weight_ref[step]
        for part in range(2):
            spot = 2 * step + part
            moved = pltpu.roll(lone, lanes - spot, 1) if spot else lone
            made[part, step] = weight * held[part, step] + jnp.where(lane_ids == 0, moved, 0.0)

    def backward(chunk, carry):
        rows = pl.ds(pl.multiple_of(chunk * 8, 8), 8)
        pairs = [(made[0, step, rows, :], made[1, step, rows, :]) for step in range(steps)]
        for step, pair in enumerate(turned(complex_dft(pairs, 1.0), rows, 1.0)):
            made[0, step, rows, :] = pair[0]
            made[1, step, rows, :] = pair[1]
        return carry

    lax.fori_loop(0, size // 8, backward, 0)
    half = each // 2
    for step in range(0, steps, 2):
        block = [
            jnp.concatenate([made[part, step + k] for k in range(2)], axis=1) for part in range(2)
        ]
        high, low = split(jnp.concatenate(block, axis=0))
        done = dot(back_ref[0], high) + dot(back_ref[1], high) + dot(back_ref[0], low)
        for k in range(2):
            ready[step + k] = done[:, k * lanes : (k + 1) * lanes]
    for turn in range(count):
        target = me_ref[0] ^ turn
        for part in range(2):
            for inner in range(2):
                start = pl.multiple_of(part * size + target * each + inner * half, 8)
                for step in range(steps):
                    rows = pl.ds(step * half, half)
                    out_refs[inner * count + turn][part, rows, :] = ready[step, pl.ds(start, half), :]


def weight_pick_body(w_ref, pick_ref, out_ref):
    count, thick, lanes = out_ref.shape
    packs, _, width = w_ref.shape
    piece = lanes // packs
    chosen = []
    for pack in range(packs):
        high, low = split(w_ref[pack])
        chosen.append(dot(high, pick_ref[...]) + dot(low, pick_ref[...]))
    lane_ids = lax.broadcasted_iota(jnp.int32, (thick, lanes), 1)
    for target in range(count):
        start = target * piece // lanes * lanes
        total = None
        for pack in range(packs):
            moved = chosen[pack][:, start : start + lanes]
            shift = (pack - target) % packs * piece
            if shift:
                moved = pltpu.roll(moved, shift, 1)
            total = moved if pack == 0 else jnp.where(lane_ids >= pack * piece, moved, total)
        out_ref[target] = total


def weight_place_body(in_ref, place_ref, flip_ref, weight_ref, mirror_ref):
    count, depth, lanes = in_ref.shape
    steps, size, _ = weight_ref.shape
    packs = steps * size // depth
    inner = depth // size
    total = 0.0
    for source in range(count):
        high, low = split(in_ref[source])
        chosen = place_ref[pl.ds(source * lanes, lanes), :]
        total = total + dot(high, chosen) + dot(low, chosen)

    def block(step, side):
        pack, rest = divmod(step, inner)
        start = (2 * pack + side) * lanes if side < 2 else 2 * packs * lanes
        return total[rest * size : (rest + 1) * size, start : start + lanes]

    def flipped(cells):
        high, low = split(cells)
        return dot(flip_ref[...], high) + dot(flip_ref[...], low)

    lane_ids = lax.broadcasted_iota(jnp.int32, (size, lanes), 1)
    extra = [block(step, 2) for step in range(steps)]
    extra = [
        pltpu.roll(cells, lanes - step // inner, 1) if step // inner else cells
        for step, cells in enumerate(extra)
    ]
    straight = jnp.zeros((size, lanes), jnp.float32)
    opposite = straight
    for step in range(steps):
        against = facing(extra, step)
        for part in range(2):
            spot = 2 * step + part
            sign = 1.0 - 2.0 * part
            straight = jnp.where(lane_ids == spot, sign * roll_to(extra[step], spot), straight)
            opposite = jnp.where(lane_ids == spot, sign * roll_to(against, spot), opposite)
    mirror_ref[...] = straight + flipped(opposite)
    backs = [block(step, 1) for step in range(steps)]
    for step in range(0, steps, 2):
        both = jnp.concatenate([facing(backs, step), facing(backs, step + 1)], axis=1)
        both = flipped(both)
        weight_ref[step] = block(step, 0) + both[:, :lanes]
        weight_ref[step + 1] = block(step + 1, 0) + both[:, lanes:]


def roll_to(cells, spot):
    return pltpu.roll(cells, spot, 1) if spot else cells


def filtered(values, dirty, weights):
    height, length = values.shape
    count = lax.axis_size("rows")
    lanes = length // (2 * count)
    steps = height // 16
    size = length // steps
    width = weights.shape[1]
    f32 = jnp.float32
    pick, place, flip = [jnp.asarray(table) for table in weight_tables(length, count, steps)]
    there, back = [jnp.asarray(table) for table in row_tables(length, count)]
    down, up, turns = [jnp.asarray(table) for table in column_tables(length, count, steps)]
    shape = lambda *dims: jax.ShapeDtypeStruct(dims, f32)
    packs = lanes * count // width
    depth = length // packs
    half = height // 2
    vmem = pl.BlockSpec(memory_space=pltpu.VMEM)
    smem = pl.BlockSpec(memory_space=pltpu.SMEM)
    me = jnp.reshape(lax.axis_index("rows"), (1,)).astype(jnp.int32)

    thick = depth // 2
    sent = pl.pallas_call(
        weight_pick_body,
        grid=(2,),
        in_specs=[
            pl.BlockSpec((packs, thick, width), lambda i: (0, i, 0)),
            pl.BlockSpec((width, width), lambda i: (0, 0)),
        ],
        out_specs=pl.BlockSpec((count, thick, lanes), lambda i: (0, i, 0)),
        out_shape=shape(count, depth, lanes),
        compiler_params=pltpu.CompilerParams(vmem_limit_bytes=56 * mebibyte),
        name="weight_pick",
        cost_estimate=busy(4),
    )(weights.reshape(packs, depth, width), pick)
    sent = lax.all_to_all(sent, "rows", 0, 0, tiled=True)
    ahead = pl.pallas_call(
        functools.partial(row_forward_body, steps),
        in_specs=[smem, vmem, vmem],
        out_specs=[vmem] * count,
        out_shape=[shape(2, height, lanes)] * count,
        scratch_shapes=[pltpu.VMEM((2, count, height, 2 * lanes), jnp.bfloat16)],
        compiler_params=pltpu.CompilerParams(vmem_limit_bytes=56 * mebibyte),
        name="row_forward",
        cost_estimate=busy(6),
    )(me, values, there)

    def over_rows(pieces):
        return [pieces[0]] + [
            lax.ppermute(pieces[turn], "rows", [(i, i ^ turn) for i in range(count)])
            for turn in range(1, count)
        ]

    ahead = over_rows(ahead)
    mine = jnp.where(lax.axis_index("rows") == 0, place[0], place[1])
    weight, mirror = whole_call(
        weight_place_body,
        [shape(steps, size, lanes), shape(size, lanes)],
        [],
        "weight_place",
        10,
    )(sent, mine, flip)
    behind = pl.pallas_call(
        functools.partial(column_body, steps, count),
        in_specs=[smem] + [vmem] * (count + 6),
        out_specs=[vmem] * (2 * count),
        out_shape=[shape(2, half, lanes)] * (2 * count),
        scratch_shapes=[
            pltpu.VMEM((2 * size, steps * lanes), f32),
            pltpu.VMEM((2, steps, size, lanes), f32),
            pltpu.VMEM((2, steps, size, lanes), f32),
            pltpu.VMEM((steps, 2 * size, lanes), f32),
        ],
        compiler_params=pltpu.CompilerParams(vmem_limit_bytes=24 * mebibyte),
        name="column_filter",
        cost_estimate=busy(10),
    )(me, *ahead, down, up, turns, weight, mirror, flip)
    edge, core = over_rows(behind[:count]), behind[count:]
    core = over_rows(core)
    chans = lax.axis_size("chan")
    part = length // chans
    quarter = height // 4

    def row_inverse(cells, old, blocks):
        rows_spec = pl.BlockSpec((quarter, length), lambda i: (blocks[0] + i * blocks[1], 0))
        whole = lambda *dims: pl.BlockSpec(dims, lambda i: (0,) * len(dims))
        return pl.pallas_call(
            functools.partial(row_inverse_body, steps, count),
            grid=(2,),
            in_specs=[smem]
            + [whole(2, half, lanes)] * count
            + [
                whole(*back.shape),
                rows_spec,
                rows_spec,
                pl.BlockSpec(memory_space=pl.ANY),
            ],
            out_specs=[rows_spec, whole(chans, half + 8, part)],
            out_shape=[shape(height, length), shape(chans, half + 8, part)],
            scratch_shapes=[pltpu.VMEM((count, half, 2 * lanes), f32)],
            input_output_aliases={count + 4: 0} if old is not dirty else {},
            compiler_params=pltpu.CompilerParams(vmem_limit_bytes=56 * mebibyte),
            name="row_inverse",
        cost_estimate=busy(5),
        )(me, *cells, back, values, dirty, old)

    def pieces_for(cells):
        me = lax.axis_index("chan")
        return [
            lax.dynamic_index_in_dim(cells, me ^ turn, 0, keepdims=False) for turn in range(chans)
        ]

    def over_chans(pieces):
        return [pieces[0]] + [
            lax.ppermute(pieces[turn], "chan", [(i, i ^ turn) for i in range(chans)])
            for turn in range(1, chans)
        ]

    def in_order(earlier, later):
        both = lax.optimization_barrier((*earlier, *later))
        return list(both[: len(earlier)]), list(both[len(earlier) :])

    residual, outer = row_inverse(edge, dirty, (0, 3))
    outer = over_chans(pieces_for(outer))
    residual, inner = row_inverse(core, residual, (1, 1))
    inner = over_chans(pieces_for(inner))
    outer, (inner[1],) = in_order(outer, [inner[1]])
    ahead_pairs = [(i, i + 1) for i in range(count - 1)]
    back_pairs = [(i + 1, i) for i in range(count - 1)]
    last = jnp.stack([cells[half - halo_rows :] for cells in outer])
    first = jnp.stack(
        [jnp.concatenate([cells[:halo_rows], cells[half:]], axis=0) for cells in outer]
    )
    last = lax.ppermute(last, "rows", ahead_pairs)
    first = lax.ppermute(first, "rows", back_pairs)
    above = [last[c] for c in range(chans)]
    below = [first[c] for c in range(chans)]
    chan_id, row_id = lax.axis_index("chan"), lax.axis_index("rows")
    at_end = jnp.stack(
        [chan_id == 0, chan_id == chans - 1, row_id == 0, row_id == count - 1]
    ).astype(jnp.int32)

    def starlet(sources, before, rows, spans, fills, microseconds):
        extent = max(fill[0] + fill[3] for fill in fills) + 16
        cells = pltpu.VMEM((chans, extent, part + lanes), f32)
        return pl.pallas_call(
            functools.partial(starlet_body, chans, spans, fills),
            in_specs=[smem] + [vmem] * (1 + len(sources)),
            out_specs=[vmem] * 2,
            out_shape=[shape(chans, 4, rows, part), shape(3, 8, lanes)],
            scratch_shapes=[cells, cells],
            compiler_params=pltpu.CompilerParams(vmem_limit_bytes=20 * mebibyte),
            name="starlet",
            cost_estimate=busy(microseconds),
        )(at_end, before, *sources)

    reach = quarter + halo_rows
    most = quarter - halo_rows
    skirt = halo_rows // 8
    outer_details, outer_peaks = starlet(
        outer + above + below,
        jnp.zeros((3, 8, lanes), f32),
        2 * most,
        (
            (0, reach // 8, 0, True, False),
            (reach + 16, reach // 8, most, False, True),
        ),
        (
            (0, 1, 0, halo_rows, halo_rows, (half - halo_rows) // 8),
            (halo_rows, 0, 0, quarter, half, 0),
            (reach + 16, 0, quarter, quarter, half, quarter // 8),
            (reach + 16 + quarter, 2, 0, halo_rows, halo_rows, 0),
        ),
        12,
    )
    inner_details, peaks = starlet(
        outer + inner,
        outer_peaks,
        half + 2 * halo_rows,
        ((0, half // 8 + 4 * skirt, 0, False, False),),
        (
            (0, 0, quarter - 2 * halo_rows, 2 * halo_rows, half, (quarter - 2 * halo_rows) // 8),
            (2 * halo_rows, 1, 0, half, half, 0),
            (2 * halo_rows + half, 0, quarter, 2 * halo_rows, half, quarter // 8),
        ),
        12,
    )
    peaks = max_over(peaks, "rows", range(1, 2))
    peaks = max_over(peaks, "rows", range(2, count, 2))
    peaks = max_over(peaks, "chan", range(1, chans))

    def shrink(details):
        rows = details.shape[2]
        thick = rows // 2
        return pl.pallas_call(
            functools.partial(shrink_body, chans),
            grid=(2,),
            in_specs=[
                pl.BlockSpec((chans, 4, thick, part), lambda i: (0, 0, i, 0)),
                pl.BlockSpec((3, 8, lanes), lambda i: (0, 0, 0)),
            ],
            out_specs=[pl.BlockSpec((thick, part), lambda i: (i, 0))] * chans,
            out_shape=[shape(rows, part)] * chans,
            compiler_params=pltpu.CompilerParams(vmem_limit_bytes=14 * mebibyte),
            name="shrink",
            cost_estimate=busy(3),
        )(details, peaks)

    outer = over_chans(shrink(outer_details))
    outer, inner = in_order(outer, shrink(inner_details))
    inner = over_chans(inner)
    new_estimate = pl.pallas_call(
        join_body,
        in_specs=[pl.BlockSpec(memory_space=pltpu.SMEM)] + [vmem] * (2 * chans),
        out_specs=vmem,
        out_shape=shape(height, length),
        compiler_params=pltpu.CompilerParams(vmem_limit_bytes=12 * mebibyte),
        name="join",
        cost_estimate=busy(4),
    )(jnp.reshape(chan_id, (1,)).astype(jnp.int32), *outer, *inner)
    return new_estimate, residual


def filtered_plain(values, dirty, weights):
    height, length = values.shape
    row_count = lax.axis_size("rows")
    narrow = length // row_count
    spec_real, spec_imag = dft_last(values, jnp.zeros_like(values), -1.0)
    spec_real = spec_real.reshape(height, row_count, narrow)
    spec_imag = spec_imag.reshape(height, row_count, narrow)
    col_real, col_imag = columns_forward(
        (
            lax.all_to_all(spec_real, "rows", split_axis=1, concat_axis=0, tiled=True),
            lax.all_to_all(spec_imag, "rows", split_axis=1, concat_axis=0, tiled=True),
        )
    )
    prod_real = weights * col_real[:, 0, :]
    prod_imag = weights * col_imag[:, 0, :]
    back_real, back_imag = dft_first(prod_real, prod_imag, 1.0)
    back_real = back_real.reshape(row_count, height, narrow)
    back_imag = back_imag.reshape(row_count, height, narrow)
    blurred = rows_inverse(
        (
            lax.all_to_all(back_real, "rows", split_axis=0, concat_axis=2, tiled=True),
            lax.all_to_all(back_imag, "rows", split_axis=0, concat_axis=2, tiled=True),
        )
    )[0]
    residual = dirty - blurred
    return residual, values + step_size * residual


def joined_plain(halfway):
    height, length = halfway.shape
    depth = 14
    chan_count = lax.axis_size("chan")
    part = length // chan_count
    padded = with_halo(halfway, (("rows", 0),), depth)
    padded = jnp.pad(padded, ((0, 0), (depth, depth)))
    pieces = jnp.stack(
        [padded[:, q * part : (q + 1) * part + 2 * depth] for q in range(chan_count)]
    )
    current = lax.all_to_all(pieces, "chan", split_axis=0, concat_axis=0, tiled=True)
    row_ids = lax.axis_index("rows") * height - depth + lax.iota(jnp.int32, height + 2 * depth)
    col_ids = lax.axis_index("chan") * part - depth + lax.iota(jnp.int32, part + 2 * depth)
    margin = depth
    details = []
    for scale_level in range(3):
        reach = 2 << scale_level
        smoother = smooth_both(current, 1 << scale_level)
        row_ids = row_ids[reach:-reach]
        col_ids = col_ids[reach:-reach]
        inside = ((row_ids >= 0) & (row_ids < length))[:, None] & (
            (col_ids >= 0) & (col_ids < length)
        )[None, :]
        smoother = jnp.where(inside[None], smoother, 0.0)
        new_margin = margin - reach
        details.append(
            current[:, margin : margin + height, margin : margin + part]
            - smoother[:, new_margin : new_margin + height, new_margin : new_margin + part]
        )
        current = smoother
        margin = new_margin
    energies = [jnp.sum(detail * detail, axis=0) for detail in details]
    peaks = jnp.stack([jnp.broadcast_to(jnp.max(energy), (128,)) for energy in energies])
    for axis in ("rows", "chan"):
        peaks = lax.pmax(peaks, axis)
    output = current
    for scale_level in range(3):
        threshold = fractions[scale_level] * jnp.sqrt(peaks[scale_level, 0])
        factor = 1.0 - threshold / jnp.maximum(jnp.sqrt(energies[scale_level]), threshold)
        output = output + factor[None] * details[scale_level]
    output = lax.all_to_all(output, "chan", split_axis=0, concat_axis=2, tiled=True)[0]
    return output


def shards(estimate, dirty_image, psf_weights):
    values, dirty, weights = estimate[0], dirty_image[0], psf_weights[0]
    height, length = values.shape
    row_count, chan_count = lax.axis_size("rows"), lax.axis_size("chan")
    whole_tiles = length == 2 * row_count * lane_count and length % (chan_count * lane_count) == 0
    if whole_tiles and chan_count & (chan_count - 1) == 0:
        new_estimate, residual = filtered(values, dirty, weights)
    else:
        residual, halfway = filtered_plain(values, dirty, weights)
        new_estimate = joined_plain(halfway)
    return (new_estimate[None], residual[None])


def solution(mesh):
    return jax.shard_map(
        shards,
        mesh=mesh,
        in_specs=(P("chan", "rows", None), P("chan", "rows", None), P("chan", None, "rows")),
        out_specs=(P("chan", "rows", None), P("chan", "rows", None)),
        check_vma=False,
    )
```

```python
import functools
import math

import jax
import jax.numpy as jnp
import ml_dtypes
import numpy as np
from jax import lax
from jax.experimental import pallas as pl
from jax.experimental.pallas import tpu as pltpu
from jax.sharding import PartitionSpec as P

fractions = (0.03, 0.02, 0.015)
taps = (0.0625, 0.25, 0.375, 0.25, 0.0625)
step_size = 0.9
inner_length = 128
highest = lax.Precision.HIGHEST
lane_count = 128
mebibyte = 1024 * 1024
rim = 16
halo_rows = 16


def with_halo(cells, sides, width):
    for axis, dim in sides:
        count = lax.axis_size(axis)
        ends = count - 1
        head = lax.slice_in_dim(cells, 0, width, axis=dim)
        tail = lax.slice_in_dim(cells, cells.shape[dim] - width, cells.shape[dim], axis=dim)
        cells = jnp.concatenate(
            [
                lax.ppermute(tail, axis, [(i, (i + 1) % count) for i in range(ends)]),
                cells,
                lax.ppermute(head, axis, [((i + 1) % count, i) for i in range(ends)]),
            ],
            axis=dim,
        )
    return cells


def phase_table(first_count, second_count, length, sign):
    first_ids = lax.iota(jnp.int32, first_count)
    second_ids = lax.iota(jnp.int32, second_count)
    angles = (first_ids[:, None] * second_ids[None, :] % length).astype(jnp.float32) * (
        2.0 * math.pi / length
    )
    return (jnp.cos(angles), sign * jnp.sin(angles))


def dft_last(real_in, imag_in, sign):
    batch, length = real_in.shape
    outer = length // inner_length
    real_part = real_in.reshape(batch, outer, inner_length)
    imag_part = imag_in.reshape(batch, outer, inner_length)
    cos_small, sin_small = phase_table(outer, outer, outer, sign)
    first_real = jnp.einsum("kn,bnm->bkm", cos_small, real_part, precision=highest) - jnp.einsum(
        "kn,bnm->bkm", sin_small, imag_part, precision=highest
    )
    first_imag = jnp.einsum("kn,bnm->bkm", cos_small, imag_part, precision=highest) + jnp.einsum(
        "kn,bnm->bkm", sin_small, real_part, precision=highest
    )
    cos_twist, sin_twist = phase_table(outer, inner_length, length, sign)
    twist_real = first_real * cos_twist - first_imag * sin_twist
    twist_imag = first_imag * cos_twist + first_real * sin_twist
    cos_large, sin_large = phase_table(inner_length, inner_length, inner_length, sign)
    last_real = jnp.einsum("bkm,mj->bkj", twist_real, cos_large, precision=highest) - jnp.einsum(
        "bkm,mj->bkj", twist_imag, sin_large, precision=highest
    )
    last_imag = jnp.einsum("bkm,mj->bkj", twist_imag, cos_large, precision=highest) + jnp.einsum(
        "bkm,mj->bkj", twist_real, sin_large, precision=highest
    )
    return (
        jnp.transpose(last_real, (0, 2, 1)).reshape(batch, length),
        jnp.transpose(last_imag, (0, 2, 1)).reshape(batch, length),
    )


def dft_first(real_in, imag_in, sign):
    length, width = real_in.shape
    outer = length // inner_length
    real_part = real_in.reshape(outer, inner_length, width)
    imag_part = imag_in.reshape(outer, inner_length, width)
    cos_small, sin_small = phase_table(outer, outer, outer, sign)
    first_real = jnp.einsum("kn,nmw->kmw", cos_small, real_part, precision=highest) - jnp.einsum(
        "kn,nmw->kmw", sin_small, imag_part, precision=highest
    )
    first_imag = jnp.einsum("kn,nmw->kmw", cos_small, imag_part, precision=highest) + jnp.einsum(
        "kn,nmw->kmw", sin_small, real_part, precision=highest
    )
    cos_twist, sin_twist = phase_table(outer, inner_length, length, sign)
    cos_twist = cos_twist[:, :, None]
    sin_twist = sin_twist[:, :, None]
    twist_real = first_real * cos_twist - first_imag * sin_twist
    twist_imag = first_imag * cos_twist + first_real * sin_twist
    cos_large, sin_large = phase_table(inner_length, inner_length, inner_length, sign)
    last_real = jnp.einsum("kmw,mj->kjw", twist_real, cos_large, precision=highest) - jnp.einsum(
        "kmw,mj->kjw", twist_imag, sin_large, precision=highest
    )
    last_imag = jnp.einsum("kmw,mj->kjw", twist_imag, cos_large, precision=highest) + jnp.einsum(
        "kmw,mj->kjw", twist_real, sin_large, precision=highest
    )
    return (
        jnp.transpose(last_real, (1, 0, 2)).reshape(length, width),
        jnp.transpose(last_imag, (1, 0, 2)).reshape(length, width),
    )


def columns_forward(pieces):
    real_out, imag_out = dft_first(pieces[0][:, 0, :], pieces[1][:, 0, :], -1.0)
    return (real_out[:, None, :], imag_out[:, None, :])


def rows_inverse(pieces):
    real_in = pieces[0][0]
    imag_in = pieces[1][0]
    length = real_in.shape[1]
    real_out, imag_out = dft_last(real_in, imag_in, 1.0)
    return (real_out * (1.0 / (length * length)))[None]


def max_over(cells, axis, distances):
    count = lax.axis_size(axis)
    others = [
        lax.ppermute(cells, axis, [(i, i ^ distance) for i in range(count)])
        for distance in distances
    ]
    for other in others:
        cells = jnp.maximum(cells, other)
    return cells


def smooth_both(values, spacing):
    for dim in (2, 1):
        count = values.shape[dim] - 4 * spacing
        total = taps[0] * lax.slice_in_dim(values, 0, count, axis=dim)
        for tap_index in range(1, 5):
            start = tap_index * spacing
            total = total + taps[tap_index] * lax.slice_in_dim(
                values, start, start + count, axis=dim
            )
        values = total
    return values


def real_dft(parts):
    count = len(parts)
    if count == 1:
        return [(parts[0], None)]
    if count == 2:
        return [(parts[0] + parts[1], None), (parts[0] - parts[1], None)]
    even = real_dft(parts[0::2])
    odd = real_dft(parts[1::2])
    out = [None] * (count // 2 + 1)
    for k in range(count // 4 + 1):
        turned = spin(odd[k], -2.0 * math.pi * k / count)
        out[k] = pair_add(even[k], turned)
        low = pair_sub(even[k], turned)
        out[count // 2 - k] = (low[0], None if low[1] is None else -low[1])
    out[0] = (out[0][0], None)
    out[count // 2] = (out[count // 2][0], None)
    return out


def real_inverse_dft(pairs):
    count = 2 * (len(pairs) - 1)
    if count == 2:
        return [pairs[0][0] + pairs[1][0], pairs[0][0] - pairs[1][0]]
    even, odd = [], []
    for k in range(count // 4 + 1):
        low = pairs[k]
        high = pairs[count // 2 - k]
        high = (high[0], None if high[1] is None else -high[1])
        even.append(pair_add(low, high))
        odd.append(spin(pair_sub(low, high), 2.0 * math.pi * k / count))
    for half in (even, odd):
        half[0] = (half[0][0], None)
        half[-1] = (half[-1][0], None)
    even = real_inverse_dft(even)
    odd = real_inverse_dft(odd)
    return [cells for both in zip(even, odd) for cells in both]


def complex_dft(pairs, sign):
    count = len(pairs)
    if count == 1:
        return pairs
    even = complex_dft(pairs[0::2], sign)
    odd = complex_dft(pairs[1::2], sign)
    turned = [spin(odd[k], sign * 2.0 * math.pi * k / count) for k in range(count // 2)]
    return [pair_add(a, b) for a, b in zip(even, turned)] + [
        pair_sub(a, b) for a, b in zip(even, turned)
    ]


def pair_add(a, b):
    if a[1] is None or b[1] is None:
        return (a[0] + b[0], a[1] if b[1] is None else b[1])
    return (a[0] + b[0], a[1] + b[1])


def pair_sub(a, b):
    if b[1] is None:
        return (a[0] - b[0], a[1])
    return (a[0] - b[0], -b[1] if a[1] is None else a[1] - b[1])


def spin(pair, angle):
    quarter = angle / (0.5 * math.pi)
    turns = round(quarter)
    real, imag = pair
    if abs(quarter - turns) < 1e-9:
        turns %= 4
        if turns == 0:
            return pair
        if turns == 2:
            return (-real, None if imag is None else -imag)
        if imag is None:
            return (jnp.zeros_like(real), real if turns == 1 else -real)
        return (-imag, real) if turns == 1 else (imag, -real)
    cosine, sine = math.cos(angle), math.sin(angle)
    if imag is None:
        return (real * cosine, real * sine)
    if abs(abs(cosine) - abs(sine)) < 1e-9:
        a, b = math.copysign(1.0, cosine), math.copysign(1.0, sine)
        root = abs(cosine)
        first = real if a > 0 else -real
        second = imag if b > 0 else -imag
        third = real if b > 0 else -real
        fourth = imag if a > 0 else -imag
        return ((first - second) * root, (third + fourth) * root)
    return (real * cosine - imag * sine, real * sine + imag * cosine)


def split(cells):
    high = cells.astype(jnp.bfloat16)
    return high, (cells - high.astype(jnp.float32)).astype(jnp.bfloat16)


def dot(a, b):
    return jnp.dot(a, b, preferred_element_type=jnp.float32)


def split_table(table):
    high = table.astype(np.float32).astype(ml_dtypes.bfloat16)
    low = (table - high.astype(np.float64)).astype(np.float32).astype(ml_dtypes.bfloat16)
    return np.stack([high, low], axis=-3)


def group_columns(length, count, group):
    radix = 2 * count
    lanes = length // radix
    spots = np.arange(lanes)
    if group:
        return group + radix * spots
    half = lanes // 2
    return np.where(spots < half, radix * spots, count + radix * (spots - half))


def row_tables(length, count):
    radix = 2 * count
    lanes = length // radix
    half = lanes // 2
    spots = np.arange(lanes)
    there, back = [], []
    for group in range(count):
        columns = group_columns(length, count, group)
        angles = 2.0 * np.pi * (np.outer(spots, columns) % length) / length
        cosine, sine = np.cos(angles), np.sin(angles)
        ahead = np.zeros((2, lanes, 2, lanes))
        behind = np.zeros((2, lanes, 2, lanes))
        if group:
            ahead[0, :, 0], ahead[0, :, 1] = cosine, -sine
            ahead[1, :, 0], ahead[1, :, 1] = sine, cosine
            behind[0, :, 0], behind[0, :, 1] = cosine.T, sine.T
            behind[1, :, 0], behind[1, :, 1] = -sine.T, cosine.T
        else:
            for part, where in enumerate((slice(0, half), slice(half, lanes))):
                ahead[part, :, 0, where] = cosine[:, where]
                ahead[part, :, 1, where] = -sine[:, where]
                behind[0, where, part] = 2.0 * cosine[:, where].T
                behind[1, where, part] = -2.0 * sine[:, where].T
            ahead[0, :, 1, 0] = (-1.0) ** spots
            behind[0, 0, 0] = 1.0
            behind[1, 0, 0] = (-1.0) ** spots
        there.append(ahead.reshape(2 * lanes, 2 * lanes))
        back.append(behind.reshape(2 * lanes, 2 * lanes) / float(length) ** 2)
    return split_table(np.stack(there)), split_table(np.stack(back))


def column_tables(length, count, steps):
    size = length // steps
    each = size // count
    quarter = each // 4
    order = np.r_[0:quarter, each - quarter : each, quarter : each - quarter]
    order = (np.arange(count)[:, None] * each + order[None]).reshape(-1)
    order = np.concatenate([order, size + order])
    spots = np.arange(size)
    angles = 2.0 * np.pi * (np.outer(spots, spots) % size) / size
    cosine, sine = np.cos(angles), np.sin(angles)
    there = np.block([[cosine, sine], [-sine, cosine]])
    turns = np.zeros((2, size, lane_count), np.float32)
    angles = 2.0 * np.pi * np.outer(spots, np.arange(steps)) / length
    turns[0, :, :steps], turns[1, :, :steps] = np.cos(angles), np.sin(angles)
    return split_table(there), split_table(there.T[order]), turns


def weight_tables(length, count, steps):
    width = length // count
    lanes = length // (2 * count)
    per_class = width // (2 * count)
    packs = lanes // (2 * per_class)
    radix = 2 * count

    def classes(group):
        return (group, radix - group) if group else (0, count)

    pick = np.zeros((width, count, 2, per_class))
    for group in range(count):
        for which, kind in enumerate(classes(group)):
            for q in range(per_class):
                pick[radix * q + kind, group, which, q] = 1.0
    place = np.zeros((2, count, lanes, packs * 2 + 1, lanes))

    def slot(group, column, pack):
        column %= length
        source, rest = divmod(column, width)
        which = classes(group).index(rest % radix)
        return source, pack * 2 * per_class + which * per_class + rest // radix

    for version, group in ((0, 0), (1, 1)):
        columns = group_columns(length, count, group)
        for pack in range(packs):
            for lane in range(lanes):
                column = int(columns[lane])
                mates = [(column, 0, 0.5), (-column, 1, 0.5)]
                if group == 0 and lane == 0:
                    mates = [(c, s, 0.25) for c in (0, length // 2) for s in (0, 1)]
                for mate, side, value in mates:
                    source, where = slot(group, mate, pack)
                    place[version, source, where, pack * 2 + side, lane] += value
            if group == 0:
                for mate, value in ((0, 0.25), (length // 2, -0.25)):
                    source, where = slot(group, mate, pack)
                    place[version, source, where, packs * 2, pack] += value
    flip = np.zeros((length // steps, length // steps))
    flip[np.arange(len(flip)), -np.arange(len(flip))] = 1.0
    as_half = lambda table: table.astype(np.float32).astype(ml_dtypes.bfloat16)
    return (
        as_half(pick.reshape(width, width)),
        as_half(place.reshape(2, count * lanes, (packs * 2 + 1) * lanes)),
        as_half(flip),
    )


def busy(microseconds):
    return pl.CostEstimate(
        flops=0, bytes_accessed=int(microseconds * 3.5e6), transcendentals=0
    )


def whole_call(body, out_shapes, scratch, name, microseconds):
    return pl.pallas_call(
        body,
        out_shape=out_shapes,
        scratch_shapes=scratch,
        compiler_params=pltpu.CompilerParams(vmem_limit_bytes=24 * mebibyte),
        name=name,
        cost_estimate=busy(microseconds),
    )


def row_forward_body(steps, me_ref, x_ref, table_ref, *refs):
    out_refs, held = refs[:-1], refs[-1]
    groups = len(out_refs)
    _, height, lanes = out_refs[0].shape
    each = height // steps
    for start in range(0, height, 16):
        rows = pl.ds(start, 16)
        tiles = [x_ref[rows, pl.ds(lanes * t, lanes)] for t in range(2 * groups)]
        pairs = real_dft(tiles)
        pairs = [(pairs[0][0], pairs[groups][0])] + pairs[1:groups]
        for group in range(groups):
            high, low = split(jnp.concatenate(pairs[group], axis=1))
            held[0, group, rows, :] = high
            held[1, group, rows, :] = low
    for turn, out_ref in enumerate(out_refs):
        group = me_ref[0] ^ turn
        done = (
            dot(held[0, group], table_ref[group, 0])
            + dot(held[1, group], table_ref[group, 0])
            + dot(held[0, group], table_ref[group, 1])
        )
        for start in range(0, height, 8):
            spread = pl.ds(start % steps * each + start // steps, 8, stride=each)
            out_ref[0, spread, :] = done[start : start + 8, :lanes]
            out_ref[1, spread, :] = done[start : start + 8, lanes:]


def row_inverse_body(steps, groups, me_ref, *refs):
    in_refs = refs[:groups]
    table_ref, est_ref, dirty_ref, _, res_ref, half_ref, held = refs[groups:]
    _, chunk, lanes = in_refs[0].shape
    parts, _, wide = half_ref.shape
    each = chunk // steps
    block = est_ref.shape[0]
    turn = pl.program_id(0)

    @pl.when(turn == 0)
    def _():
        for partner, in_ref in enumerate(in_refs):
            group = me_ref[0] ^ partner
            halves = []
            for part in range(2):
                pieces = [
                    in_ref[part, pl.ds(start % steps * each + start // steps, 8, stride=each), :]
                    for start in range(0, chunk, 8)
                ]
                halves.append(jnp.concatenate(pieces, axis=0))
            high, low = split(jnp.concatenate(halves, axis=1))
            held[group] = (
                dot(high, table_ref[group, 0])
                + dot(low, table_ref[group, 0])
                + dot(high, table_ref[group, 1])
            )

    per = wide // lanes
    lane_ids = lax.broadcasted_iota(jnp.int32, (8, lanes), 1)
    sides = [None] * parts
    for start in range(0, block, 8):
        rows = pl.ds(start, 8)
        chunk_rows = pl.ds(pl.multiple_of(turn * block + start, 8), 8)
        pairs = [
            (held[group, chunk_rows, pl.ds(0, lanes)], held[group, chunk_rows, pl.ds(lanes, lanes)])
            for group in range(groups)
        ]
        pairs = [(pairs[0][0], None)] + pairs[1:] + [(pairs[0][1], None)]
        tiles = real_inverse_dft(pairs)
        for t in range(2 * groups):
            where = pl.ds(lanes * t, lanes)
            residual = dirty_ref[rows, where] - tiles[t]
            res_ref[rows, where] = residual
            tiles[t] = est_ref[rows, where] + step_size * residual
            half_ref[t // per, chunk_rows, pl.ds(lanes * (t % per), lanes)] = tiles[t]
        offset = start // 8 * 2 * rim % lanes
        for part in range(parts):
            done = jnp.zeros_like(tiles[0]) if offset == 0 else sides[part]
            if part > 0:
                turned = pltpu.roll(tiles[part * per - 1], (offset + rim) % lanes, 1)
                done = jnp.where((lane_ids >= offset) & (lane_ids < offset + rim), turned, done)
            if part < parts - 1:
                turned = pltpu.roll(tiles[(part + 1) * per], (offset + rim) % lanes, 1)
                done = jnp.where(
                    (lane_ids >= offset + rim) & (lane_ids < offset + 2 * rim), turned, done
                )
            sides[part] = done
            if offset + 2 * rim == lanes:
                spot = turn * (block // 8 * 2 * rim // lanes) + start // 8 * 2 * rim // lanes
                where = pl.ds(pl.multiple_of(spot * lanes, lanes), lanes)
                half_ref[part, pl.ds(chunk, 8), where] = done


def starlet_body(chans, spans, fills, ends_ref, before_ref, *refs):
    sources, (detail_ref, peak_ref, ping, pong) = refs[:-4], refs[-4:]
    part = detail_ref.shape[3]
    lanes = lane_count
    tiles = part // lanes
    total = part + lanes
    no_left, no_right = ends_ref[0] > 0, ends_ref[1] > 0
    no_top, no_bottom = ends_ref[2] > 0, ends_ref[3] > 0
    lane_ids = lax.broadcasted_iota(jnp.int32, (8, lanes), 1)
    outside = ((lane_ids >= lanes // 2) & no_left) | ((lane_ids < lanes // 2) & no_right)
    for chan in range(chans):
        for target, index, source_row, count, pack_row, group in fills:
            source = sources[index * chans + chan]
            to = pl.ds(8 + target, count)
            ping[chan, to, pl.ds(0, part)] = source[pl.ds(source_row, count), :]
            for i in range(count // 8):
                spot = (group + i) * 2 * rim
                tile = source[pl.ds(pack_row, 8), pl.ds(spot // lanes * lanes, lanes)]
                shift = (lanes - spot % lanes - rim) % lanes
                to = pl.ds(8 + target + 8 * i, 8)
                ping[chan, to, pl.ds(part, lanes)] = pltpu.roll(tile, shift, 1)

    skirt = halo_rows // 8
    peaks = [jnp.zeros((8, part), jnp.float32)] * 3
    for start, blocks, out_start, top, bottom in spans:
        for level in range(3):
            gap = 1 << level
            before, after = (ping, pong) if level % 2 == 0 else (pong, ping)

            def step(i, peak, level, gap, before, after):
                base = 8 + start + 8 * i
                if not isinstance(i, int):
                    base = pl.multiple_of(base, 8)
                inner = not isinstance(i, int)
                energy = 0.0
                for chan in range(chans):
                    window = before[chan, pl.ds(base - 8, 24), :]
                    near = window[8 - gap : 16 - gap] + window[8 + gap : 16 + gap]
                    far = window[8 - 2 * gap : 16 - 2 * gap] + window[8 + 2 * gap : 16 + 2 * gap]
                    row = (far + 4.0 * near) + 6.0 * window[8:16]
                    near = pltpu.roll(row, gap, 1) + pltpu.roll(row, total - gap, 1)
                    far = pltpu.roll(row, 2 * gap, 1) + pltpu.roll(row, total - 2 * gap, 1)
                    smooth = ((far + 4.0 * near) + 6.0 * row) * (1.0 / 256.0)
                    whole = smooth[:, :part]
                    if level < 2:
                        side = jnp.where(outside, 0.0, smooth[:, part:])
                        if not inner and (top if i < skirt else bottom):
                            gone = no_top if i < skirt else no_bottom
                            side = jnp.where(gone, 0.0, side)
                            after[chan, pl.ds(base, 8), pl.ds(0, part)] = jnp.where(
                                gone, 0.0, whole
                            )
                        else:
                            after[chan, pl.ds(base, 8), pl.ds(0, part)] = whole
                        after[chan, pl.ds(base, 8), pl.ds(part, lanes)] = side
                    if inner:
                        to = pl.ds(pl.multiple_of(out_start + 8 * i - halo_rows, 8), 8)
                        detail = window[8:16, :part] - whole
                        detail_ref[chan, level, to, :] = detail
                        if level == 2:
                            detail_ref[chan, 3, to, :] = whole
                        energy = energy + detail * detail
                return jnp.maximum(peak, energy) if inner else peak

            step = functools.partial(step, level=level, gap=gap, before=before, after=after)
            for i in range(level, skirt):
                step(i, None)
                step(blocks - 1 - i, None)
            peaks[level] = lax.fori_loop(
                skirt, blocks - skirt, step, peaks[level], unroll=(blocks - 2 * skirt) // 2
            )
    for level in range(3):
        most = before_ref[level]
        for t in range(tiles):
            most = jnp.maximum(most, peaks[level][:, t * lanes : (t + 1) * lanes])
        peak_ref[level] = most


def shrink_body(chans, detail_ref, peak_ref, *out_refs):
    factors = []
    for level in range(3):
        energy = 0.0
        for chan in range(chans):
            detail = detail_ref[chan, level]
            energy = energy + detail * detail
        energy = jnp.sqrt(energy)
        threshold = fractions[level] * jnp.sqrt(jnp.max(peak_ref[level], keepdims=True))
        threshold = jnp.broadcast_to(threshold, energy.shape)
        factors.append(1.0 - threshold / jnp.maximum(energy, threshold))
    for chan in range(chans):
        total = detail_ref[chan, 3]
        for level in range(3):
            total = total + factors[level] * detail_ref[chan, level]
        out_refs[chan][...] = total


def join_body(me_ref, *refs):
    chans = (len(refs) - 1) // 2
    out_ref = refs[-1]
    part = refs[0].shape[1]
    outer_rows, inner_rows = refs[0].shape[0] // 2, refs[chans].shape[0]
    for chan in range(chans):
        outer, inner = refs[chan], refs[chans + chan]
        columns = pl.ds(pl.multiple_of((me_ref[0] ^ chan) * part, part), part)
        out_ref[pl.ds(0, outer_rows), columns] = outer[pl.ds(0, outer_rows), :]
        out_ref[pl.ds(outer_rows, inner_rows), columns] = inner[...]
        out_ref[pl.ds(outer_rows + inner_rows, outer_rows), columns] = outer[
            pl.ds(outer_rows, outer_rows), :
        ]


def facing(blocks, step):
    rows = lax.broadcasted_iota(jnp.int32, blocks[0].shape, 0)
    return jnp.where(rows == 0, blocks[-step % len(blocks)], blocks[len(blocks) - 1 - step])


def column_body(steps, count, me_ref, *refs):
    in_refs = refs[:count]
    there_ref, back_ref, turn_ref, weight_ref, mirror_ref, flip_ref = refs[count : count + 6]
    out_refs, (gathered, held, made, ready) = refs[count + 6 : 3 * count + 6], refs[3 * count + 6 :]
    _, height, lanes = in_refs[0].shape
    each = height // steps
    size = each * count
    for turn, in_ref in enumerate(in_refs):
        source = me_ref[0] ^ turn
        for part in range(2):
            to = pl.ds(pl.multiple_of(part * size + source * each, 8), each)
            for step in range(steps):
                gathered[to, pl.ds(step * lanes, lanes)] = in_ref[part, pl.ds(step * each, each), :]
    for step in range(0, steps, 2):
        high, low = split(gathered[:, pl.ds(step * lanes, 2 * lanes)])
        done = dot(there_ref[0], high) + dot(there_ref[1], high) + dot(there_ref[0], low)
        for k in range(2):
            held[0, step + k] = done[:size, k * lanes : (k + 1) * lanes]
            held[1, step + k] = done[size:, k * lanes : (k + 1) * lanes]

    def turned(pairs, rows, sign):
        cosines, sines = turn_ref[0, rows, :], turn_ref[1, rows, :]
        out = [pairs[0]]
        for step in range(1, steps):
            real, imag = pairs[step]
            cosine = jnp.broadcast_to(cosines[:, step : step + 1], real.shape)
            sine = sign * jnp.broadcast_to(sines[:, step : step + 1], real.shape)
            out.append((real * cosine - imag * sine, imag * cosine + real * sine))
        return out

    def forward(chunk, carry):
        rows = pl.ds(pl.multiple_of(chunk * 8, 8), 8)
        pairs = [(held[0, step, rows, :], held[1, step, rows, :]) for step in range(steps)]
        for step, pair in enumerate(complex_dft(turned(pairs, rows, -1.0), -1.0)):
            held[0, step, rows, :] = pair[0]
            held[1, step, rows, :] = pair[1]
        return carry

    lax.fori_loop(0, size // 8, forward, 0, unroll=4)
    lane_ids = lax.broadcasted_iota(jnp.int32, (size, lanes), 1)
    lone = jnp.zeros((size, lanes), jnp.float32)
    for step in range(steps):
        for part in range(2):
            spot = 2 * step + part
            moved = facing([held[part, other] for other in range(steps)], step)
            if spot:
                moved = pltpu.roll(moved, spot, 1)
            lone = jnp.where(lane_ids == spot, moved, lone)
    high, low = split(lone)
    lone = (dot(flip_ref[...], high) + dot(flip_ref[...], low)) * mirror_ref[...]
    for step in range(steps):
        weight = weight_ref[step]
        for part in range(2):
            spot = 2 * step + part
            moved = pltpu.roll(lone, lanes - spot, 1) if spot else lone
            made[part, step] = weight * held[part, step] + jnp.where(lane_ids == 0, moved, 0.0)

    def backward(chunk, carry):
        rows = pl.ds(pl.multiple_of(chunk * 8, 8), 8)
        pairs = [(made[0, step, rows, :], made[1, step, rows, :]) for step in range(steps)]
        for step, pair in enumerate(turned(complex_dft(pairs, 1.0), rows, 1.0)):
            made[0, step, rows, :] = pair[0]
            made[1, step, rows, :] = pair[1]
        return carry

    lax.fori_loop(0, size // 8, backward, 0, unroll=4)
    half = each // 2
    for step in range(0, steps, 2):
        block = [
            jnp.concatenate([made[part, step + k] for k in range(2)], axis=1) for part in range(2)
        ]
        high, low = split(jnp.concatenate(block, axis=0))
        done = dot(back_ref[0], high) + dot(back_ref[1], high) + dot(back_ref[0], low)
        for k in range(2):
            ready[step + k] = done[:, k * lanes : (k + 1) * lanes]
    for turn in range(count):
        target = me_ref[0] ^ turn
        for part in range(2):
            for inner in range(2):
                start = pl.multiple_of(part * size + target * each + inner * half, 8)
                for step in range(steps):
                    rows = pl.ds(step * half, half)
                    out_refs[inner * count + turn][part, rows, :] = ready[step, pl.ds(start, half), :]


def weight_pick_body(w_ref, pick_ref, out_ref):
    count, thick, lanes = out_ref.shape
    packs, _, width = w_ref.shape
    piece = lanes // packs
    chosen = []
    for pack in range(packs):
        high, low = split(w_ref[pack])
        chosen.append(dot(high, pick_ref[...]) + dot(low, pick_ref[...]))
    lane_ids = lax.broadcasted_iota(jnp.int32, (thick, lanes), 1)
    for target in range(count):
        start = target * piece // lanes * lanes
        total = None
        for pack in range(packs):
            moved = chosen[pack][:, start : start + lanes]
            shift = (pack - target) % packs * piece
            if shift:
                moved = pltpu.roll(moved, shift, 1)
            total = moved if pack == 0 else jnp.where(lane_ids >= pack * piece, moved, total)
        out_ref[target] = total


def weight_place_body(in_ref, place_ref, flip_ref, weight_ref, mirror_ref):
    count, depth, lanes = in_ref.shape
    steps, size, _ = weight_ref.shape
    packs = steps * size // depth
    inner = depth // size
    total = 0.0
    for source in range(count):
        high, low = split(in_ref[source])
        chosen = place_ref[pl.ds(source * lanes, lanes), :]
        total = total + dot(high, chosen) + dot(low, chosen)

    def block(step, side):
        pack, rest = divmod(step, inner)
        start = (2 * pack + side) * lanes if side < 2 else 2 * packs * lanes
        return total[rest * size : (rest + 1) * size, start : start + lanes]

    def flipped(cells):
        high, low = split(cells)
        return dot(flip_ref[...], high) + dot(flip_ref[...], low)

    lane_ids = lax.broadcasted_iota(jnp.int32, (size, lanes), 1)
    extra = [block(step, 2) for step in range(steps)]
    extra = [
        pltpu.roll(cells, lanes - step // inner, 1) if step // inner else cells
        for step, cells in enumerate(extra)
    ]
    straight = jnp.zeros((size, lanes), jnp.float32)
    opposite = straight
    for step in range(steps):
        against = facing(extra, step)
        for part in range(2):
            spot = 2 * step + part
            sign = 1.0 - 2.0 * part
            straight = jnp.where(lane_ids == spot, sign * roll_to(extra[step], spot), straight)
            opposite = jnp.where(lane_ids == spot, sign * roll_to(against, spot), opposite)
    mirror_ref[...] = straight + flipped(opposite)
    backs = [block(step, 1) for step in range(steps)]
    for step in range(0, steps, 2):
        both = jnp.concatenate([facing(backs, step), facing(backs, step + 1)], axis=1)
        both = flipped(both)
        weight_ref[step] = block(step, 0) + both[:, :lanes]
        weight_ref[step + 1] = block(step + 1, 0) + both[:, lanes:]


def roll_to(cells, spot):
    return pltpu.roll(cells, spot, 1) if spot else cells


def filtered(values, dirty, weights):
    height, length = values.shape
    count = lax.axis_size("rows")
    lanes = length // (2 * count)
    steps = height // 16
    size = length // steps
    width = weights.shape[1]
    f32 = jnp.float32
    pick, place, flip = [jnp.asarray(table) for table in weight_tables(length, count, steps)]
    there, back = [jnp.asarray(table) for table in row_tables(length, count)]
    down, up, turns = [jnp.asarray(table) for table in column_tables(length, count, steps)]
    shape = lambda *dims: jax.ShapeDtypeStruct(dims, f32)
    packs = lanes * count // width
    depth = length // packs
    half = height // 2
    vmem = pl.BlockSpec(memory_space=pltpu.VMEM)
    smem = pl.BlockSpec(memory_space=pltpu.SMEM)
    me = jnp.reshape(lax.axis_index("rows"), (1,)).astype(jnp.int32)

    thick = depth // 2
    sent = pl.pallas_call(
        weight_pick_body,
        grid=(2,),
        in_specs=[
            pl.BlockSpec((packs, thick, width), lambda i: (0, i, 0)),
            pl.BlockSpec((width, width), lambda i: (0, 0)),
        ],
        out_specs=pl.BlockSpec((count, thick, lanes), lambda i: (0, i, 0)),
        out_shape=shape(count, depth, lanes),
        compiler_params=pltpu.CompilerParams(vmem_limit_bytes=56 * mebibyte),
        name="weight_pick",
        cost_estimate=busy(4),
    )(weights.reshape(packs, depth, width), pick)
    sent = lax.all_to_all(sent, "rows", 0, 0, tiled=True)
    ahead = pl.pallas_call(
        functools.partial(row_forward_body, steps),
        in_specs=[smem, vmem, vmem],
        out_specs=[vmem] * count,
        out_shape=[shape(2, height, lanes)] * count,
        scratch_shapes=[pltpu.VMEM((2, count, height, 2 * lanes), jnp.bfloat16)],
        compiler_params=pltpu.CompilerParams(vmem_limit_bytes=56 * mebibyte),
        name="row_forward",
        cost_estimate=busy(6),
    )(me, values, there)

    def over_rows(pieces):
        return [pieces[0]] + [
            lax.ppermute(pieces[turn], "rows", [(i, i ^ turn) for i in range(count)])
            for turn in range(1, count)
        ]

    ahead = over_rows(ahead)
    mine = jnp.where(lax.axis_index("rows") == 0, place[0], place[1])
    weight, mirror = whole_call(
        weight_place_body,
        [shape(steps, size, lanes), shape(size, lanes)],
        [],
        "weight_place",
        10,
    )(sent, mine, flip)
    behind = pl.pallas_call(
        functools.partial(column_body, steps, count),
        in_specs=[smem] + [vmem] * (count + 6),
        out_specs=[vmem] * (2 * count),
        out_shape=[shape(2, half, lanes)] * (2 * count),
        scratch_shapes=[
            pltpu.VMEM((2 * size, steps * lanes), f32),
            pltpu.VMEM((2, steps, size, lanes), f32),
            pltpu.VMEM((2, steps, size, lanes), f32),
            pltpu.VMEM((steps, 2 * size, lanes), f32),
        ],
        compiler_params=pltpu.CompilerParams(vmem_limit_bytes=24 * mebibyte),
        name="column_filter",
        cost_estimate=busy(10),
    )(me, *ahead, down, up, turns, weight, mirror, flip)
    edge, core = over_rows(behind[:count]), behind[count:]
    core = over_rows(core)
    chans = lax.axis_size("chan")
    part = length // chans
    quarter = height // 4

    def row_inverse(cells, old, blocks):
        rows_spec = pl.BlockSpec((quarter, length), lambda i: (blocks[0] + i * blocks[1], 0))
        whole = lambda *dims: pl.BlockSpec(dims, lambda i: (0,) * len(dims))
        return pl.pallas_call(
            functools.partial(row_inverse_body, steps, count),
            grid=(2,),
            in_specs=[smem]
            + [whole(2, half, lanes)] * count
            + [
                whole(*back.shape),
                rows_spec,
                rows_spec,
                pl.BlockSpec(memory_space=pl.ANY),
            ],
            out_specs=[rows_spec, whole(chans, half + 8, part)],
            out_shape=[shape(height, length), shape(chans, half + 8, part)],
            scratch_shapes=[pltpu.VMEM((count, half, 2 * lanes), f32)],
            input_output_aliases={count + 4: 0} if old is not dirty else {},
            compiler_params=pltpu.CompilerParams(vmem_limit_bytes=56 * mebibyte),
            name="row_inverse",
        cost_estimate=busy(5),
        )(me, *cells, back, values, dirty, old)

    def pieces_for(cells):
        me = lax.axis_index("chan")
        return [
            lax.dynamic_index_in_dim(cells, me ^ turn, 0, keepdims=False) for turn in range(chans)
        ]

    def over_chans(pieces):
        return [pieces[0]] + [
            lax.ppermute(pieces[turn], "chan", [(i, i ^ turn) for i in range(chans)])
            for turn in range(1, chans)
        ]

    def in_order(earlier, later):
        both = lax.optimization_barrier((*earlier, *later))
        return list(both[: len(earlier)]), list(both[len(earlier) :])

    residual, outer = row_inverse(edge, dirty, (0, 3))
    outer = over_chans(pieces_for(outer))
    residual, inner = row_inverse(core, residual, (1, 1))
    inner = over_chans(pieces_for(inner))
    outer, (inner[1],) = in_order(outer, [inner[1]])
    ahead_pairs = [(i, i + 1) for i in range(count - 1)]
    back_pairs = [(i + 1, i) for i in range(count - 1)]
    last = jnp.stack([cells[half - halo_rows :] for cells in outer])
    first = jnp.stack(
        [jnp.concatenate([cells[:halo_rows], cells[half:]], axis=0) for cells in outer]
    )
    last = lax.ppermute(last, "rows", ahead_pairs)
    first = lax.ppermute(first, "rows", back_pairs)
    above = [last[c] for c in range(chans)]
    below = [first[c] for c in range(chans)]
    chan_id, row_id = lax.axis_index("chan"), lax.axis_index("rows")
    at_end = jnp.stack(
        [chan_id == 0, chan_id == chans - 1, row_id == 0, row_id == count - 1]
    ).astype(jnp.int32)

    def starlet(sources, before, rows, spans, fills, microseconds):
        extent = max(fill[0] + fill[3] for fill in fills) + 16
        cells = pltpu.VMEM((chans, extent, part + lanes), f32)
        return pl.pallas_call(
            functools.partial(starlet_body, chans, spans, fills),
            in_specs=[smem] + [vmem] * (1 + len(sources)),
            out_specs=[vmem] * 2,
            out_shape=[shape(chans, 4, rows, part), shape(3, 8, lanes)],
            scratch_shapes=[cells, cells],
            compiler_params=pltpu.CompilerParams(vmem_limit_bytes=20 * mebibyte),
            name="starlet",
            cost_estimate=busy(microseconds),
        )(at_end, before, *sources)

    reach = quarter + halo_rows
    most = quarter - halo_rows
    skirt = halo_rows // 8
    outer_details, outer_peaks = starlet(
        outer + above + below,
        jnp.zeros((3, 8, lanes), f32),
        2 * most,
        (
            (0, reach // 8, 0, True, False),
            (reach + 16, reach // 8, most, False, True),
        ),
        (
            (0, 1, 0, halo_rows, halo_rows, (half - halo_rows) // 8),
            (halo_rows, 0, 0, quarter, half, 0),
            (reach + 16, 0, quarter, quarter, half, quarter // 8),
            (reach + 16 + quarter, 2, 0, halo_rows, halo_rows, 0),
        ),
        12,
    )
    inner_details, peaks = starlet(
        outer + inner,
        outer_peaks,
        half + 2 * halo_rows,
        ((0, half // 8 + 4 * skirt, 0, False, False),),
        (
            (0, 0, quarter - 2 * halo_rows, 2 * halo_rows, half, (quarter - 2 * halo_rows) // 8),
            (2 * halo_rows, 1, 0, half, half, 0),
            (2 * halo_rows + half, 0, quarter, 2 * halo_rows, half, quarter // 8),
        ),
        12,
    )
    peaks = max_over(peaks, "rows", range(1, 2))
    peaks = max_over(peaks, "rows", range(2, count, 2))
    peaks = max_over(peaks, "chan", range(1, chans))

    def shrink(details):
        rows = details.shape[2]
        thick = rows // 2
        return pl.pallas_call(
            functools.partial(shrink_body, chans),
            grid=(2,),
            in_specs=[
                pl.BlockSpec((chans, 4, thick, part), lambda i: (0, 0, i, 0)),
                pl.BlockSpec((3, 8, lanes), lambda i: (0, 0, 0)),
            ],
            out_specs=[pl.BlockSpec((thick, part), lambda i: (i, 0))] * chans,
            out_shape=[shape(rows, part)] * chans,
            compiler_params=pltpu.CompilerParams(vmem_limit_bytes=14 * mebibyte),
            name="shrink",
            cost_estimate=busy(3),
        )(details, peaks)

    outer = over_chans(shrink(outer_details))
    outer, inner = in_order(outer, shrink(inner_details))
    inner = over_chans(inner)
    new_estimate = pl.pallas_call(
        join_body,
        in_specs=[pl.BlockSpec(memory_space=pltpu.SMEM)] + [vmem] * (2 * chans),
        out_specs=vmem,
        out_shape=shape(height, length),
        compiler_params=pltpu.CompilerParams(vmem_limit_bytes=12 * mebibyte),
        name="join",
        cost_estimate=busy(4),
    )(jnp.reshape(chan_id, (1,)).astype(jnp.int32), *outer, *inner)
    return new_estimate, residual


def filtered_plain(values, dirty, weights):
    height, length = values.shape
    row_count = lax.axis_size("rows")
    narrow = length // row_count
    spec_real, spec_imag = dft_last(values, jnp.zeros_like(values), -1.0)
    spec_real = spec_real.reshape(height, row_count, narrow)
    spec_imag = spec_imag.reshape(height, row_count, narrow)
    col_real, col_imag = columns_forward(
        (
            lax.all_to_all(spec_real, "rows", split_axis=1, concat_axis=0, tiled=True),
            lax.all_to_all(spec_imag, "rows", split_axis=1, concat_axis=0, tiled=True),
        )
    )
    prod_real = weights * col_real[:, 0, :]
    prod_imag = weights * col_imag[:, 0, :]
    back_real, back_imag = dft_first(prod_real, prod_imag, 1.0)
    back_real = back_real.reshape(row_count, height, narrow)
    back_imag = back_imag.reshape(row_count, height, narrow)
    blurred = rows_inverse(
        (
            lax.all_to_all(back_real, "rows", split_axis=0, concat_axis=2, tiled=True),
            lax.all_to_all(back_imag, "rows", split_axis=0, concat_axis=2, tiled=True),
        )
    )[0]
    residual = dirty - blurred
    return residual, values + step_size * residual


def joined_plain(halfway):
    height, length = halfway.shape
    depth = 14
    chan_count = lax.axis_size("chan")
    part = length // chan_count
    padded = with_halo(halfway, (("rows", 0),), depth)
    padded = jnp.pad(padded, ((0, 0), (depth, depth)))
    pieces = jnp.stack(
        [padded[:, q * part : (q + 1) * part + 2 * depth] for q in range(chan_count)]
    )
    current = lax.all_to_all(pieces, "chan", split_axis=0, concat_axis=0, tiled=True)
    row_ids = lax.axis_index("rows") * height - depth + lax.iota(jnp.int32, height + 2 * depth)
    col_ids = lax.axis_index("chan") * part - depth + lax.iota(jnp.int32, part + 2 * depth)
    margin = depth
    details = []
    for scale_level in range(3):
        reach = 2 << scale_level
        smoother = smooth_both(current, 1 << scale_level)
        row_ids = row_ids[reach:-reach]
        col_ids = col_ids[reach:-reach]
        inside = ((row_ids >= 0) & (row_ids < length))[:, None] & (
            (col_ids >= 0) & (col_ids < length)
        )[None, :]
        smoother = jnp.where(inside[None], smoother, 0.0)
        new_margin = margin - reach
        details.append(
            current[:, margin : margin + height, margin : margin + part]
            - smoother[:, new_margin : new_margin + height, new_margin : new_margin + part]
        )
        current = smoother
        margin = new_margin
    energies = [jnp.sum(detail * detail, axis=0) for detail in details]
    peaks = jnp.stack([jnp.broadcast_to(jnp.max(energy), (128,)) for energy in energies])
    for axis in ("rows", "chan"):
        peaks = lax.pmax(peaks, axis)
    output = current
    for scale_level in range(3):
        threshold = fractions[scale_level] * jnp.sqrt(peaks[scale_level, 0])
        factor = 1.0 - threshold / jnp.maximum(jnp.sqrt(energies[scale_level]), threshold)
        output = output + factor[None] * details[scale_level]
    output = lax.all_to_all(output, "chan", split_axis=0, concat_axis=2, tiled=True)[0]
    return output


def shards(estimate, dirty_image, psf_weights):
    values, dirty, weights = estimate[0], dirty_image[0], psf_weights[0]
    height, length = values.shape
    row_count, chan_count = lax.axis_size("rows"), lax.axis_size("chan")
    whole_tiles = length == 2 * row_count * lane_count and length % (chan_count * lane_count) == 0
    if whole_tiles and chan_count & (chan_count - 1) == 0:
        new_estimate, residual = filtered(values, dirty, weights)
    else:
        residual, halfway = filtered_plain(values, dirty, weights)
        new_estimate = joined_plain(halfway)
    return (new_estimate[None], residual[None])


def solution(mesh):
    return jax.shard_map(
        shards,
        mesh=mesh,
        in_specs=(P("chan", "rows", None), P("chan", "rows", None), P("chan", None, "rows")),
        out_specs=(P("chan", "rows", None), P("chan", "rows", None)),
        check_vma=False,
    )
```

```python
import functools
import math

import jax
import jax.numpy as jnp
import ml_dtypes
import numpy as np
from jax import lax
from jax.experimental import pallas as pl
from jax.experimental.pallas import tpu as pltpu
from jax.sharding import PartitionSpec as P

fractions = (0.03, 0.02, 0.015)
taps = (0.0625, 0.25, 0.375, 0.25, 0.0625)
step_size = 0.9
inner_length = 128
highest = lax.Precision.HIGHEST
lane_count = 128
mebibyte = 1024 * 1024
rim = 16
halo_rows = 16


def with_halo(cells, sides, width):
    for axis, dim in sides:
        count = lax.axis_size(axis)
        ends = count - 1
        head = lax.slice_in_dim(cells, 0, width, axis=dim)
        tail = lax.slice_in_dim(cells, cells.shape[dim] - width, cells.shape[dim], axis=dim)
        cells = jnp.concatenate(
            [
                lax.ppermute(tail, axis, [(i, (i + 1) % count) for i in range(ends)]),
                cells,
                lax.ppermute(head, axis, [((i + 1) % count, i) for i in range(ends)]),
            ],
            axis=dim,
        )
    return cells


def phase_table(first_count, second_count, length, sign):
    first_ids = lax.iota(jnp.int32, first_count)
    second_ids = lax.iota(jnp.int32, second_count)
    angles = (first_ids[:, None] * second_ids[None, :] % length).astype(jnp.float32) * (
        2.0 * math.pi / length
    )
    return (jnp.cos(angles), sign * jnp.sin(angles))


def dft_last(real_in, imag_in, sign):
    batch, length = real_in.shape
    outer = length // inner_length
    real_part = real_in.reshape(batch, outer, inner_length)
    imag_part = imag_in.reshape(batch, outer, inner_length)
    cos_small, sin_small = phase_table(outer, outer, outer, sign)
    first_real = jnp.einsum("kn,bnm->bkm", cos_small, real_part, precision=highest) - jnp.einsum(
        "kn,bnm->bkm", sin_small, imag_part, precision=highest
    )
    first_imag = jnp.einsum("kn,bnm->bkm", cos_small, imag_part, precision=highest) + jnp.einsum(
        "kn,bnm->bkm", sin_small, real_part, precision=highest
    )
    cos_twist, sin_twist = phase_table(outer, inner_length, length, sign)
    twist_real = first_real * cos_twist - first_imag * sin_twist
    twist_imag = first_imag * cos_twist + first_real * sin_twist
    cos_large, sin_large = phase_table(inner_length, inner_length, inner_length, sign)
    last_real = jnp.einsum("bkm,mj->bkj", twist_real, cos_large, precision=highest) - jnp.einsum(
        "bkm,mj->bkj", twist_imag, sin_large, precision=highest
    )
    last_imag = jnp.einsum("bkm,mj->bkj", twist_imag, cos_large, precision=highest) + jnp.einsum(
        "bkm,mj->bkj", twist_real, sin_large, precision=highest
    )
    return (
        jnp.transpose(last_real, (0, 2, 1)).reshape(batch, length),
        jnp.transpose(last_imag, (0, 2, 1)).reshape(batch, length),
    )


def dft_first(real_in, imag_in, sign):
    length, width = real_in.shape
    outer = length // inner_length
    real_part = real_in.reshape(outer, inner_length, width)
    imag_part = imag_in.reshape(outer, inner_length, width)
    cos_small, sin_small = phase_table(outer, outer, outer, sign)
    first_real = jnp.einsum("kn,nmw->kmw", cos_small, real_part, precision=highest) - jnp.einsum(
        "kn,nmw->kmw", sin_small, imag_part, precision=highest
    )
    first_imag = jnp.einsum("kn,nmw->kmw", cos_small, imag_part, precision=highest) + jnp.einsum(
        "kn,nmw->kmw", sin_small, real_part, precision=highest
    )
    cos_twist, sin_twist = phase_table(outer, inner_length, length, sign)
    cos_twist = cos_twist[:, :, None]
    sin_twist = sin_twist[:, :, None]
    twist_real = first_real * cos_twist - first_imag * sin_twist
    twist_imag = first_imag * cos_twist + first_real * sin_twist
    cos_large, sin_large = phase_table(inner_length, inner_length, inner_length, sign)
    last_real = jnp.einsum("kmw,mj->kjw", twist_real, cos_large, precision=highest) - jnp.einsum(
        "kmw,mj->kjw", twist_imag, sin_large, precision=highest
    )
    last_imag = jnp.einsum("kmw,mj->kjw", twist_imag, cos_large, precision=highest) + jnp.einsum(
        "kmw,mj->kjw", twist_real, sin_large, precision=highest
    )
    return (
        jnp.transpose(last_real, (1, 0, 2)).reshape(length, width),
        jnp.transpose(last_imag, (1, 0, 2)).reshape(length, width),
    )


def columns_forward(pieces):
    real_out, imag_out = dft_first(pieces[0][:, 0, :], pieces[1][:, 0, :], -1.0)
    return (real_out[:, None, :], imag_out[:, None, :])


def rows_inverse(pieces):
    real_in = pieces[0][0]
    imag_in = pieces[1][0]
    length = real_in.shape[1]
    real_out, imag_out = dft_last(real_in, imag_in, 1.0)
    return (real_out * (1.0 / (length * length)))[None]


def max_over(cells, axis, distances):
    count = lax.axis_size(axis)
    others = [
        lax.ppermute(cells, axis, [(i, i ^ distance) for i in range(count)])
        for distance in distances
    ]
    for other in others:
        cells = jnp.maximum(cells, other)
    return cells


def smooth_both(values, spacing):
    for dim in (2, 1):
        count = values.shape[dim] - 4 * spacing
        total = taps[0] * lax.slice_in_dim(values, 0, count, axis=dim)
        for tap_index in range(1, 5):
            start = tap_index * spacing
            total = total + taps[tap_index] * lax.slice_in_dim(
                values, start, start + count, axis=dim
            )
        values = total
    return values


def real_dft(parts):
    count = len(parts)
    if count == 1:
        return [(parts[0], None)]
    if count == 2:
        return [(parts[0] + parts[1], None), (parts[0] - parts[1], None)]
    even = real_dft(parts[0::2])
    odd = real_dft(parts[1::2])
    out = [None] * (count // 2 + 1)
    for k in range(count // 4 + 1):
        turned = spin(odd[k], -2.0 * math.pi * k / count)
        out[k] = pair_add(even[k], turned)
        low = pair_sub(even[k], turned)
        out[count // 2 - k] = (low[0], None if low[1] is None else -low[1])
    out[0] = (out[0][0], None)
    out[count // 2] = (out[count // 2][0], None)
    return out


def real_inverse_dft(pairs):
    count = 2 * (len(pairs) - 1)
    if count == 2:
        return [pairs[0][0] + pairs[1][0], pairs[0][0] - pairs[1][0]]
    even, odd = [], []
    for k in range(count // 4 + 1):
        low = pairs[k]
        high = pairs[count // 2 - k]
        high = (high[0], None if high[1] is None else -high[1])
        even.append(pair_add(low, high))
        odd.append(spin(pair_sub(low, high), 2.0 * math.pi * k / count))
    for half in (even, odd):
        half[0] = (half[0][0], None)
        half[-1] = (half[-1][0], None)
    even = real_inverse_dft(even)
    odd = real_inverse_dft(odd)
    return [cells for both in zip(even, odd) for cells in both]


def complex_dft(pairs, sign):
    count = len(pairs)
    if count == 1:
        return pairs
    even = complex_dft(pairs[0::2], sign)
    odd = complex_dft(pairs[1::2], sign)
    turned = [spin(odd[k], sign * 2.0 * math.pi * k / count) for k in range(count // 2)]
    return [pair_add(a, b) for a, b in zip(even, turned)] + [
        pair_sub(a, b) for a, b in zip(even, turned)
    ]


def pair_add(a, b):
    if a[1] is None or b[1] is None:
        return (a[0] + b[0], a[1] if b[1] is None else b[1])
    return (a[0] + b[0], a[1] + b[1])


def pair_sub(a, b):
    if b[1] is None:
        return (a[0] - b[0], a[1])
    return (a[0] - b[0], -b[1] if a[1] is None else a[1] - b[1])


def spin(pair, angle):
    quarter = angle / (0.5 * math.pi)
    turns = round(quarter)
    real, imag = pair
    if abs(quarter - turns) < 1e-9:
        turns %= 4
        if turns == 0:
            return pair
        if turns == 2:
            return (-real, None if imag is None else -imag)
        if imag is None:
            return (jnp.zeros_like(real), real if turns == 1 else -real)
        return (-imag, real) if turns == 1 else (imag, -real)
    cosine, sine = math.cos(angle), math.sin(angle)
    if imag is None:
        return (real * cosine, real * sine)
    if abs(abs(cosine) - abs(sine)) < 1e-9:
        a, b = math.copysign(1.0, cosine), math.copysign(1.0, sine)
        root = abs(cosine)
        first = real if a > 0 else -real
        second = imag if b > 0 else -imag
        third = real if b > 0 else -real
        fourth = imag if a > 0 else -imag
        return ((first - second) * root, (third + fourth) * root)
    return (real * cosine - imag * sine, real * sine + imag * cosine)


def split(cells):
    high = cells.astype(jnp.bfloat16)
    return high, (cells - high.astype(jnp.float32)).astype(jnp.bfloat16)


def dot(a, b):
    return jnp.dot(a, b, preferred_element_type=jnp.float32)


def split_table(table):
    high = table.astype(np.float32).astype(ml_dtypes.bfloat16)
    low = (table - high.astype(np.float64)).astype(np.float32).astype(ml_dtypes.bfloat16)
    return np.stack([high, low], axis=-3)


def group_columns(length, count, group):
    radix = 2 * count
    lanes = length // radix
    spots = np.arange(lanes)
    if group:
        return group + radix * spots
    half = lanes // 2
    return np.where(spots < half, radix * spots, count + radix * (spots - half))


def row_tables(length, count):
    radix = 2 * count
    lanes = length // radix
    half = lanes // 2
    spots = np.arange(lanes)
    there, back = [], []
    for group in range(2):
        columns = group_columns(length, count, 0) if group == 0 else radix * spots
        angles = 2.0 * np.pi * (np.outer(spots, columns) % length) / length
        cosine, sine = np.cos(angles), np.sin(angles)
        ahead = np.zeros((2, lanes, 2, lanes))
        behind = np.zeros((2, lanes, 2, lanes))
        if group:
            ahead[0, :, 0], ahead[0, :, 1] = cosine, -sine
            ahead[1, :, 0], ahead[1, :, 1] = sine, cosine
            behind[0, :, 0], behind[0, :, 1] = cosine.T, sine.T
            behind[1, :, 0], behind[1, :, 1] = -sine.T, cosine.T
        else:
            for part, where in enumerate((slice(0, half), slice(half, lanes))):
                ahead[part, :, 0, where] = cosine[:, where]
                ahead[part, :, 1, where] = -sine[:, where]
                behind[0, where, part] = 2.0 * cosine[:, where].T
                behind[1, where, part] = -2.0 * sine[:, where].T
            ahead[0, :, 1, 0] = (-1.0) ** spots
            behind[0, 0, 0] = 1.0
            behind[1, 0, 0] = (-1.0) ** spots
        there.append(ahead.reshape(2 * lanes, 2 * lanes))
        back.append(behind.reshape(2 * lanes, 2 * lanes) / float(length) ** 2)
    angles = 2.0 * np.pi * np.outer(np.arange(count), spots) / length
    turns = np.stack([np.cos(angles), np.sin(angles)]).astype(np.float32)
    return split_table(np.stack(there)), split_table(np.stack(back)), turns


def column_tables(length, count, steps):
    size = length // steps
    each = size // count
    quarter = each // 4
    order = np.r_[0:quarter, each - quarter : each, quarter : each - quarter]
    order = (np.arange(count)[:, None] * each + order[None]).reshape(-1)
    order = np.concatenate([order, size + order])
    spots = np.arange(size)
    angles = 2.0 * np.pi * (np.outer(spots, spots) % size) / size
    cosine, sine = np.cos(angles), np.sin(angles)
    there = np.block([[cosine, sine], [-sine, cosine]])
    turns = np.zeros((2, size, lane_count), np.float32)
    angles = 2.0 * np.pi * np.outer(spots, np.arange(steps)) / length
    turns[0, :, :steps], turns[1, :, :steps] = np.cos(angles), np.sin(angles)
    return split_table(there), split_table(there.T[order]), turns


def weight_tables(length, count, steps):
    width = length // count
    lanes = length // (2 * count)
    per_class = width // (2 * count)
    packs = lanes // (2 * per_class)
    radix = 2 * count

    def classes(group):
        return (group, radix - group) if group else (0, count)

    pick = np.zeros((width, count, 2, per_class))
    for group in range(count):
        for which, kind in enumerate(classes(group)):
            for q in range(per_class):
                pick[radix * q + kind, group, which, q] = 1.0
    place = np.zeros((2, count, lanes, packs * 2 + 1, lanes))

    def slot(group, column, pack):
        column %= length
        source, rest = divmod(column, width)
        which = classes(group).index(rest % radix)
        return source, pack * 2 * per_class + which * per_class + rest // radix

    for version, group in ((0, 0), (1, 1)):
        columns = group_columns(length, count, group)
        for pack in range(packs):
            for lane in range(lanes):
                column = int(columns[lane])
                mates = [(column, 0, 0.5), (-column, 1, 0.5)]
                if group == 0 and lane == 0:
                    mates = [(c, s, 0.25) for c in (0, length // 2) for s in (0, 1)]
                for mate, side, value in mates:
                    source, where = slot(group, mate, pack)
                    place[version, source, where, pack * 2 + side, lane] += value
            if group == 0:
                for mate, value in ((0, 0.25), (length // 2, -0.25)):
                    source, where = slot(group, mate, pack)
                    place[version, source, where, packs * 2, pack] += value
    flip = np.zeros((length // steps, length // steps))
    flip[np.arange(len(flip)), -np.arange(len(flip))] = 1.0
    as_half = lambda table: table.astype(np.float32).astype(ml_dtypes.bfloat16)
    return (
        as_half(pick.reshape(width, width)),
        as_half(place.reshape(2, count * lanes, (packs * 2 + 1) * lanes)),
        as_half(flip),
    )


def busy(microseconds):
    return pl.CostEstimate(
        flops=0, bytes_accessed=int(microseconds * 3.5e6), transcendentals=0
    )


def whole_call(body, out_shapes, scratch, name, microseconds):
    return pl.pallas_call(
        body,
        out_shape=out_shapes,
        scratch_shapes=scratch,
        compiler_params=pltpu.CompilerParams(vmem_limit_bytes=24 * mebibyte),
        name=name,
        cost_estimate=busy(microseconds),
    )


def spun(pairs, spin_ref, sign):
    out = [pairs[0]]
    for group in range(1, len(pairs)):
        real, imag = pairs[group]
        cosine = jnp.broadcast_to(spin_ref[0, pl.ds(group, 1), :], real.shape)
        sine = sign * jnp.broadcast_to(spin_ref[1, pl.ds(group, 1), :], real.shape)
        out.append((real * cosine - imag * sine, imag * cosine + real * sine))
    return out


def row_forward_body(steps, me_ref, x_ref, table_ref, spin_ref, *refs):
    out_refs, held = refs[:-1], refs[-1]
    groups = len(out_refs)
    _, height, lanes = out_refs[0].shape
    each = height // steps
    for start in range(0, height, 16):
        rows = pl.ds(start, 16)
        tiles = [x_ref[rows, pl.ds(lanes * t, lanes)] for t in range(2 * groups)]
        pairs = real_dft(tiles)
        pairs = [(pairs[0][0], pairs[groups][0])] + pairs[1:groups]
        pairs = spun(pairs, spin_ref, -1.0)
        for group in range(groups):
            high, low = split(jnp.concatenate(pairs[group], axis=1))
            held[0, group, rows, :] = high
            held[1, group, rows, :] = low
    for turn, out_ref in enumerate(out_refs):
        group = me_ref[0] ^ turn
        kind = jnp.minimum(group, 1)
        done = (
            dot(held[0, group], table_ref[kind, 0])
            + dot(held[1, group], table_ref[kind, 0])
            + dot(held[0, group], table_ref[kind, 1])
        )
        for start in range(0, height, 8):
            spread = pl.ds(start % steps * each + start // steps, 8, stride=each)
            out_ref[0, spread, :] = done[start : start + 8, :lanes]
            out_ref[1, spread, :] = done[start : start + 8, lanes:]


def row_inverse_body(steps, groups, me_ref, *refs):
    in_refs = refs[:groups]
    table_ref, spin_ref, est_ref, dirty_ref, _, res_ref, half_ref, held = refs[groups:]
    _, chunk, lanes = in_refs[0].shape
    parts, _, wide = half_ref.shape
    each = chunk // steps
    block = est_ref.shape[0]
    turn = pl.program_id(0)

    @pl.when(turn == 0)
    def _():
        for partner, in_ref in enumerate(in_refs):
            group = me_ref[0] ^ partner
            kind = jnp.minimum(group, 1)
            halves = []
            for part in range(2):
                pieces = [
                    in_ref[part, pl.ds(start % steps * each + start // steps, 8, stride=each), :]
                    for start in range(0, chunk, 8)
                ]
                halves.append(jnp.concatenate(pieces, axis=0))
            high, low = split(jnp.concatenate(halves, axis=1))
            held[group] = (
                dot(high, table_ref[kind, 0])
                + dot(low, table_ref[kind, 0])
                + dot(high, table_ref[kind, 1])
            )

    per = wide // lanes
    lane_ids = lax.broadcasted_iota(jnp.int32, (8, lanes), 1)
    sides = [None] * parts
    for start in range(0, block, 8):
        rows = pl.ds(start, 8)
        chunk_rows = pl.ds(pl.multiple_of(turn * block + start, 8), 8)
        pairs = [
            (held[group, chunk_rows, pl.ds(0, lanes)], held[group, chunk_rows, pl.ds(lanes, lanes)])
            for group in range(groups)
        ]
        pairs = spun(pairs, spin_ref, 1.0)
        pairs = [(pairs[0][0], None)] + pairs[1:] + [(pairs[0][1], None)]
        tiles = real_inverse_dft(pairs)
        for t in range(2 * groups):
            where = pl.ds(lanes * t, lanes)
            residual = dirty_ref[rows, where] - tiles[t]
            res_ref[rows, where] = residual
            tiles[t] = est_ref[rows, where] + step_size * residual
            half_ref[t // per, chunk_rows, pl.ds(lanes * (t % per), lanes)] = tiles[t]
        offset = start // 8 * 2 * rim % lanes
        for part in range(parts):
            done = jnp.zeros_like(tiles[0]) if offset == 0 else sides[part]
            if part > 0:
                turned = pltpu.roll(tiles[part * per - 1], (offset + rim) % lanes, 1)
                done = jnp.where((lane_ids >= offset) & (lane_ids < offset + rim), turned, done)
            if part < parts - 1:
                turned = pltpu.roll(tiles[(part + 1) * per], (offset + rim) % lanes, 1)
                done = jnp.where(
                    (lane_ids >= offset + rim) & (lane_ids < offset + 2 * rim), turned, done
                )
            sides[part] = done
            if offset + 2 * rim == lanes:
                spot = turn * (block // 8 * 2 * rim // lanes) + start // 8 * 2 * rim // lanes
                where = pl.ds(pl.multiple_of(spot * lanes, lanes), lanes)
                half_ref[part, pl.ds(chunk, 8), where] = done


def starlet_body(chans, spans, fills, ends_ref, before_ref, *refs):
    sources, (detail_ref, peak_ref, ping, pong) = refs[:-4], refs[-4:]
    part = detail_ref.shape[3]
    lanes = lane_count
    tiles = part // lanes
    total = part + lanes
    no_left, no_right = ends_ref[0] > 0, ends_ref[1] > 0
    no_top, no_bottom = ends_ref[2] > 0, ends_ref[3] > 0
    lane_ids = lax.broadcasted_iota(jnp.int32, (8, lanes), 1)
    outside = ((lane_ids >= lanes // 2) & no_left) | ((lane_ids < lanes // 2) & no_right)
    for chan in range(chans):
        for target, index, source_row, count, pack_row, group in fills:
            source = sources[index * chans + chan]
            to = pl.ds(8 + target, count)
            ping[chan, to, pl.ds(0, part)] = source[pl.ds(source_row, count), :]
            for i in range(count // 8):
                spot = (group + i) * 2 * rim
                tile = source[pl.ds(pack_row, 8), pl.ds(spot // lanes * lanes, lanes)]
                shift = (lanes - spot % lanes - rim) % lanes
                to = pl.ds(8 + target + 8 * i, 8)
                ping[chan, to, pl.ds(part, lanes)] = pltpu.roll(tile, shift, 1)

    skirt = halo_rows // 8
    peaks = [jnp.zeros((8, part), jnp.float32)] * 3
    for start, blocks, out_start, top, bottom in spans:
        for level in range(3):
            gap = 1 << level
            before, after = (ping, pong) if level % 2 == 0 else (pong, ping)

            def step(i, peak, level, gap, before, after):
                base = 8 + start + 8 * i
                if not isinstance(i, int):
                    base = pl.multiple_of(base, 8)
                inner = not isinstance(i, int)
                energy = 0.0
                for chan in range(chans):
                    window = before[chan, pl.ds(base - 8, 24), :]
                    near = window[8 - gap : 16 - gap] + window[8 + gap : 16 + gap]
                    far = window[8 - 2 * gap : 16 - 2 * gap] + window[8 + 2 * gap : 16 + 2 * gap]
                    row = (far + 4.0 * near) + 6.0 * window[8:16]
                    near = pltpu.roll(row, gap, 1) + pltpu.roll(row, total - gap, 1)
                    far = pltpu.roll(row, 2 * gap, 1) + pltpu.roll(row, total - 2 * gap, 1)
                    smooth = ((far + 4.0 * near) + 6.0 * row) * (1.0 / 256.0)
                    whole = smooth[:, :part]
                    if level < 2:
                        side = jnp.where(outside, 0.0, smooth[:, part:])
                        if not inner and (top if i < skirt else bottom):
                            gone = no_top if i < skirt else no_bottom
                            side = jnp.where(gone, 0.0, side)
                            after[chan, pl.ds(base, 8), pl.ds(0, part)] = jnp.where(
                                gone, 0.0, whole
                            )
                        else:
                            after[chan, pl.ds(base, 8), pl.ds(0, part)] = whole
                        after[chan, pl.ds(base, 8), pl.ds(part, lanes)] = side
                    if inner:
                        to = pl.ds(pl.multiple_of(out_start + 8 * i - halo_rows, 8), 8)
                        detail = window[8:16, :part] - whole
                        detail_ref[chan, level, to, :] = detail
                        if level == 2:
                            detail_ref[chan, 3, to, :] = whole
                        energy = energy + detail * detail
                return jnp.maximum(peak, energy) if inner else peak

            step = functools.partial(step, level=level, gap=gap, before=before, after=after)
            for i in range(level, skirt):
                step(i, None)
                step(blocks - 1 - i, None)
            peaks[level] = lax.fori_loop(
                skirt, blocks - skirt, step, peaks[level], unroll=(blocks - 2 * skirt) // 2
            )
    for level in range(3):
        most = before_ref[level]
        for t in range(tiles):
            most = jnp.maximum(most, peaks[level][:, t * lanes : (t + 1) * lanes])
        peak_ref[level] = most


def shrink_body(chans, detail_ref, peak_ref, *out_refs):
    factors = []
    for level in range(3):
        energy = 0.0
        for chan in range(chans):
            detail = detail_ref[chan, level]
            energy = energy + detail * detail
        energy = jnp.sqrt(energy)
        threshold = fractions[level] * jnp.sqrt(jnp.max(peak_ref[level], keepdims=True))
        threshold = jnp.broadcast_to(threshold, energy.shape)
        factors.append(1.0 - threshold / jnp.maximum(energy, threshold))
    for chan in range(chans):
        total = detail_ref[chan, 3]
        for level in range(3):
            total = total + factors[level] * detail_ref[chan, level]
        out_refs[chan][...] = total


def join_body(me_ref, *refs):
    chans = (len(refs) - 1) // 2
    out_ref = refs[-1]
    part = refs[0].shape[1]
    outer_rows, inner_rows = refs[0].shape[0] // 2, refs[chans].shape[0]
    for chan in range(chans):
        outer, inner = refs[chan], refs[chans + chan]
        columns = pl.ds(pl.multiple_of((me_ref[0] ^ chan) * part, part), part)
        out_ref[pl.ds(0, outer_rows), columns] = outer[pl.ds(0, outer_rows), :]
        out_ref[pl.ds(outer_rows, inner_rows), columns] = inner[...]
        out_ref[pl.ds(outer_rows + inner_rows, outer_rows), columns] = outer[
            pl.ds(outer_rows, outer_rows), :
        ]


def facing(blocks, step):
    rows = lax.broadcasted_iota(jnp.int32, blocks[0].shape, 0)
    return jnp.where(rows == 0, blocks[-step % len(blocks)], blocks[len(blocks) - 1 - step])


def column_body(steps, count, me_ref, *refs):
    in_refs = refs[:count]
    there_ref, back_ref, turn_ref, weight_ref, mirror_ref, flip_ref = refs[count : count + 6]
    out_refs, (gathered, held, made, ready) = refs[count + 6 : 3 * count + 6], refs[3 * count + 6 :]
    _, height, lanes = in_refs[0].shape
    each = height // steps
    size = each * count
    for turn, in_ref in enumerate(in_refs):
        source = me_ref[0] ^ turn
        for part in range(2):
            to = pl.ds(pl.multiple_of(part * size + source * each, 8), each)
            for step in range(steps):
                gathered[to, pl.ds(step * lanes, lanes)] = in_ref[part, pl.ds(step * each, each), :]
    for step in range(0, steps, 2):
        high, low = split(gathered[:, pl.ds(step * lanes, 2 * lanes)])
        done = dot(there_ref[0], high) + dot(there_ref[1], high) + dot(there_ref[0], low)
        for k in range(2):
            held[0, step + k] = done[:size, k * lanes : (k + 1) * lanes]
            held[1, step + k] = done[size:, k * lanes : (k + 1) * lanes]

    def turned(pairs, rows, sign):
        cosines, sines = turn_ref[0, rows, :], turn_ref[1, rows, :]
        out = [pairs[0]]
        for step in range(1, steps):
            real, imag = pairs[step]
            cosine = jnp.broadcast_to(cosines[:, step : step + 1], real.shape)
            sine = sign * jnp.broadcast_to(sines[:, step : step + 1], real.shape)
            out.append((real * cosine - imag * sine, imag * cosine + real * sine))
        return out

    def forward(chunk, carry):
        rows = pl.ds(pl.multiple_of(chunk * 8, 8), 8)
        pairs = [(held[0, step, rows, :], held[1, step, rows, :]) for step in range(steps)]
        for step, pair in enumerate(complex_dft(turned(pairs, rows, -1.0), -1.0)):
            held[0, step, rows, :] = pair[0]
            held[1, step, rows, :] = pair[1]
        return carry

    lax.fori_loop(0, size // 8, forward, 0, unroll=4)
    lane_ids = lax.broadcasted_iota(jnp.int32, (size, lanes), 1)
    lone = jnp.zeros((size, lanes), jnp.float32)
    for step in range(steps):
        for part in range(2):
            spot = 2 * step + part
            moved = facing([held[part, other] for other in range(steps)], step)
            if spot:
                moved = pltpu.roll(moved, spot, 1)
            lone = jnp.where(lane_ids == spot, moved, lone)
    high, low = split(lone)
    lone = (dot(flip_ref[...], high) + dot(flip_ref[...], low)) * mirror_ref[...]
    for step in range(steps):
        weight = weight_ref[step]
        for part in range(2):
            spot = 2 * step + part
            moved = pltpu.roll(lone, lanes - spot, 1) if spot else lone
            made[part, step] = weight * held[part, step] + jnp.where(lane_ids == 0, moved, 0.0)

    def backward(chunk, carry):
        rows = pl.ds(pl.multiple_of(chunk * 8, 8), 8)
        pairs = [(made[0, step, rows, :], made[1, step, rows, :]) for step in range(steps)]
        for step, pair in enumerate(turned(complex_dft(pairs, 1.0), rows, 1.0)):
            made[0, step, rows, :] = pair[0]
            made[1, step, rows, :] = pair[1]
        return carry

    lax.fori_loop(0, size // 8, backward, 0, unroll=4)
    half = each // 2
    for step in range(0, steps, 2):
        block = [
            jnp.concatenate([made[part, step + k] for k in range(2)], axis=1) for part in range(2)
        ]
        high, low = split(jnp.concatenate(block, axis=0))
        done = dot(back_ref[0], high) + dot(back_ref[1], high) + dot(back_ref[0], low)
        for k in range(2):
            ready[step + k] = done[:, k * lanes : (k + 1) * lanes]
    for turn in range(count):
        target = me_ref[0] ^ turn
        for part in range(2):
            for inner in range(2):
                start = pl.multiple_of(part * size + target * each + inner * half, 8)
                for step in range(steps):
                    rows = pl.ds(step * half, half)
                    out_refs[inner * count + turn][part, rows, :] = ready[step, pl.ds(start, half), :]


def weight_pick_body(w_ref, pick_ref, out_ref):
    count, thick, lanes = out_ref.shape
    packs, _, width = w_ref.shape
    piece = lanes // packs
    chosen = []
    for pack in range(packs):
        high, low = split(w_ref[pack])
        chosen.append(dot(high, pick_ref[...]) + dot(low, pick_ref[...]))
    lane_ids = lax.broadcasted_iota(jnp.int32, (thick, lanes), 1)
    for target in range(count):
        start = target * piece // lanes * lanes
        total = None
        for pack in range(packs):
            moved = chosen[pack][:, start : start + lanes]
            shift = (pack - target) % packs * piece
            if shift:
                moved = pltpu.roll(moved, shift, 1)
            total = moved if pack == 0 else jnp.where(lane_ids >= pack * piece, moved, total)
        out_ref[target] = total


def weight_place_body(in_ref, place_ref, flip_ref, weight_ref, mirror_ref):
    count, depth, lanes = in_ref.shape
    steps, size, _ = weight_ref.shape
    packs = steps * size // depth
    inner = depth // size
    total = 0.0
    for source in range(count):
        high, low = split(in_ref[source])
        chosen = place_ref[pl.ds(source * lanes, lanes), :]
        total = total + dot(high, chosen) + dot(low, chosen)

    def block(step, side):
        pack, rest = divmod(step, inner)
        start = (2 * pack + side) * lanes if side < 2 else 2 * packs * lanes
        return total[rest * size : (rest + 1) * size, start : start + lanes]

    def flipped(cells):
        high, low = split(cells)
        return dot(flip_ref[...], high) + dot(flip_ref[...], low)

    lane_ids = lax.broadcasted_iota(jnp.int32, (size, lanes), 1)
    extra = [block(step, 2) for step in range(steps)]
    extra = [
        pltpu.roll(cells, lanes - step // inner, 1) if step // inner else cells
        for step, cells in enumerate(extra)
    ]
    straight = jnp.zeros((size, lanes), jnp.float32)
    opposite = straight
    for step in range(steps):
        against = facing(extra, step)
        for part in range(2):
            spot = 2 * step + part
            sign = 1.0 - 2.0 * part
            straight = jnp.where(lane_ids == spot, sign * roll_to(extra[step], spot), straight)
            opposite = jnp.where(lane_ids == spot, sign * roll_to(against, spot), opposite)
    mirror_ref[...] = straight + flipped(opposite)
    backs = [block(step, 1) for step in range(steps)]
    for step in range(0, steps, 2):
        both = jnp.concatenate([facing(backs, step), facing(backs, step + 1)], axis=1)
        both = flipped(both)
        weight_ref[step] = block(step, 0) + both[:, :lanes]
        weight_ref[step + 1] = block(step + 1, 0) + both[:, lanes:]


def roll_to(cells, spot):
    return pltpu.roll(cells, spot, 1) if spot else cells


def filtered(values, dirty, weights):
    height, length = values.shape
    count = lax.axis_size("rows")
    lanes = length // (2 * count)
    steps = height // 16
    size = length // steps
    width = weights.shape[1]
    f32 = jnp.float32
    pick, place, flip = [jnp.asarray(table) for table in weight_tables(length, count, steps)]
    there, back, spins = [jnp.asarray(table) for table in row_tables(length, count)]
    down, up, turns = [jnp.asarray(table) for table in column_tables(length, count, steps)]
    shape = lambda *dims: jax.ShapeDtypeStruct(dims, f32)
    packs = lanes * count // width
    depth = length // packs
    half = height // 2
    vmem = pl.BlockSpec(memory_space=pltpu.VMEM)
    smem = pl.BlockSpec(memory_space=pltpu.SMEM)
    me = jnp.reshape(lax.axis_index("rows"), (1,)).astype(jnp.int32)

    thick = depth // 2
    sent = pl.pallas_call(
        weight_pick_body,
        grid=(2,),
        in_specs=[
            pl.BlockSpec((packs, thick, width), lambda i: (0, i, 0)),
            pl.BlockSpec((width, width), lambda i: (0, 0)),
        ],
        out_specs=pl.BlockSpec((count, thick, lanes), lambda i: (0, i, 0)),
        out_shape=shape(count, depth, lanes),
        compiler_params=pltpu.CompilerParams(vmem_limit_bytes=56 * mebibyte),
        name="weight_pick",
        cost_estimate=busy(4),
    )(weights.reshape(packs, depth, width), pick)
    sent = lax.all_to_all(sent, "rows", 0, 0, tiled=True)
    ahead = pl.pallas_call(
        functools.partial(row_forward_body, steps),
        in_specs=[smem, vmem, vmem, vmem],
        out_specs=[vmem] * count,
        out_shape=[shape(2, height, lanes)] * count,
        scratch_shapes=[pltpu.VMEM((2, count, height, 2 * lanes), jnp.bfloat16)],
        compiler_params=pltpu.CompilerParams(vmem_limit_bytes=56 * mebibyte),
        name="row_forward",
        cost_estimate=busy(6),
    )(me, values, there, spins)

    def over_rows(pieces):
        return [pieces[0]] + [
            lax.ppermute(pieces[turn], "rows", [(i, i ^ turn) for i in range(count)])
            for turn in range(1, count)
        ]

    ahead = over_rows(ahead)
    mine = jnp.where(lax.axis_index("rows") == 0, place[0], place[1])
    weight, mirror = whole_call(
        weight_place_body,
        [shape(steps, size, lanes), shape(size, lanes)],
        [],
        "weight_place",
        10,
    )(sent, mine, flip)
    behind = pl.pallas_call(
        functools.partial(column_body, steps, count),
        in_specs=[smem] + [vmem] * (count + 6),
        out_specs=[vmem] * (2 * count),
        out_shape=[shape(2, half, lanes)] * (2 * count),
        scratch_shapes=[
            pltpu.VMEM((2 * size, steps * lanes), f32),
            pltpu.VMEM((2, steps, size, lanes), f32),
            pltpu.VMEM((2, steps, size, lanes), f32),
            pltpu.VMEM((steps, 2 * size, lanes), f32),
        ],
        compiler_params=pltpu.CompilerParams(vmem_limit_bytes=24 * mebibyte),
        name="column_filter",
        cost_estimate=busy(10),
    )(me, *ahead, down, up, turns, weight, mirror, flip)
    edge, core = over_rows(behind[:count]), behind[count:]
    core = over_rows(core)
    chans = lax.axis_size("chan")
    part = length // chans
    quarter = height // 4

    def row_inverse(cells, old, blocks):
        rows_spec = pl.BlockSpec((quarter, length), lambda i: (blocks[0] + i * blocks[1], 0))
        whole = lambda *dims: pl.BlockSpec(dims, lambda i: (0,) * len(dims))
        return pl.pallas_call(
            functools.partial(row_inverse_body, steps, count),
            grid=(2,),
            in_specs=[smem]
            + [whole(2, half, lanes)] * count
            + [
                whole(*back.shape),
                whole(*spins.shape),
                rows_spec,
                rows_spec,
                pl.BlockSpec(memory_space=pl.ANY),
            ],
            out_specs=[rows_spec, whole(chans, half + 8, part)],
            out_shape=[shape(height, length), shape(chans, half + 8, part)],
            scratch_shapes=[pltpu.VMEM((count, half, 2 * lanes), f32)],
            input_output_aliases={count + 5: 0} if old is not dirty else {},
            compiler_params=pltpu.CompilerParams(vmem_limit_bytes=56 * mebibyte),
            name="row_inverse",
        cost_estimate=busy(5),
        )(me, *cells, back, spins, values, dirty, old)

    def pieces_for(cells):
        me = lax.axis_index("chan")
        return [
            lax.dynamic_index_in_dim(cells, me ^ turn, 0, keepdims=False) for turn in range(chans)
        ]

    def over_chans(pieces):
        return [pieces[0]] + [
            lax.ppermute(pieces[turn], "chan", [(i, i ^ turn) for i in range(chans)])
            for turn in range(1, chans)
        ]

    def in_order(earlier, later):
        both = lax.optimization_barrier((*earlier, *later))
        return list(both[: len(earlier)]), list(both[len(earlier) :])

    residual, outer = row_inverse(edge, dirty, (0, 3))
    outer = over_chans(pieces_for(outer))
    residual, inner = row_inverse(core, residual, (1, 1))
    inner = over_chans(pieces_for(inner))
    outer, (inner[1],) = in_order(outer, [inner[1]])
    ahead_pairs = [(i, i + 1) for i in range(count - 1)]
    back_pairs = [(i + 1, i) for i in range(count - 1)]
    last = jnp.stack([cells[half - halo_rows :] for cells in outer])
    first = jnp.stack(
        [jnp.concatenate([cells[:halo_rows], cells[half:]], axis=0) for cells in outer]
    )
    last = lax.ppermute(last, "rows", ahead_pairs)
    first = lax.ppermute(first, "rows", back_pairs)
    above = [last[c] for c in range(chans)]
    below = [first[c] for c in range(chans)]
    chan_id, row_id = lax.axis_index("chan"), lax.axis_index("rows")
    at_end = jnp.stack(
        [chan_id == 0, chan_id == chans - 1, row_id == 0, row_id == count - 1]
    ).astype(jnp.int32)

    def starlet(sources, before, rows, spans, fills, microseconds):
        extent = max(fill[0] + fill[3] for fill in fills) + 16
        cells = pltpu.VMEM((chans, extent, part + lanes), f32)
        return pl.pallas_call(
            functools.partial(starlet_body, chans, spans, fills),
            in_specs=[smem] + [vmem] * (1 + len(sources)),
            out_specs=[vmem] * 2,
            out_shape=[shape(chans, 4, rows, part), shape(3, 8, lanes)],
            scratch_shapes=[cells, cells],
            compiler_params=pltpu.CompilerParams(vmem_limit_bytes=20 * mebibyte),
            name="starlet",
            cost_estimate=busy(microseconds),
        )(at_end, before, *sources)

    reach = quarter + halo_rows
    most = quarter - halo_rows
    skirt = halo_rows // 8
    outer_details, outer_peaks = starlet(
        outer + above + below,
        jnp.zeros((3, 8, lanes), f32),
        2 * most,
        (
            (0, reach // 8, 0, True, False),
            (reach + 16, reach // 8, most, False, True),
        ),
        (
            (0, 1, 0, halo_rows, halo_rows, (half - halo_rows) // 8),
            (halo_rows, 0, 0, quarter, half, 0),
            (reach + 16, 0, quarter, quarter, half, quarter // 8),
            (reach + 16 + quarter, 2, 0, halo_rows, halo_rows, 0),
        ),
        12,
    )
    inner_details, peaks = starlet(
        outer + inner,
        outer_peaks,
        half + 2 * halo_rows,
        ((0, half // 8 + 4 * skirt, 0, False, False),),
        (
            (0, 0, quarter - 2 * halo_rows, 2 * halo_rows, half, (quarter - 2 * halo_rows) // 8),
            (2 * halo_rows, 1, 0, half, half, 0),
            (2 * halo_rows + half, 0, quarter, 2 * halo_rows, half, quarter // 8),
        ),
        12,
    )
    peaks = max_over(peaks, "rows", range(1, 2))
    peaks = max_over(peaks, "rows", range(2, count, 2))
    peaks = max_over(peaks, "chan", range(1, chans))

    def shrink(details):
        rows = details.shape[2]
        thick = rows // 2
        return pl.pallas_call(
            functools.partial(shrink_body, chans),
            grid=(2,),
            in_specs=[
                pl.BlockSpec((chans, 4, thick, part), lambda i: (0, 0, i, 0)),
                pl.BlockSpec((3, 8, lanes), lambda i: (0, 0, 0)),
            ],
            out_specs=[pl.BlockSpec((thick, part), lambda i: (i, 0))] * chans,
            out_shape=[shape(rows, part)] * chans,
            compiler_params=pltpu.CompilerParams(vmem_limit_bytes=14 * mebibyte),
            name="shrink",
            cost_estimate=busy(3),
        )(details, peaks)

    outer = over_chans(shrink(outer_details))
    outer, inner = in_order(outer, shrink(inner_details))
    inner = over_chans(inner)
    new_estimate = pl.pallas_call(
        join_body,
        in_specs=[pl.BlockSpec(memory_space=pltpu.SMEM)] + [vmem] * (2 * chans),
        out_specs=vmem,
        out_shape=shape(height, length),
        compiler_params=pltpu.CompilerParams(vmem_limit_bytes=12 * mebibyte),
        name="join",
        cost_estimate=busy(4),
    )(jnp.reshape(chan_id, (1,)).astype(jnp.int32), *outer, *inner)
    return new_estimate, residual


def filtered_plain(values, dirty, weights):
    height, length = values.shape
    row_count = lax.axis_size("rows")
    narrow = length // row_count
    spec_real, spec_imag = dft_last(values, jnp.zeros_like(values), -1.0)
    spec_real = spec_real.reshape(height, row_count, narrow)
    spec_imag = spec_imag.reshape(height, row_count, narrow)
    col_real, col_imag = columns_forward(
        (
            lax.all_to_all(spec_real, "rows", split_axis=1, concat_axis=0, tiled=True),
            lax.all_to_all(spec_imag, "rows", split_axis=1, concat_axis=0, tiled=True),
        )
    )
    prod_real = weights * col_real[:, 0, :]
    prod_imag = weights * col_imag[:, 0, :]
    back_real, back_imag = dft_first(prod_real, prod_imag, 1.0)
    back_real = back_real.reshape(row_count, height, narrow)
    back_imag = back_imag.reshape(row_count, height, narrow)
    blurred = rows_inverse(
        (
            lax.all_to_all(back_real, "rows", split_axis=0, concat_axis=2, tiled=True),
            lax.all_to_all(back_imag, "rows", split_axis=0, concat_axis=2, tiled=True),
        )
    )[0]
    residual = dirty - blurred
    return residual, values + step_size * residual


def joined_plain(halfway):
    height, length = halfway.shape
    depth = 14
    chan_count = lax.axis_size("chan")
    part = length // chan_count
    padded = with_halo(halfway, (("rows", 0),), depth)
    padded = jnp.pad(padded, ((0, 0), (depth, depth)))
    pieces = jnp.stack(
        [padded[:, q * part : (q + 1) * part + 2 * depth] for q in range(chan_count)]
    )
    current = lax.all_to_all(pieces, "chan", split_axis=0, concat_axis=0, tiled=True)
    row_ids = lax.axis_index("rows") * height - depth + lax.iota(jnp.int32, height + 2 * depth)
    col_ids = lax.axis_index("chan") * part - depth + lax.iota(jnp.int32, part + 2 * depth)
    margin = depth
    details = []
    for scale_level in range(3):
        reach = 2 << scale_level
        smoother = smooth_both(current, 1 << scale_level)
        row_ids = row_ids[reach:-reach]
        col_ids = col_ids[reach:-reach]
        inside = ((row_ids >= 0) & (row_ids < length))[:, None] & (
            (col_ids >= 0) & (col_ids < length)
        )[None, :]
        smoother = jnp.where(inside[None], smoother, 0.0)
        new_margin = margin - reach
        details.append(
            current[:, margin : margin + height, margin : margin + part]
            - smoother[:, new_margin : new_margin + height, new_margin : new_margin + part]
        )
        current = smoother
        margin = new_margin
    energies = [jnp.sum(detail * detail, axis=0) for detail in details]
    peaks = jnp.stack([jnp.broadcast_to(jnp.max(energy), (128,)) for energy in energies])
    for axis in ("rows", "chan"):
        peaks = lax.pmax(peaks, axis)
    output = current
    for scale_level in range(3):
        threshold = fractions[scale_level] * jnp.sqrt(peaks[scale_level, 0])
        factor = 1.0 - threshold / jnp.maximum(jnp.sqrt(energies[scale_level]), threshold)
        output = output + factor[None] * details[scale_level]
    output = lax.all_to_all(output, "chan", split_axis=0, concat_axis=2, tiled=True)[0]
    return output


def shards(estimate, dirty_image, psf_weights):
    values, dirty, weights = estimate[0], dirty_image[0], psf_weights[0]
    height, length = values.shape
    row_count, chan_count = lax.axis_size("rows"), lax.axis_size("chan")
    whole_tiles = length == 2 * row_count * lane_count and length % (chan_count * lane_count) == 0
    if whole_tiles and chan_count & (chan_count - 1) == 0:
        new_estimate, residual = filtered(values, dirty, weights)
    else:
        residual, halfway = filtered_plain(values, dirty, weights)
        new_estimate = joined_plain(halfway)
    return (new_estimate[None], residual[None])


def solution(mesh):
    return jax.shard_map(
        shards,
        mesh=mesh,
        in_specs=(P("chan", "rows", None), P("chan", "rows", None), P("chan", None, "rows")),
        out_specs=(P("chan", "rows", None), P("chan", "rows", None)),
        check_vma=False,
    )
```

```python
import functools
import math

import jax
import jax.numpy as jnp
import ml_dtypes
import numpy as np
from jax import lax
from jax.experimental import pallas as pl
from jax.experimental.pallas import tpu as pltpu
from jax.sharding import PartitionSpec as P

fractions = (0.03, 0.02, 0.015)
taps = (0.0625, 0.25, 0.375, 0.25, 0.0625)
step_size = 0.9
inner_length = 128
highest = lax.Precision.HIGHEST
lane_count = 128
mebibyte = 1024 * 1024
rim = 16
halo_rows = 16


def with_halo(cells, sides, width):
    for axis, dim in sides:
        count = lax.axis_size(axis)
        ends = count - 1
        head = lax.slice_in_dim(cells, 0, width, axis=dim)
        tail = lax.slice_in_dim(cells, cells.shape[dim] - width, cells.shape[dim], axis=dim)
        cells = jnp.concatenate(
            [
                lax.ppermute(tail, axis, [(i, (i + 1) % count) for i in range(ends)]),
                cells,
                lax.ppermute(head, axis, [((i + 1) % count, i) for i in range(ends)]),
            ],
            axis=dim,
        )
    return cells


def phase_table(first_count, second_count, length, sign):
    first_ids = lax.iota(jnp.int32, first_count)
    second_ids = lax.iota(jnp.int32, second_count)
    angles = (first_ids[:, None] * second_ids[None, :] % length).astype(jnp.float32) * (
        2.0 * math.pi / length
    )
    return (jnp.cos(angles), sign * jnp.sin(angles))


def dft_last(real_in, imag_in, sign):
    batch, length = real_in.shape
    outer = length // inner_length
    real_part = real_in.reshape(batch, outer, inner_length)
    imag_part = imag_in.reshape(batch, outer, inner_length)
    cos_small, sin_small = phase_table(outer, outer, outer, sign)
    first_real = jnp.einsum("kn,bnm->bkm", cos_small, real_part, precision=highest) - jnp.einsum(
        "kn,bnm->bkm", sin_small, imag_part, precision=highest
    )
    first_imag = jnp.einsum("kn,bnm->bkm", cos_small, imag_part, precision=highest) + jnp.einsum(
        "kn,bnm->bkm", sin_small, real_part, precision=highest
    )
    cos_twist, sin_twist = phase_table(outer, inner_length, length, sign)
    twist_real = first_real * cos_twist - first_imag * sin_twist
    twist_imag = first_imag * cos_twist + first_real * sin_twist
    cos_large, sin_large = phase_table(inner_length, inner_length, inner_length, sign)
    last_real = jnp.einsum("bkm,mj->bkj", twist_real, cos_large, precision=highest) - jnp.einsum(
        "bkm,mj->bkj", twist_imag, sin_large, precision=highest
    )
    last_imag = jnp.einsum("bkm,mj->bkj", twist_imag, cos_large, precision=highest) + jnp.einsum(
        "bkm,mj->bkj", twist_real, sin_large, precision=highest
    )
    return (
        jnp.transpose(last_real, (0, 2, 1)).reshape(batch, length),
        jnp.transpose(last_imag, (0, 2, 1)).reshape(batch, length),
    )


def dft_first(real_in, imag_in, sign):
    length, width = real_in.shape
    outer = length // inner_length
    real_part = real_in.reshape(outer, inner_length, width)
    imag_part = imag_in.reshape(outer, inner_length, width)
    cos_small, sin_small = phase_table(outer, outer, outer, sign)
    first_real = jnp.einsum("kn,nmw->kmw", cos_small, real_part, precision=highest) - jnp.einsum(
        "kn,nmw->kmw", sin_small, imag_part, precision=highest
    )
    first_imag = jnp.einsum("kn,nmw->kmw", cos_small, imag_part, precision=highest) + jnp.einsum(
        "kn,nmw->kmw", sin_small, real_part, precision=highest
    )
    cos_twist, sin_twist = phase_table(outer, inner_length, length, sign)
    cos_twist = cos_twist[:, :, None]
    sin_twist = sin_twist[:, :, None]
    twist_real = first_real * cos_twist - first_imag * sin_twist
    twist_imag = first_imag * cos_twist + first_real * sin_twist
    cos_large, sin_large = phase_table(inner_length, inner_length, inner_length, sign)
    last_real = jnp.einsum("kmw,mj->kjw", twist_real, cos_large, precision=highest) - jnp.einsum(
        "kmw,mj->kjw", twist_imag, sin_large, precision=highest
    )
    last_imag = jnp.einsum("kmw,mj->kjw", twist_imag, cos_large, precision=highest) + jnp.einsum(
        "kmw,mj->kjw", twist_real, sin_large, precision=highest
    )
    return (
        jnp.transpose(last_real, (1, 0, 2)).reshape(length, width),
        jnp.transpose(last_imag, (1, 0, 2)).reshape(length, width),
    )


def columns_forward(pieces):
    real_out, imag_out = dft_first(pieces[0][:, 0, :], pieces[1][:, 0, :], -1.0)
    return (real_out[:, None, :], imag_out[:, None, :])


def rows_inverse(pieces):
    real_in = pieces[0][0]
    imag_in = pieces[1][0]
    length = real_in.shape[1]
    real_out, imag_out = dft_last(real_in, imag_in, 1.0)
    return (real_out * (1.0 / (length * length)))[None]


def max_over(cells, axis, distances):
    count = lax.axis_size(axis)
    others = [
        lax.ppermute(cells, axis, [(i, i ^ distance) for i in range(count)])
        for distance in distances
    ]
    for other in others:
        cells = jnp.maximum(cells, other)
    return cells


def smooth_both(values, spacing):
    for dim in (2, 1):
        count = values.shape[dim] - 4 * spacing
        total = taps[0] * lax.slice_in_dim(values, 0, count, axis=dim)
        for tap_index in range(1, 5):
            start = tap_index * spacing
            total = total + taps[tap_index] * lax.slice_in_dim(
                values, start, start + count, axis=dim
            )
        values = total
    return values


def real_dft(parts):
    count = len(parts)
    if count == 1:
        return [(parts[0], None)]
    if count == 2:
        return [(parts[0] + parts[1], None), (parts[0] - parts[1], None)]
    even = real_dft(parts[0::2])
    odd = real_dft(parts[1::2])
    out = [None] * (count // 2 + 1)
    for k in range(count // 4 + 1):
        turned = spin(odd[k], -2.0 * math.pi * k / count)
        out[k] = pair_add(even[k], turned)
        low = pair_sub(even[k], turned)
        out[count // 2 - k] = (low[0], None if low[1] is None else -low[1])
    out[0] = (out[0][0], None)
    out[count // 2] = (out[count // 2][0], None)
    return out


def real_inverse_dft(pairs):
    count = 2 * (len(pairs) - 1)
    if count == 2:
        return [pairs[0][0] + pairs[1][0], pairs[0][0] - pairs[1][0]]
    even, odd = [], []
    for k in range(count // 4 + 1):
        low = pairs[k]
        high = pairs[count // 2 - k]
        high = (high[0], None if high[1] is None else -high[1])
        even.append(pair_add(low, high))
        odd.append(spin(pair_sub(low, high), 2.0 * math.pi * k / count))
    for half in (even, odd):
        half[0] = (half[0][0], None)
        half[-1] = (half[-1][0], None)
    even = real_inverse_dft(even)
    odd = real_inverse_dft(odd)
    return [cells for both in zip(even, odd) for cells in both]


def complex_dft(pairs, sign):
    count = len(pairs)
    if count == 1:
        return pairs
    even = complex_dft(pairs[0::2], sign)
    odd = complex_dft(pairs[1::2], sign)
    turned = [spin(odd[k], sign * 2.0 * math.pi * k / count) for k in range(count // 2)]
    return [pair_add(a, b) for a, b in zip(even, turned)] + [
        pair_sub(a, b) for a, b in zip(even, turned)
    ]


def pair_add(a, b):
    if a[1] is None or b[1] is None:
        return (a[0] + b[0], a[1] if b[1] is None else b[1])
    return (a[0] + b[0], a[1] + b[1])


def pair_sub(a, b):
    if b[1] is None:
        return (a[0] - b[0], a[1])
    return (a[0] - b[0], -b[1] if a[1] is None else a[1] - b[1])


def spin(pair, angle):
    quarter = angle / (0.5 * math.pi)
    turns = round(quarter)
    real, imag = pair
    if abs(quarter - turns) < 1e-9:
        turns %= 4
        if turns == 0:
            return pair
        if turns == 2:
            return (-real, None if imag is None else -imag)
        if imag is None:
            return (jnp.zeros_like(real), real if turns == 1 else -real)
        return (-imag, real) if turns == 1 else (imag, -real)
    cosine, sine = math.cos(angle), math.sin(angle)
    if imag is None:
        return (real * cosine, real * sine)
    if abs(abs(cosine) - abs(sine)) < 1e-9:
        a, b = math.copysign(1.0, cosine), math.copysign(1.0, sine)
        root = abs(cosine)
        first = real if a > 0 else -real
        second = imag if b > 0 else -imag
        third = real if b > 0 else -real
        fourth = imag if a > 0 else -imag
        return ((first - second) * root, (third + fourth) * root)
    return (real * cosine - imag * sine, real * sine + imag * cosine)


def split(cells):
    high = cells.astype(jnp.bfloat16)
    return high, (cells - high.astype(jnp.float32)).astype(jnp.bfloat16)


def dot(a, b):
    return jnp.dot(a, b, preferred_element_type=jnp.float32)


def split_table(table):
    high = table.astype(np.float32).astype(ml_dtypes.bfloat16)
    low = (table - high.astype(np.float64)).astype(np.float32).astype(ml_dtypes.bfloat16)
    return np.stack([high, low], axis=-3)


def group_columns(length, count, group):
    radix = 2 * count
    lanes = length // radix
    spots = np.arange(lanes)
    if group:
        return group + radix * spots
    half = lanes // 2
    return np.where(spots < half, radix * spots, count + radix * (spots - half))


def row_tables(length, count):
    radix = 2 * count
    lanes = length // radix
    half = lanes // 2
    spots = np.arange(lanes)
    there, back = [], []
    for group in range(2):
        columns = group_columns(length, count, 0) if group == 0 else radix * spots
        angles = 2.0 * np.pi * (np.outer(spots, columns) % length) / length
        cosine, sine = np.cos(angles), np.sin(angles)
        ahead = np.zeros((2, lanes, 2, lanes))
        behind = np.zeros((2, lanes, 2, lanes))
        if group:
            ahead[0, :, 0], ahead[0, :, 1] = cosine, -sine
            ahead[1, :, 0], ahead[1, :, 1] = sine, cosine
            behind[0, :, 0], behind[0, :, 1] = cosine.T, sine.T
            behind[1, :, 0], behind[1, :, 1] = -sine.T, cosine.T
        else:
            for part, where in enumerate((slice(0, half), slice(half, lanes))):
                ahead[part, :, 0, where] = cosine[:, where]
                ahead[part, :, 1, where] = -sine[:, where]
                behind[0, where, part] = 2.0 * cosine[:, where].T
                behind[1, where, part] = -2.0 * sine[:, where].T
            ahead[0, :, 1, 0] = (-1.0) ** spots
            behind[0, 0, 0] = 1.0
            behind[1, 0, 0] = (-1.0) ** spots
        there.append(ahead.reshape(2 * lanes, 2 * lanes))
        back.append(behind.reshape(2 * lanes, 2 * lanes) / float(length) ** 2)
    angles = 2.0 * np.pi * np.outer(np.arange(count), spots) / length
    turns = np.stack([np.cos(angles), np.sin(angles)]).astype(np.float32)
    return split_table(np.stack(there)), split_table(np.stack(back)), turns


def column_tables(length, count, steps):
    size = length // steps
    each = size // count
    quarter = each // 4
    order = np.r_[0:quarter, each - quarter : each, quarter : each - quarter]
    order = (np.arange(count)[:, None] * each + order[None]).reshape(-1)
    order = np.concatenate([order, size + order])
    spots = np.arange(size)
    angles = 2.0 * np.pi * (np.outer(spots, spots) % size) / size
    cosine, sine = np.cos(angles), np.sin(angles)
    there = np.block([[cosine, sine], [-sine, cosine]])
    turns = np.zeros((2, size, lane_count), np.float32)
    angles = 2.0 * np.pi * np.outer(spots, np.arange(steps)) / length
    turns[0, :, :steps], turns[1, :, :steps] = np.cos(angles), np.sin(angles)
    return split_table(there), split_table(there.T[order]), turns


def weight_tables(length, count, steps):
    width = length // count
    lanes = length // (2 * count)
    per_class = width // (2 * count)
    packs = lanes // (2 * per_class)
    radix = 2 * count

    def classes(group):
        return (group, radix - group) if group else (0, count)

    pick = np.zeros((width, count, 2, per_class))
    for group in range(count):
        for which, kind in enumerate(classes(group)):
            for q in range(per_class):
                pick[radix * q + kind, group, which, q] = 1.0
    place = np.zeros((2, count, lanes, packs * 2 + 1, lanes))

    def slot(group, column, pack):
        column %= length
        source, rest = divmod(column, width)
        which = classes(group).index(rest % radix)
        return source, pack * 2 * per_class + which * per_class + rest // radix

    for version, group in ((0, 0), (1, 1)):
        columns = group_columns(length, count, group)
        for pack in range(packs):
            for lane in range(lanes):
                column = int(columns[lane])
                mates = [(column, 0, 0.5), (-column, 1, 0.5)]
                if group == 0 and lane == 0:
                    mates = [(c, s, 0.25) for c in (0, length // 2) for s in (0, 1)]
                for mate, side, value in mates:
                    source, where = slot(group, mate, pack)
                    place[version, source, where, pack * 2 + side, lane] += value
            if group == 0:
                for mate, value in ((0, 0.25), (length // 2, -0.25)):
                    source, where = slot(group, mate, pack)
                    place[version, source, where, packs * 2, pack] += value
    flip = np.zeros((length // steps, length // steps))
    flip[np.arange(len(flip)), -np.arange(len(flip))] = 1.0
    as_half = lambda table: table.astype(np.float32).astype(ml_dtypes.bfloat16)
    return (
        as_half(pick.reshape(width, width)),
        as_half(place.reshape(2, count * lanes, (packs * 2 + 1) * lanes)),
        as_half(flip),
    )


def busy(microseconds):
    return pl.CostEstimate(
        flops=0, bytes_accessed=int(microseconds * 3.5e6), transcendentals=0
    )


def whole_call(body, out_shapes, scratch, name, microseconds):
    return pl.pallas_call(
        body,
        out_shape=out_shapes,
        scratch_shapes=scratch,
        compiler_params=pltpu.CompilerParams(vmem_limit_bytes=24 * mebibyte),
        name=name,
        cost_estimate=busy(microseconds),
    )


def spun(pairs, spin_ref, sign):
    out = [pairs[0]]
    for group in range(1, len(pairs)):
        real, imag = pairs[group]
        cosine = jnp.broadcast_to(spin_ref[0, pl.ds(group, 1), :], real.shape)
        sine = sign * jnp.broadcast_to(spin_ref[1, pl.ds(group, 1), :], real.shape)
        out.append((real * cosine - imag * sine, imag * cosine + real * sine))
    return out


def row_forward_body(steps, me_ref, x_ref, table_ref, spin_ref, *refs):
    out_refs, held = refs[:-1], refs[-1]
    groups = len(out_refs)
    _, height, lanes = out_refs[0].shape
    each = height // steps
    for start in range(0, height, 16):
        rows = pl.ds(start, 16)
        tiles = [x_ref[rows, pl.ds(lanes * t, lanes)] for t in range(2 * groups)]
        pairs = real_dft(tiles)
        pairs = [(pairs[0][0], pairs[groups][0])] + pairs[1:groups]
        pairs = spun(pairs, spin_ref, -1.0)
        for group in range(groups):
            high, low = split(jnp.concatenate(pairs[group], axis=1))
            held[0, group, rows, :] = high
            held[1, group, rows, :] = low
    for turn, out_ref in enumerate(out_refs):
        group = me_ref[0] ^ turn
        kind = jnp.minimum(group, 1)
        done = (
            dot(held[0, group], table_ref[kind, 0])
            + dot(held[1, group], table_ref[kind, 0])
            + dot(held[0, group], table_ref[kind, 1])
        )
        for start in range(0, height, 8):
            spread = pl.ds(start % steps * each + start // steps, 8, stride=each)
            out_ref[0, spread, :] = done[start : start + 8, :lanes]
            out_ref[1, spread, :] = done[start : start + 8, lanes:]


def row_inverse_body(steps, groups, me_ref, *refs):
    in_refs = refs[:groups]
    table_ref, spin_ref, est_ref, dirty_ref, _, res_ref, half_ref, held = refs[groups:]
    _, chunk, lanes = in_refs[0].shape
    parts, _, wide = half_ref.shape
    each = chunk // steps
    block = est_ref.shape[0]
    turn = pl.program_id(0)

    @pl.when(turn == 0)
    def _():
        for partner, in_ref in enumerate(in_refs):
            group = me_ref[0] ^ partner
            kind = jnp.minimum(group, 1)
            halves = []
            for part in range(2):
                pieces = [
                    in_ref[part, pl.ds(start % steps * each + start // steps, 8, stride=each), :]
                    for start in range(0, chunk, 8)
                ]
                halves.append(jnp.concatenate(pieces, axis=0))
            high, low = split(jnp.concatenate(halves, axis=1))
            held[group] = (
                dot(high, table_ref[kind, 0])
                + dot(low, table_ref[kind, 0])
                + dot(high, table_ref[kind, 1])
            )

    per = wide // lanes
    lane_ids = lax.broadcasted_iota(jnp.int32, (8, lanes), 1)
    sides = [None] * parts
    for start in range(0, block, 8):
        rows = pl.ds(start, 8)
        chunk_rows = pl.ds(pl.multiple_of(turn * block + start, 8), 8)
        pairs = [
            (held[group, chunk_rows, pl.ds(0, lanes)], held[group, chunk_rows, pl.ds(lanes, lanes)])
            for group in range(groups)
        ]
        pairs = spun(pairs, spin_ref, 1.0)
        pairs = [(pairs[0][0], None)] + pairs[1:] + [(pairs[0][1], None)]
        tiles = real_inverse_dft(pairs)
        for t in range(2 * groups):
            where = pl.ds(lanes * t, lanes)
            residual = dirty_ref[rows, where] - tiles[t]
            res_ref[rows, where] = residual
            tiles[t] = est_ref[rows, where] + step_size * residual
            half_ref[t // per, chunk_rows, pl.ds(lanes * (t % per), lanes)] = tiles[t]
        offset = start // 8 * 2 * rim % lanes
        for part in range(parts):
            done = jnp.zeros_like(tiles[0]) if offset == 0 else sides[part]
            if part > 0:
                turned = pltpu.roll(tiles[part * per - 1], (offset + rim) % lanes, 1)
                done = jnp.where((lane_ids >= offset) & (lane_ids < offset + rim), turned, done)
            if part < parts - 1:
                turned = pltpu.roll(tiles[(part + 1) * per], (offset + rim) % lanes, 1)
                done = jnp.where(
                    (lane_ids >= offset + rim) & (lane_ids < offset + 2 * rim), turned, done
                )
            sides[part] = done
            if offset + 2 * rim == lanes:
                spot = turn * (block // 8 * 2 * rim // lanes) + start // 8 * 2 * rim // lanes
                where = pl.ds(pl.multiple_of(spot * lanes, lanes), lanes)
                half_ref[part, pl.ds(chunk, 8), where] = done


def starlet_body(chans, spans, fills, ends_ref, before_ref, *refs):
    sources, (detail_ref, peak_ref, ping, pong) = refs[:-4], refs[-4:]
    part = detail_ref.shape[3]
    lanes = lane_count
    tiles = part // lanes
    total = part + lanes
    no_left, no_right = ends_ref[0] > 0, ends_ref[1] > 0
    no_top, no_bottom = ends_ref[2] > 0, ends_ref[3] > 0
    lane_ids = lax.broadcasted_iota(jnp.int32, (8, lanes), 1)
    outside = ((lane_ids >= lanes // 2) & no_left) | ((lane_ids < lanes // 2) & no_right)
    for chan in range(chans):
        for target, index, source_row, count, pack_row, group in fills:
            source = sources[index * chans + chan]
            to = pl.ds(8 + target, count)
            ping[chan, to, pl.ds(0, part)] = source[pl.ds(source_row, count), :]
            for i in range(count // 8):
                spot = (group + i) * 2 * rim
                tile = source[pl.ds(pack_row, 8), pl.ds(spot // lanes * lanes, lanes)]
                shift = (lanes - spot % lanes - rim) % lanes
                to = pl.ds(8 + target + 8 * i, 8)
                ping[chan, to, pl.ds(part, lanes)] = pltpu.roll(tile, shift, 1)

    skirt = halo_rows // 8
    peaks = [jnp.zeros((8, part), jnp.float32)] * 3
    for start, blocks, out_start, top, bottom in spans:
        for level in range(3):
            gap = 1 << level
            before, after = (ping, pong) if level % 2 == 0 else (pong, ping)

            def step(i, peak, level, gap, before, after):
                base = 8 + start + 8 * i
                if not isinstance(i, int):
                    base = pl.multiple_of(base, 8)
                inner = not isinstance(i, int)
                energy = 0.0
                for chan in range(chans):
                    window = before[chan, pl.ds(base - 8, 24), :]
                    near = window[8 - gap : 16 - gap] + window[8 + gap : 16 + gap]
                    far = window[8 - 2 * gap : 16 - 2 * gap] + window[8 + 2 * gap : 16 + 2 * gap]
                    row = (far + 4.0 * near) + 6.0 * window[8:16]
                    near = pltpu.roll(row, gap, 1) + pltpu.roll(row, total - gap, 1)
                    far = pltpu.roll(row, 2 * gap, 1) + pltpu.roll(row, total - 2 * gap, 1)
                    smooth = ((far + 4.0 * near) + 6.0 * row) * (1.0 / 256.0)
                    whole = smooth[:, :part]
                    if level < 2:
                        side = jnp.where(outside, 0.0, smooth[:, part:])
                        if not inner and (top if i < skirt else bottom):
                            gone = no_top if i < skirt else no_bottom
                            side = jnp.where(gone, 0.0, side)
                            after[chan, pl.ds(base, 8), pl.ds(0, part)] = jnp.where(
                                gone, 0.0, whole
                            )
                        else:
                            after[chan, pl.ds(base, 8), pl.ds(0, part)] = whole
                        after[chan, pl.ds(base, 8), pl.ds(part, lanes)] = side
                    if inner:
                        to = pl.ds(pl.multiple_of(out_start + 8 * i - halo_rows, 8), 8)
                        detail = window[8:16, :part] - whole
                        detail_ref[chan, level, to, :] = detail
                        if level == 2:
                            detail_ref[chan, 3, to, :] = whole
                        energy = energy + detail * detail
                return jnp.maximum(peak, energy) if inner else peak

            step = functools.partial(step, level=level, gap=gap, before=before, after=after)
            for i in range(level, skirt):
                step(i, None)
                step(blocks - 1 - i, None)
            peaks[level] = lax.fori_loop(
                skirt, blocks - skirt, step, peaks[level], unroll=(blocks - 2 * skirt) // 2
            )
    for level in range(3):
        most = before_ref[level]
        for t in range(tiles):
            most = jnp.maximum(most, peaks[level][:, t * lanes : (t + 1) * lanes])
        peak_ref[level] = most


def shrink_body(chans, detail_ref, peak_ref, *out_refs):
    thresholds = [
        fractions[level] * jnp.sqrt(jnp.max(peak_ref[level], keepdims=True)) for level in range(3)
    ]
    for start in range(0, out_refs[0].shape[0], 16):
        rows = pl.ds(start, 16)
        factors = []
        for level in range(3):
            energy = 0.0
            for chan in range(chans):
                detail = detail_ref[chan, level, rows, :]
                energy = energy + detail * detail
            energy = jnp.sqrt(energy)
            threshold = jnp.broadcast_to(thresholds[level], energy.shape)
            factors.append(1.0 - threshold / jnp.maximum(energy, threshold))
        for chan in range(chans):
            total = detail_ref[chan, 3, rows, :]
            for level in range(3):
                total = total + factors[level] * detail_ref[chan, level, rows, :]
            out_refs[chan][rows, :] = total


def join_body(me_ref, *refs):
    chans = (len(refs) - 1) // 2
    out_ref = refs[-1]
    part = refs[0].shape[1]
    outer_rows, inner_rows = refs[0].shape[0] // 2, refs[chans].shape[0]
    for chan in range(chans):
        outer, inner = refs[chan], refs[chans + chan]
        columns = pl.ds(pl.multiple_of((me_ref[0] ^ chan) * part, part), part)
        out_ref[pl.ds(0, outer_rows), columns] = outer[pl.ds(0, outer_rows), :]
        out_ref[pl.ds(outer_rows, inner_rows), columns] = inner[...]
        out_ref[pl.ds(outer_rows + inner_rows, outer_rows), columns] = outer[
            pl.ds(outer_rows, outer_rows), :
        ]


def facing(blocks, step):
    rows = lax.broadcasted_iota(jnp.int32, blocks[0].shape, 0)
    return jnp.where(rows == 0, blocks[-step % len(blocks)], blocks[len(blocks) - 1 - step])


def column_body(steps, count, me_ref, *refs):
    in_refs = refs[:count]
    there_ref, back_ref, turn_ref, weight_ref, mirror_ref, flip_ref = refs[count : count + 6]
    out_refs, (gathered, held, made, ready) = refs[count + 6 : 3 * count + 6], refs[3 * count + 6 :]
    _, height, lanes = in_refs[0].shape
    each = height // steps
    size = each * count
    for turn, in_ref in enumerate(in_refs):
        source = me_ref[0] ^ turn
        for part in range(2):
            to = pl.ds(pl.multiple_of(part * size + source * each, 8), each)
            for step in range(steps):
                gathered[to, pl.ds(step * lanes, lanes)] = in_ref[part, pl.ds(step * each, each), :]
    for step in range(0, steps, 2):
        high, low = split(gathered[:, pl.ds(step * lanes, 2 * lanes)])
        done = dot(there_ref[0], high) + dot(there_ref[1], high) + dot(there_ref[0], low)
        for k in range(2):
            held[0, step + k] = done[:size, k * lanes : (k + 1) * lanes]
            held[1, step + k] = done[size:, k * lanes : (k + 1) * lanes]

    def turned(pairs, rows, sign):
        cosines, sines = turn_ref[0, rows, :], turn_ref[1, rows, :]
        out = [pairs[0]]
        for step in range(1, steps):
            real, imag = pairs[step]
            cosine = jnp.broadcast_to(cosines[:, step : step + 1], real.shape)
            sine = sign * jnp.broadcast_to(sines[:, step : step + 1], real.shape)
            out.append((real * cosine - imag * sine, imag * cosine + real * sine))
        return out

    def forward(chunk, carry):
        rows = pl.ds(pl.multiple_of(chunk * 8, 8), 8)
        pairs = [(held[0, step, rows, :], held[1, step, rows, :]) for step in range(steps)]
        for step, pair in enumerate(complex_dft(turned(pairs, rows, -1.0), -1.0)):
            held[0, step, rows, :] = pair[0]
            held[1, step, rows, :] = pair[1]
        return carry

    lax.fori_loop(0, size // 8, forward, 0, unroll=8)
    lane_ids = lax.broadcasted_iota(jnp.int32, (size, lanes), 1)
    lone = jnp.zeros((size, lanes), jnp.float32)
    for step in range(steps):
        for part in range(2):
            spot = 2 * step + part
            moved = facing([held[part, other] for other in range(steps)], step)
            if spot:
                moved = pltpu.roll(moved, spot, 1)
            lone = jnp.where(lane_ids == spot, moved, lone)
    high, low = split(lone)
    lone = (dot(flip_ref[...], high) + dot(flip_ref[...], low)) * mirror_ref[...]
    for step in range(steps):
        weight = weight_ref[step]
        for part in range(2):
            spot = 2 * step + part
            moved = pltpu.roll(lone, lanes - spot, 1) if spot else lone
            made[part, step] = weight * held[part, step] + jnp.where(lane_ids == 0, moved, 0.0)

    def backward(chunk, carry):
        rows = pl.ds(pl.multiple_of(chunk * 8, 8), 8)
        pairs = [(made[0, step, rows, :], made[1, step, rows, :]) for step in range(steps)]
        for step, pair in enumerate(turned(complex_dft(pairs, 1.0), rows, 1.0)):
            made[0, step, rows, :] = pair[0]
            made[1, step, rows, :] = pair[1]
        return carry

    lax.fori_loop(0, size // 8, backward, 0, unroll=8)
    half = each // 2
    for step in range(0, steps, 2):
        block = [
            jnp.concatenate([made[part, step + k] for k in range(2)], axis=1) for part in range(2)
        ]
        high, low = split(jnp.concatenate(block, axis=0))
        done = dot(back_ref[0], high) + dot(back_ref[1], high) + dot(back_ref[0], low)
        for k in range(2):
            ready[step + k] = done[:, k * lanes : (k + 1) * lanes]
    for turn in range(count):
        target = me_ref[0] ^ turn
        for part in range(2):
            for inner in range(2):
                start = pl.multiple_of(part * size + target * each + inner * half, 8)
                for step in range(steps):
                    rows = pl.ds(step * half, half)
                    out_refs[inner * count + turn][part, rows, :] = ready[step, pl.ds(start, half), :]


def weight_pick_body(w_ref, pick_ref, out_ref):
    count, thick, lanes = out_ref.shape
    packs, _, width = w_ref.shape
    piece = lanes // packs
    chosen = []
    for pack in range(packs):
        high, low = split(w_ref[pack])
        chosen.append(dot(high, pick_ref[...]) + dot(low, pick_ref[...]))
    lane_ids = lax.broadcasted_iota(jnp.int32, (thick, lanes), 1)
    for target in range(count):
        start = target * piece // lanes * lanes
        total = None
        for pack in range(packs):
            moved = chosen[pack][:, start : start + lanes]
            shift = (pack - target) % packs * piece
            if shift:
                moved = pltpu.roll(moved, shift, 1)
            total = moved if pack == 0 else jnp.where(lane_ids >= pack * piece, moved, total)
        out_ref[target] = total


def weight_place_body(in_ref, place_ref, flip_ref, weight_ref, mirror_ref):
    count, depth, lanes = in_ref.shape
    steps, size, _ = weight_ref.shape
    packs = steps * size // depth
    inner = depth // size
    total = 0.0
    for source in range(count):
        high, low = split(in_ref[source])
        chosen = place_ref[pl.ds(source * lanes, lanes), :]
        total = total + dot(high, chosen) + dot(low, chosen)

    def block(step, side):
        pack, rest = divmod(step, inner)
        start = (2 * pack + side) * lanes if side < 2 else 2 * packs * lanes
        return total[rest * size : (rest + 1) * size, start : start + lanes]

    def flipped(cells):
        high, low = split(cells)
        return dot(flip_ref[...], high) + dot(flip_ref[...], low)

    lane_ids = lax.broadcasted_iota(jnp.int32, (size, lanes), 1)
    extra = [block(step, 2) for step in range(steps)]
    extra = [
        pltpu.roll(cells, lanes - step // inner, 1) if step // inner else cells
        for step, cells in enumerate(extra)
    ]
    straight = jnp.zeros((size, lanes), jnp.float32)
    opposite = straight
    for step in range(steps):
        against = facing(extra, step)
        for part in range(2):
            spot = 2 * step + part
            sign = 1.0 - 2.0 * part
            straight = jnp.where(lane_ids == spot, sign * roll_to(extra[step], spot), straight)
            opposite = jnp.where(lane_ids == spot, sign * roll_to(against, spot), opposite)
    mirror_ref[...] = straight + flipped(opposite)
    backs = [block(step, 1) for step in range(steps)]
    for step in range(0, steps, 2):
        both = jnp.concatenate([facing(backs, step), facing(backs, step + 1)], axis=1)
        both = flipped(both)
        weight_ref[step] = block(step, 0) + both[:, :lanes]
        weight_ref[step + 1] = block(step + 1, 0) + both[:, lanes:]


def roll_to(cells, spot):
    return pltpu.roll(cells, spot, 1) if spot else cells


def filtered(values, dirty, weights):
    height, length = values.shape
    count = lax.axis_size("rows")
    lanes = length // (2 * count)
    steps = height // 16
    size = length // steps
    width = weights.shape[1]
    f32 = jnp.float32
    pick, place, flip = [jnp.asarray(table) for table in weight_tables(length, count, steps)]
    there, back, spins = [jnp.asarray(table) for table in row_tables(length, count)]
    down, up, turns = [jnp.asarray(table) for table in column_tables(length, count, steps)]
    shape = lambda *dims: jax.ShapeDtypeStruct(dims, f32)
    packs = lanes * count // width
    depth = length // packs
    half = height // 2
    vmem = pl.BlockSpec(memory_space=pltpu.VMEM)
    smem = pl.BlockSpec(memory_space=pltpu.SMEM)
    me = jnp.reshape(lax.axis_index("rows"), (1,)).astype(jnp.int32)

    thick = depth // 2
    sent = pl.pallas_call(
        weight_pick_body,
        grid=(2,),
        in_specs=[
            pl.BlockSpec((packs, thick, width), lambda i: (0, i, 0)),
            pl.BlockSpec((width, width), lambda i: (0, 0)),
        ],
        out_specs=pl.BlockSpec((count, thick, lanes), lambda i: (0, i, 0)),
        out_shape=shape(count, depth, lanes),
        compiler_params=pltpu.CompilerParams(vmem_limit_bytes=56 * mebibyte),
        name="weight_pick",
        cost_estimate=busy(4),
    )(weights.reshape(packs, depth, width), pick)
    sent = lax.all_to_all(sent, "rows", 0, 0, tiled=True)
    ahead = pl.pallas_call(
        functools.partial(row_forward_body, steps),
        in_specs=[smem, vmem, vmem, vmem],
        out_specs=[vmem] * count,
        out_shape=[shape(2, height, lanes)] * count,
        scratch_shapes=[pltpu.VMEM((2, count, height, 2 * lanes), jnp.bfloat16)],
        compiler_params=pltpu.CompilerParams(vmem_limit_bytes=56 * mebibyte),
        name="row_forward",
        cost_estimate=busy(6),
    )(me, values, there, spins)

    def over_rows(pieces):
        return [pieces[0]] + [
            lax.ppermute(pieces[turn], "rows", [(i, i ^ turn) for i in range(count)])
            for turn in range(1, count)
        ]

    ahead = over_rows(ahead)
    mine = jnp.where(lax.axis_index("rows") == 0, place[0], place[1])
    weight, mirror = whole_call(
        weight_place_body,
        [shape(steps, size, lanes), shape(size, lanes)],
        [],
        "weight_place",
        10,
    )(sent, mine, flip)
    behind = pl.pallas_call(
        functools.partial(column_body, steps, count),
        in_specs=[smem] + [vmem] * (count + 6),
        out_specs=[vmem] * (2 * count),
        out_shape=[shape(2, half, lanes)] * (2 * count),
        scratch_shapes=[
            pltpu.VMEM((2 * size, steps * lanes), f32),
            pltpu.VMEM((2, steps, size, lanes), f32),
            pltpu.VMEM((2, steps, size, lanes), f32),
            pltpu.VMEM((steps, 2 * size, lanes), f32),
        ],
        compiler_params=pltpu.CompilerParams(vmem_limit_bytes=24 * mebibyte),
        name="column_filter",
        cost_estimate=busy(10),
    )(me, *ahead, down, up, turns, weight, mirror, flip)
    edge, core = over_rows(behind[:count]), behind[count:]
    core = over_rows(core)
    chans = lax.axis_size("chan")
    part = length // chans
    quarter = height // 4

    def row_inverse(cells, old, blocks, microseconds):
        rows_spec = pl.BlockSpec((quarter, length), lambda i: (blocks[0] + i * blocks[1], 0))
        whole = lambda *dims: pl.BlockSpec(dims, lambda i: (0,) * len(dims))
        return pl.pallas_call(
            functools.partial(row_inverse_body, steps, count),
            grid=(2,),
            in_specs=[smem]
            + [whole(2, half, lanes)] * count
            + [
                whole(*back.shape),
                whole(*spins.shape),
                rows_spec,
                rows_spec,
                pl.BlockSpec(memory_space=pl.ANY),
            ],
            out_specs=[rows_spec, whole(chans, half + 8, part)],
            out_shape=[shape(height, length), shape(chans, half + 8, part)],
            scratch_shapes=[pltpu.VMEM((count, half, 2 * lanes), f32)],
            input_output_aliases={count + 5: 0} if old is not dirty else {},
            compiler_params=pltpu.CompilerParams(vmem_limit_bytes=56 * mebibyte),
            name="row_inverse",
        cost_estimate=busy(microseconds),
        )(me, *cells, back, spins, values, dirty, old)

    def pieces_for(cells):
        me = lax.axis_index("chan")
        return [
            lax.dynamic_index_in_dim(cells, me ^ turn, 0, keepdims=False) for turn in range(chans)
        ]

    def over_chans(pieces):
        return [pieces[0]] + [
            lax.ppermute(pieces[turn], "chan", [(i, i ^ turn) for i in range(chans)])
            for turn in range(1, chans)
        ]

    def in_order(earlier, later):
        both = lax.optimization_barrier((*earlier, *later))
        return list(both[: len(earlier)]), list(both[len(earlier) :])

    residual, outer = row_inverse(edge, dirty, (0, 3), 20)
    outer = over_chans(pieces_for(outer))
    residual, inner = row_inverse(core, residual, (1, 1), 5)
    inner = over_chans(pieces_for(inner))
    outer, (inner[1],) = in_order(outer, [inner[1]])
    ahead_pairs = [(i, i + 1) for i in range(count - 1)]
    back_pairs = [(i + 1, i) for i in range(count - 1)]
    last = jnp.stack([cells[half - halo_rows :] for cells in outer])
    first = jnp.stack(
        [jnp.concatenate([cells[:halo_rows], cells[half:]], axis=0) for cells in outer]
    )
    last = lax.ppermute(last, "rows", ahead_pairs)
    first = lax.ppermute(first, "rows", back_pairs)
    above = [last[c] for c in range(chans)]
    below = [first[c] for c in range(chans)]
    chan_id, row_id = lax.axis_index("chan"), lax.axis_index("rows")
    at_end = jnp.stack(
        [chan_id == 0, chan_id == chans - 1, row_id == 0, row_id == count - 1]
    ).astype(jnp.int32)

    def starlet(sources, before, rows, spans, fills, microseconds):
        extent = max(fill[0] + fill[3] for fill in fills) + 16
        cells = pltpu.VMEM((chans, extent, part + lanes), f32)
        return pl.pallas_call(
            functools.partial(starlet_body, chans, spans, fills),
            in_specs=[smem] + [vmem] * (1 + len(sources)),
            out_specs=[vmem] * 2,
            out_shape=[shape(chans, 4, rows, part), shape(3, 8, lanes)],
            scratch_shapes=[cells, cells],
            compiler_params=pltpu.CompilerParams(vmem_limit_bytes=20 * mebibyte),
            name="starlet",
            cost_estimate=busy(microseconds),
        )(at_end, before, *sources)

    reach = quarter + halo_rows
    most = quarter - halo_rows
    skirt = halo_rows // 8
    outer_details, outer_peaks = starlet(
        outer + above + below,
        jnp.zeros((3, 8, lanes), f32),
        2 * most,
        (
            (0, reach // 8, 0, True, False),
            (reach + 16, reach // 8, most, False, True),
        ),
        (
            (0, 1, 0, halo_rows, halo_rows, (half - halo_rows) // 8),
            (halo_rows, 0, 0, quarter, half, 0),
            (reach + 16, 0, quarter, quarter, half, quarter // 8),
            (reach + 16 + quarter, 2, 0, halo_rows, halo_rows, 0),
        ),
        12,
    )
    inner_details, peaks = starlet(
        outer + inner,
        outer_peaks,
        half + 2 * halo_rows,
        ((0, half // 8 + 4 * skirt, 0, False, False),),
        (
            (0, 0, quarter - 2 * halo_rows, 2 * halo_rows, half, (quarter - 2 * halo_rows) // 8),
            (2 * halo_rows, 1, 0, half, half, 0),
            (2 * halo_rows + half, 0, quarter, 2 * halo_rows, half, quarter // 8),
        ),
        12,
    )
    peaks = max_over(peaks, "rows", range(1, 2))
    peaks = max_over(peaks, "rows", range(2, count, 2))
    peaks = max_over(peaks, "chan", range(1, chans))

    def shrink(details):
        rows = details.shape[2]
        return pl.pallas_call(
            functools.partial(shrink_body, chans),
            in_specs=[vmem, vmem],
            out_specs=[vmem] * chans,
            out_shape=[shape(rows, part)] * chans,
            compiler_params=pltpu.CompilerParams(vmem_limit_bytes=14 * mebibyte),
            name="shrink",
            cost_estimate=busy(3),
        )(details, peaks)

    outer = over_chans(shrink(outer_details))
    outer, inner = in_order(outer, shrink(inner_details))
    inner = over_chans(inner)
    new_estimate = pl.pallas_call(
        join_body,
        in_specs=[pl.BlockSpec(memory_space=pltpu.SMEM)] + [vmem] * (2 * chans),
        out_specs=vmem,
        out_shape=shape(height, length),
        compiler_params=pltpu.CompilerParams(vmem_limit_bytes=12 * mebibyte),
        name="join",
        cost_estimate=busy(4),
    )(jnp.reshape(chan_id, (1,)).astype(jnp.int32), *outer, *inner)
    return new_estimate, residual


def filtered_plain(values, dirty, weights):
    height, length = values.shape
    row_count = lax.axis_size("rows")
    narrow = length // row_count
    spec_real, spec_imag = dft_last(values, jnp.zeros_like(values), -1.0)
    spec_real = spec_real.reshape(height, row_count, narrow)
    spec_imag = spec_imag.reshape(height, row_count, narrow)
    col_real, col_imag = columns_forward(
        (
            lax.all_to_all(spec_real, "rows", split_axis=1, concat_axis=0, tiled=True),
            lax.all_to_all(spec_imag, "rows", split_axis=1, concat_axis=0, tiled=True),
        )
    )
    prod_real = weights * col_real[:, 0, :]
    prod_imag = weights * col_imag[:, 0, :]
    back_real, back_imag = dft_first(prod_real, prod_imag, 1.0)
    back_real = back_real.reshape(row_count, height, narrow)
    back_imag = back_imag.reshape(row_count, height, narrow)
    blurred = rows_inverse(
        (
            lax.all_to_all(back_real, "rows", split_axis=0, concat_axis=2, tiled=True),
            lax.all_to_all(back_imag, "rows", split_axis=0, concat_axis=2, tiled=True),
        )
    )[0]
    residual = dirty - blurred
    return residual, values + step_size * residual


def joined_plain(halfway):
    height, length = halfway.shape
    depth = 14
    chan_count = lax.axis_size("chan")
    part = length // chan_count
    padded = with_halo(halfway, (("rows", 0),), depth)
    padded = jnp.pad(padded, ((0, 0), (depth, depth)))
    pieces = jnp.stack(
        [padded[:, q * part : (q + 1) * part + 2 * depth] for q in range(chan_count)]
    )
    current = lax.all_to_all(pieces, "chan", split_axis=0, concat_axis=0, tiled=True)
    row_ids = lax.axis_index("rows") * height - depth + lax.iota(jnp.int32, height + 2 * depth)
    col_ids = lax.axis_index("chan") * part - depth + lax.iota(jnp.int32, part + 2 * depth)
    margin = depth
    details = []
    for scale_level in range(3):
        reach = 2 << scale_level
        smoother = smooth_both(current, 1 << scale_level)
        row_ids = row_ids[reach:-reach]
        col_ids = col_ids[reach:-reach]
        inside = ((row_ids >= 0) & (row_ids < length))[:, None] & (
            (col_ids >= 0) & (col_ids < length)
        )[None, :]
        smoother = jnp.where(inside[None], smoother, 0.0)
        new_margin = margin - reach
        details.append(
            current[:, margin : margin + height, margin : margin + part]
            - smoother[:, new_margin : new_margin + height, new_margin : new_margin + part]
        )
        current = smoother
        margin = new_margin
    energies = [jnp.sum(detail * detail, axis=0) for detail in details]
    peaks = jnp.stack([jnp.broadcast_to(jnp.max(energy), (128,)) for energy in energies])
    for axis in ("rows", "chan"):
        peaks = lax.pmax(peaks, axis)
    output = current
    for scale_level in range(3):
        threshold = fractions[scale_level] * jnp.sqrt(peaks[scale_level, 0])
        factor = 1.0 - threshold / jnp.maximum(jnp.sqrt(energies[scale_level]), threshold)
        output = output + factor[None] * details[scale_level]
    output = lax.all_to_all(output, "chan", split_axis=0, concat_axis=2, tiled=True)[0]
    return output


def shards(estimate, dirty_image, psf_weights):
    values, dirty, weights = estimate[0], dirty_image[0], psf_weights[0]
    height, length = values.shape
    row_count, chan_count = lax.axis_size("rows"), lax.axis_size("chan")
    whole_tiles = length == 2 * row_count * lane_count and length % (chan_count * lane_count) == 0
    if whole_tiles and chan_count & (chan_count - 1) == 0:
        new_estimate, residual = filtered(values, dirty, weights)
    else:
        residual, halfway = filtered_plain(values, dirty, weights)
        new_estimate = joined_plain(halfway)
    return (new_estimate[None], residual[None])


def solution(mesh):
    return jax.shard_map(
        shards,
        mesh=mesh,
        in_specs=(P("chan", "rows", None), P("chan", "rows", None), P("chan", None, "rows")),
        out_specs=(P("chan", "rows", None), P("chan", "rows", None)),
        check_vma=False,
    )
```
